256 devices in a mesh: tm: 16 (over y_lo, z), gx: 4 (over y_hi, core), gy: 4 (over x).
Axes of the slice: x: 4, y: 4 (y_hi: 2, y_lo: 2; y = y_hi * 2 + y_lo), z: 8, core: 2. Of those that a mesh axis runs over, the one named last changes fastest.
Arguments:
- initial_temp: float32 [64, 32, 512], P(None, 'gx', 'gy'), may hold values from -4 to 4
- conductivity: float32 [64, 32, 512], P(None, 'gx', 'gy'), may hold values from 0.5 to 2
- vert_cond: float32 [64], replicated, may hold values from 0.5 to 2
- borehole_cells: int32 [4, 4, 16], P('gx', 'gy'), may hold values from 0 to 1023
- borehole_profiles: int32 [4, 4, 16], P('gx', 'gy'), may hold values from 0 to 7
- heat_table: float32 [8, 16], P(None, 'tm'), may hold values from 0.1 to 0.8
Outputs:
- end_temp: float32 [16, 64, 32, 512], P('tm', None, 'gx', 'gy')
The draws below stay inside these ranges and needn't reach their ends.
Inputs may be any that keep to these rules, and one draw needn't show every extreme that they name: `borehole_cells`: cell x * 128 + y of the lateral tile of its (gx, gy) block; cells may repeat, and then their heat adds.
All inputs are finite; a program needn't handle non-finite values.
Results may differ from the reference program's by a relative error of at most 0.0003.
Values sent between devices are 32-bit elements; how exact they have to be, the bound alone decides.
No kernel may reach another device: no remote copies, remote signals or barrier semaphores. Data moves between devices by JAX's collectives and lax.ppermute only.
A program may use at most 128 MiB of HBM per device.

```python
import math
from functools import partial
import jax
import jax.numpy as jnp
from jax import lax

ZC = 64
CX = 8
CY = 128
BH_DEV = 16
PROFILES = 8
ITERS = 2
SLICES = 16
NX = 32
NY = 512
TILE_ROWS = 4
TILE_COLUMNS = 4


def draw_initial_temp(key, part):
    shape_full = (ZC, NX, NY)
    return jnp.clip(jax.random.normal(key, shape_full, jnp.float32), -4.0, 4.0)


def touch_ends(array, rng, low, top_value):
    shape = array.shape
    spot = [jax.random.randint(jax.random.fold_in(rng, axis), (), 0, shape[axis]) for axis in range(len(shape))]
    array = array.at[tuple(spot)].set(low)
    longest = shape.index(max(shape))
    spot[longest] = (spot[longest] + 1) % shape[longest]
    return array.at[tuple(spot)].set(top_value)


def block_levels(key, dims, pieces, least, top_value):
    level = 1.0
    for position, parts in pieces:
        draws = jax.random.uniform(jax.random.fold_in(jax.random.fold_in(key, 6), position), (parts,), jnp.float32, least / len(pieces), top_value / len(pieces))
        level = level * jnp.repeat(jnp.exp(draws), dims[position] // parts).reshape((-1,) + (1,) * (len(dims) - 1 - position))
    return level


def setup_inputs(seed: int = 0) -> dict:
    key_list = jax.random.split(jax.random.key(seed), 7)
    initial_temp = draw_initial_temp(jax.random.fold_in(key_list[6], 71), 0)
    conductivity = jnp.clip(jnp.exp(math.log(2.0) - 1.3862944 * jax.random.uniform(key_list[1], (ZC, NX, NY), jnp.float32) ** block_levels(key_list[1], (ZC, NX, NY), ((1, 4), (2, 4)), -0.2, 0.2)), 0.5, 2.0)
    vert_cond = jnp.clip(jnp.exp(jax.random.uniform(key_list[2], (ZC,), jnp.float32, math.log(0.5), math.log(2.0))), 0.5, 2.0)
    borehole_cells = touch_ends(jax.random.randint(key_list[3], (TILE_ROWS, TILE_COLUMNS, BH_DEV), 0, CX * CY), jax.random.fold_in(key_list[3], 1), 0, (CX * CY) - 1).astype(jnp.int32)
    borehole_profiles = touch_ends(jax.random.randint(key_list[4], (TILE_ROWS, TILE_COLUMNS, BH_DEV), 0, PROFILES), jax.random.fold_in(key_list[4], 1), 0, PROFILES - 1).astype(jnp.int32)
    heat_table = jnp.clip(jnp.exp(math.log(0.8) - 2.0794415 * jax.random.uniform(key_list[5], (PROFILES, SLICES), jnp.float32) ** block_levels(key_list[5], (PROFILES, SLICES), ((1, 16),), -0.2, 0.2)), 0.1, 0.8)
    return dict(initial_temp=initial_temp, conductivity=conductivity, vert_cond=vert_cond, borehole_cells=borehole_cells, borehole_profiles=borehole_profiles, heat_table=heat_table)


LATERAL = 0.3
VERTICAL = 4.0
SPAN = 1.0
FINE_NODES = [0.0, (1.0 - math.sqrt(3.0 / 7.0)) / 2.0, 0.5, (1.0 + math.sqrt(3.0 / 7.0)) / 2.0, 1.0]
COARSE_NODES = [0.0, 0.5, 1.0]

def basis_coeffs(times_list, basis_index):
    coeffs = [1.0]
    denominator = 1.0
    for other_index in range(len(times_list)):
        if other_index != basis_index:
            other_time = times_list[other_index]
            widened = [0.0] * (len(coeffs) + 1)
            for power in range(len(coeffs)):
                widened[power + 1] = widened[power + 1] + coeffs[power]
                widened[power] = widened[power] - other_time * coeffs[power]
            coeffs = widened
            denominator = denominator * (times_list[basis_index] - other_time)
    return [entry / denominator for entry in coeffs]

def poly_value(coeffs, point):
    total = 0.0
    for power in range(len(coeffs)):
        total = total + coeffs[power] * point ** power
    return total

def poly_integral(coeffs, lower, upper):
    total = 0.0
    for power in range(len(coeffs)):
        total = total + coeffs[power] * (upper ** (power + 1) - lower ** (power + 1)) / (power + 1)
    return total

def node_integrals(times_list):
    integrals = []
    for interval in range(len(times_list) - 1):
        entries = []
        for basis_index in range(len(times_list)):
            entries.append(float(poly_integral(basis_coeffs(times_list, basis_index), times_list[interval], times_list[interval + 1])))
        integrals.append(entries)
    return integrals

def node_values(times_list, targets):
    return [[float(poly_value(basis_coeffs(times_list, basis_index), target)) for basis_index in range(len(times_list))] for target in targets]

def vertical_matrix(vert_cond):
    depth = vert_cond.shape[0]
    lower_faces = jnp.concatenate([vert_cond[1:], jnp.zeros((1,), jnp.float32)])
    centre = -VERTICAL * (vert_cond + lower_faces)
    levels = jnp.arange(depth, dtype=jnp.int32)
    row_index = levels[:, None]
    col_index = levels[None, :]
    matrix = jnp.where(row_index == col_index, centre[:, None], 0.0)
    matrix = matrix + jnp.where(col_index == row_index - 1, VERTICAL * vert_cond[:, None], 0.0)
    matrix = matrix + jnp.where(col_index == row_index + 1, VERTICAL * lower_faces[:, None], 0.0)
    return matrix

def propagator(matrix, interval):
    depth = matrix.shape[0]
    identity = jnp.eye(depth, dtype=matrix.dtype)
    factor = jnp.linalg.cholesky(identity - interval * matrix)
    halfway = jax.scipy.linalg.solve_triangular(factor, identity, lower=True)
    return jax.scipy.linalg.solve_triangular(factor, halfway, trans=1, lower=True)

def column_apply(matrix, volume):
    depth = volume.shape[0]
    flattened = volume.reshape(depth, -1)
    product = jnp.dot(matrix.astype(jnp.float32), flattened.astype(jnp.float32), precision=lax.Precision.HIGHEST, preferred_element_type=jnp.float32)
    return product.reshape(volume.shape)

def lateral_term(extended, conduct, coefficient):
    centre = extended[:, 1:-1, 1:-1]
    beside_all = extended[:, 2:, 1:-1] + extended[:, :-2, 1:-1] + extended[:, 1:-1, 2:] + extended[:, 1:-1, :-2]
    return coefficient * conduct * (beside_all - 4.0 * centre)

def padded_lateral(volume, conduct, coefficient):
    return lateral_term(jnp.pad(volume, ((0, 0), (1, 1), (1, 1))), conduct, coefficient)

def restrict(volume):
    depth, rows_x, rows_y = volume.shape
    return lax.optimization_barrier(jnp.mean(volume.reshape(depth, rows_x // 2, 2, rows_y // 2, 2), axis=(2, 4)))

def restrict_plane(heat_plane):
    rows_x, rows_y = heat_plane.shape
    return lax.optimization_barrier(jnp.mean(heat_plane.reshape(rows_x // 2, 2, rows_y // 2, 2), axis=(1, 3)))

def expand(volume):
    return jnp.repeat(jnp.repeat(volume, 2, axis=1), 2, axis=2)

def integrate(integrals, totals):
    interval_sums = []
    for interval in range(len(integrals)):
        running = integrals[interval][0] * totals[0]
        for basis_index in range(1, len(totals)):
            running = running + integrals[interval][basis_index] * totals[basis_index]
        interval_sums.append(running)
    return interval_sums

def node_sweep(start_value, start_explicit, start_implicit, known_terms, propagators, step_lengths, explicit_fn):
    states = [start_value]
    explicit_list = [start_explicit]
    implicit_list = [start_implicit]
    for interval in range(len(step_lengths)):
        rhs_value = states[interval] + step_lengths[interval] * explicit_list[interval] + known_terms[interval]
        advanced = column_apply(propagators[interval], rhs_value)
        implicit_list.append((advanced - rhs_value) / step_lengths[interval])
        states.append(advanced)
        explicit_list.append(explicit_fn(advanced))
    return (states, explicit_list, implicit_list)

def blend(weights, fine_index, deltas):
    return weights[fine_index][0] * deltas[0] + weights[fine_index][1] * deltas[1] + weights[fine_index][2] * deltas[2]

def correct(values_list, deltas, weights):
    return [values_list[fine_index] + expand(blend(weights, fine_index, deltas)) for fine_index in range(len(values_list))]

def source_plane(borehole_cells, borehole_profiles, heat_table, slice_index):
    tile_rows, tile_columns, per_tile = borehole_cells.shape
    global_rows = jnp.arange(tile_rows, dtype=jnp.int32)[:, None, None] * CX + borehole_cells // CY
    global_columns = jnp.arange(tile_columns, dtype=jnp.int32)[None, :, None] * CY + borehole_cells % CY
    heat_rates = heat_table[borehole_profiles, slice_index]
    heat_plane = jnp.zeros((NX, NY), heat_table.dtype)
    return heat_plane.at[global_rows.reshape(-1), global_columns.reshape(-1)].add(heat_rates.reshape(-1))

def reference(initial_temp, conductivity, vert_cond, borehole_cells, borehole_profiles, heat_table):
    matrix = vertical_matrix(vert_cond)
    fine_steps = [SPAN * (FINE_NODES[interval + 1] - FINE_NODES[interval]) for interval in range(4)]
    coarse_steps = [SPAN * (COARSE_NODES[interval + 1] - COARSE_NODES[interval]) for interval in range(2)]
    fine_props = [propagator(matrix, step_length) for step_length in fine_steps]
    coarse_props = [propagator(matrix, step_length) for step_length in coarse_steps]
    fine_integrals = node_integrals(FINE_NODES)
    weights = node_values(COARSE_NODES, FINE_NODES)
    coarse_conduct = restrict(conductivity)
    explicit_fine = partial(padded_lateral, conduct=conductivity, coefficient=LATERAL)
    explicit_coarse = partial(padded_lateral, conduct=coarse_conduct, coefficient=LATERAL / 4.0)
    explicit_init = explicit_fine(initial_temp)
    implicit_init = column_apply(matrix, initial_temp)
    earlier_fine = None
    earlier_coarse = None
    results = []
    for slice_index in range(SLICES):
        heat_plane = source_plane(borehole_cells, borehole_profiles, heat_table, slice_index)
        coarse_plane = restrict_plane(heat_plane)
        fine_state = [initial_temp] * 5
        fine_explicit = [explicit_init] * 5
        fine_implicit = [implicit_init] * 5
        fine_ends = []
        coarse_ends = []
        for sweep_index in range(ITERS):
            if slice_index == 0 or sweep_index == 0:
                start_value = initial_temp
            else:
                start_value = earlier_fine[sweep_index - 1]
            old_sums = integrate(fine_integrals, [fine_explicit[node_index] + fine_implicit[node_index] for node_index in range(5)])
            known_terms = [SPAN * old_sums[interval] + fine_steps[interval] * heat_plane - fine_steps[interval] * (fine_explicit[interval] + fine_implicit[interval + 1]) for interval in range(4)]
            fine_state, fine_explicit, fine_implicit = node_sweep(start_value, explicit_fine(start_value), column_apply(matrix, start_value), known_terms, fine_props, fine_steps, explicit_fine)
            new_sums = integrate(fine_integrals, [fine_explicit[node_index] + fine_implicit[node_index] for node_index in range(5)])
            coarse_old = [restrict(fine_state[0]), restrict(fine_state[2]), restrict(fine_state[4])]
            coarse_explicit_old = [explicit_coarse(member) for member in coarse_old]
            coarse_implicit_old = [column_apply(matrix, member) for member in coarse_old]
            coarse_known = [SPAN * restrict(new_sums[2 * interval] + new_sums[2 * interval + 1]) + coarse_steps[interval] * coarse_plane - coarse_steps[interval] * (coarse_explicit_old[interval] + coarse_implicit_old[interval + 1]) for interval in range(2)]
            if slice_index == 0:
                coarse_start = coarse_old[0]
            else:
                coarse_start = earlier_coarse[sweep_index]
            coarse_state, coarse_explicit, coarse_implicit = node_sweep(coarse_start, explicit_coarse(coarse_start), column_apply(matrix, coarse_start), coarse_known, coarse_props, coarse_steps, explicit_coarse)
            coarse_ends.append(coarse_state[2])
            delta_state = [coarse_state[member] - coarse_old[member] for member in range(3)]
            delta_explicit = [coarse_explicit[member] - coarse_explicit_old[member] for member in range(3)]
            delta_implicit = [coarse_implicit[member] - coarse_implicit_old[member] for member in range(3)]
            fine_state = correct(fine_state, delta_state, weights)
            fine_explicit = correct(fine_explicit, delta_explicit, weights)
            fine_implicit = correct(fine_implicit, delta_implicit, weights)
            fine_ends.append(fine_state[4])
        earlier_fine = fine_ends
        earlier_coarse = coarse_ends
        results.append(fine_state[4])
    return jnp.stack(results)
```

```python
import functools
import math

import jax
import jax.numpy as jnp
from jax import lax
from jax.experimental import pallas as pl
from jax.experimental.pallas import tpu as pltpu
from jax.sharding import PartitionSpec as P

F32 = jnp.float32
BF16 = jnp.bfloat16
LATERAL = 0.3
VERTICAL = 4.0
FINE_NODES = [0.0, (1.0 - math.sqrt(3.0 / 7.0)) / 2.0, 0.5, (1.0 + math.sqrt(3.0 / 7.0)) / 2.0, 1.0]
COARSE_NODES = [0.0, 0.5, 1.0]
HALF = 0.5
DEPTH = 64
TX = 8
CXT = 4
FX = 32
GX = 16
LANES = 128
MIB = 2**20


def basis_coeffs(times_list, basis_index):
    coeffs = [1.0]
    denominator = 1.0
    for other_index in range(len(times_list)):
        if other_index != basis_index:
            other_time = times_list[other_index]
            widened = [0.0] * (len(coeffs) + 1)
            for power in range(len(coeffs)):
                widened[power + 1] = widened[power + 1] + coeffs[power]
                widened[power] = widened[power] - other_time * coeffs[power]
            coeffs = widened
            denominator = denominator * (times_list[basis_index] - other_time)
    return [entry / denominator for entry in coeffs]


def poly_value(coeffs, point):
    return sum(coeffs[power] * point**power for power in range(len(coeffs)))


def poly_integral(coeffs, lower, upper):
    return sum(
        coeffs[power] * (upper ** (power + 1) - lower ** (power + 1)) / (power + 1)
        for power in range(len(coeffs))
    )


H = [FINE_NODES[m + 1] - FINE_NODES[m] for m in range(4)]
S = [
    [poly_integral(basis_coeffs(FINE_NODES, j), FINE_NODES[m], FINE_NODES[m + 1]) for j in range(5)]
    for m in range(4)
]
W = [[poly_value(basis_coeffs(COARSE_NODES, c), t) for c in range(3)] for t in FINE_NODES]
SC = [[S[2 * m][j] + S[2 * m + 1][j] for j in range(5)] for m in range(2)]
SW = [[sum(S[m][j] * W[j][c] for j in range(5)) for c in range(3)] for m in range(4)]
ALPHA = [[SW[m][c] - H[m] * W[m][c] for c in range(3)] for m in range(4)]
BETA = [[SW[m][c] - H[m] * W[m + 1][c] for c in range(3)] for m in range(4)]
KE = [[S[m][j] - (H[m] if j == m else 0.0) for j in range(5)] for m in range(4)]
KI = [[S[m][j] - (H[m] if j == m + 1 else 0.0) for j in range(5)] for m in range(4)]


def loop(count, body, unroll=1):
    def step(index, carry):
        body(index)
        return carry

    lax.fori_loop(0, count, step, 0, unroll=unroll)


def roll(value, shift):
    return pltpu.roll(value, shift % value.shape[-1], value.ndim - 1)


def lane(shape):
    return lax.broadcasted_iota(jnp.int32, shape, len(shape) - 1)


def apply4(lhs, value):
    high = value.astype(BF16)
    low = (value - high.astype(F32)).astype(BF16)
    stacked = jnp.concatenate([high, low, high, low], axis=0)
    return jnp.dot(lhs, stacked, preferred_element_type=F32)


def split3(value):
    high = value.astype(BF16)
    rest = value - high.astype(F32)
    mid = rest.astype(BF16)
    low = (rest - mid.astype(F32)).astype(BF16)
    return high, mid, low


def fine_lap(src, row):
    u = src[row + 1]
    even, odd = u[:, :LANES], u[:, LANES:]
    beside = jnp.concatenate([odd + roll(odd, 1), even + roll(even, -1)], axis=1)
    return u, (src[row] + src[row + 2]) + beside - 4.0 * u


def coarse_lap(src, row):
    u = src[row + 1]
    return u, (src[row] + src[row + 2]) + (roll(u, 1) + roll(u, -1)) - 4.0 * u


def pool(first, second):
    total = first + second
    return 0.25 * (total[:, :LANES] + total[:, LANES:])


def twice(value):
    return jnp.concatenate([value, value], axis=1)


def rows8(value):
    return jnp.concatenate([value] * (DEPTH // 8), axis=0)


def zero_edges(ref):
    edge = jnp.zeros(ref.shape[1:], F32)
    ref[0] = edge
    ref[ref.shape[0] - 1] = edge


def coarse_step(src, dst, cc, prop, known=None):
    for pair in range(GX // 2):
        parts = []
        for row in (2 * pair, 2 * pair + 1):
            u, lap = coarse_lap(src, row)
            rhs = u + HALF * (cc[row] * lap)
            parts.append(rhs if known is None else rhs + known[row])
        node = apply4(prop, jnp.concatenate(parts, axis=1))
        dst[2 * pair + 1] = node[:, :LANES]
        dst[2 * pair + 2] = node[:, LANES:]


def chain_power(first, second, cc, prop, steps):
    def body(_):
        coarse_step(first, second, cc, prop)
        coarse_step(second, first, cc, prop)

    loop(steps, body)


def sweep(bufs, cond, lhs, known, ga, uc, saved=None):
    for m in range(4):
        src, dst = bufs[m], bufs[m + 1]
        prop = lhs[0] if m in (0, 3) else lhs[1]

        def body(pair, m=m, src=src, dst=dst, prop=prop):
            us, es, im = [], [], []
            for row in (2 * pair, 2 * pair + 1):
                u, lap = fine_lap(src, row)
                e = cond[row] * lap
                rhs = u + H[m] * e + known(m, row)
                node = apply4(prop, rhs)
                dst[row + 1] = node
                i = (node - rhs) * (1.0 / H[m])
                if saved is not None:
                    saved[0][m, row] = e
                    saved[1][m + 1, row] = i
                us.append(u)
                es.append(e)
                im.append(i)
            e_sum, i_sum = pool(*es), pool(*im)
            for k in range(2):
                value = SC[k][m] * e_sum + SC[k][m + 1] * i_sum
                ga[k, pair] = value if m == 0 else ga[k, pair] + value
            if m in (0, 2):
                uc[m // 2][pair + 1] = pool(*us)

        loop(GX, body, unroll=4)

    def last(pair):
        us, es = [], []
        for row in (2 * pair, 2 * pair + 1):
            u, lap = fine_lap(bufs[4], row)
            us.append(u)
            es.append(cond[row] * lap)
            if saved is not None:
                finish_known(saved, row, es[-1])
        e_sum = pool(*es)
        for k in range(2):
            ga[k, pair] = ga[k, pair] + SC[k][4] * e_sum
        uc[2][pair + 1] = pool(*us)

    loop(GX, last, unroll=2)


def finish_known(saved, row, e_last):
    es, im, k0, plane = saved
    flat = rows8(plane[row])
    values = [es[j, row] for j in range(4)] + [e_last]
    implicit = [im[j, row] for j in range(5)]
    for m in range(4):
        total = H[m] * flat
        for j in range(5):
            total = total + KE[m][j] * values[j] + KI[m][j] * implicit[j]
        k0[m, row] = total


def coarse_known(ga, uc, cc, plane, lhs, kc, k0=None):
    matrix = lhs[3]

    def body(pair):
        rows = (2 * pair, 2 * pair + 1)
        ic, ec = [], []
        for c in range(3):
            laps = [coarse_lap(uc[c], row) for row in rows]
            ec.append([cc[row] * lap for row, (_, lap) in zip(rows, laps)])
            both = apply4(matrix, jnp.concatenate([u for u, _ in laps], axis=1))
            ic.append([both[:, :LANES], both[:, LANES:]])
        for place, row in enumerate(rows):
            flat = rows8(plane[row])
            for k in range(2):
                kc[k, row] = (
                    (ga[k, row] + SC[k][0] * ic[0][place])
                    + HALF * flat
                    - HALF * (ec[k][place] + ic[k + 1][place])
                )
            if k0 is not None:
                for m in range(4):
                    total = ALPHA[m][0] * ec[0][place] + BETA[m][0] * ic[0][place]
                    for c in (1, 2):
                        total = total + ALPHA[m][c] * ec[c][place] + BETA[m][c] * ic[c][place]
                    wide = twice(total)
                    k0[m, 2 * row] = k0[m, 2 * row] - wide
                    k0[m, 2 * row + 1] = k0[m, 2 * row + 1] - wide

    loop(GX // 2, body, unroll=2)


def pack(c_ref, base, main, to_right, to_left):
    rows = [c_ref[base + r] for r in range(CXT)]
    at = lane((DEPTH, LANES))
    for half in range(2):
        main[half] = jnp.where(at < 64, roll(rows[2 * half], -32), roll(rows[2 * half + 1], 32))
    for out, start in ((to_right, 64), (to_left, 32)):
        value = roll(rows[0], -start)
        for r in range(1, CXT):
            value = jnp.where(at < 32 * r, value, roll(rows[r], 32 * r - start))
        out[0] = value


def unpack(got, dst):
    at = lane((DEPTH, LANES))
    for g in range(GX // CXT):
        for r in range(CXT):
            centre = roll(got[g, r // 2], 32 if r % 2 == 0 else -32)
            left = roll(got[g, 2], -32 * r)
            right = roll(got[g, 3], 96 - 32 * r)
            value = jnp.where(at < 32, left, jnp.where(at < 96, centre, right))
            dst[CXT * g + r + 1] = value


def props_kernel(upper_ref, lower_ref, out_ref):
    upper, lower = upper_ref[...], lower_ref[...]
    shape = (DEPTH, LANES)
    row = lax.broadcasted_iota(jnp.int32, shape, 0)
    col = lane(shape)
    level = jnp.where(col < DEPTH, col, col - DEPTH)
    eye = jnp.where(row == level, 1.0, 0.0).astype(F32)

    def shifted(value, step):
        return pltpu.roll(value, step % DEPTH, 0)

    def inverse(length):
        a = -VERTICAL * length * jnp.where(row == 0, 0.0, upper)
        c = -VERTICAL * length * lower
        b = 1.0 + VERTICAL * length * (upper + lower)
        r = eye
        step = 1
        while step < DEPTH:
            alpha = -a / shifted(b, step)
            gamma = -c / shifted(b, -step)
            b, r, a, c = (
                b + alpha * shifted(c, step) + gamma * shifted(a, -step),
                r + alpha * shifted(r, step) + gamma * shifted(r, -step),
                alpha * shifted(a, step),
                gamma * shifted(c, -step),
            )
            step *= 2
        return r / b

    def store(index, value):
        high = value.astype(BF16)
        out_ref[index, :, :LANES] = high
        out_ref[index, :, LANES:] = (value - high.astype(F32)).astype(BF16)

    fine = inverse(jnp.where(col < DEPTH, H[0], H[1]).astype(F32))
    other = roll(fine, DEPTH)
    store(0, jnp.where(col < DEPTH, fine, other))
    store(1, jnp.where(col < DEPTH, other, fine))
    store(2, inverse(jnp.full(shape, HALF, F32)))
    matrix = jnp.where(row == level, -VERTICAL * (upper + lower), 0.0)
    matrix = matrix + jnp.where(level == row - 1, VERTICAL * upper, 0.0)
    matrix = matrix + jnp.where(level == row + 1, VERTICAL * lower, 0.0)
    store(3, matrix)


def prep_kernel(field_ref, count_ref, main, to_right, to_left):
    src = lax.broadcasted_iota(jnp.int32, (LANES, LANES), 0)
    dst = lane((LANES, LANES))
    target = jnp.where(dst < 64, 2 * dst, 2 * (dst - 64) + 1)
    pick = jnp.where(src == target, 1.0, 0.0).astype(BF16)
    for row in range(TX):
        main[row, : 2 * DEPTH] = sum(
            jnp.dot(part, pick, preferred_element_type=F32) for part in split3(field_ref[row])
        )
    counts = count_ref[...].reshape(TX * 8, LANES).astype(BF16)
    counts = jnp.dot(counts, pick, preferred_element_type=F32)
    for row in range(TX):
        main[row, 2 * DEPTH :] = counts[8 * row : 8 * row + 8]
    at = lane((2 * DEPTH + 8, LANES))
    for slab in range(TX // 2):
        low, high = main[slab], main[slab + TX // 2]
        to_right[slab] = jnp.where(
            at < 64,
            jnp.where(at < 32, roll(low, -32), roll(low, -64)),
            jnp.where(at < 96, roll(high, 32), high),
        )
        to_left[slab] = jnp.where(
            at < 64,
            jnp.where(at < 32, low, roll(low, -32)),
            jnp.where(at < 96, roll(high, 64), roll(high, 32)),
        )


def first_kernel(
    flags,
    place,
    main,
    strip,
    tables,
    lhs,
    c_out,
    hop,
    k0,
    v_out,
    kc_out,
    cc,
    cond,
    plane_c,
    init,
    buf_a,
    buf_b,
    planes,
    es,
    im,
    uc0,
    uc1,
    uc2,
    ga,
    kc,
    node_a,
    node_b,
    planes_c,
):
    for ref in (init, buf_a, buf_b, uc0, uc1, uc2, node_a, node_b):
        zero_edges(ref)
    at = lane((2 * DEPTH + 8, LANES))

    def assemble(g):
        for q in range(TX):
            row = TX * g + q
            centre = main[g, q]
            left, right = strip[g, q % 4], strip[g, 4 + q % 4]
            off = 64 * (q // 4)
            halves = []
            for odd in range(2):
                a = roll(left, -(off + 32 * odd))
                b = roll(centre, 32 if odd == 0 else -32)
                c = roll(right, 96 - off - 32 * odd)
                halves.append(jnp.where(at < 32, a, jnp.where(at < 96, b, c)))
            window = jnp.concatenate(halves, axis=1)
            init[row + 1] = window[:DEPTH]
            cond[row] = LATERAL * window[DEPTH : 2 * DEPTH]
            counts = window[2 * DEPTH :]
            for t in range(3):
                rate = jnp.concatenate([tables[t], tables[t]], axis=1)
                heat = jnp.sum(counts * rate, axis=0, keepdims=True)
                planes[t, row] = jnp.broadcast_to(heat, (8, 2 * LANES))

    loop(FX // TX, assemble)

    def coarsen(row):
        cc[row] = 0.25 * pool(cond[2 * row], cond[2 * row + 1])
        for t in range(3):
            planes_c[t, row] = pool(planes[t, 2 * row], planes[t, 2 * row + 1])

    loop(GX, coarsen, unroll=4)
    uc = (uc0, uc1, uc2)
    bufs = (init, buf_a, buf_b, buf_a, buf_b)
    prop = lhs[2]

    def start_from_zero():
        def body(pair):
            both = apply4(prop, jnp.concatenate([kc[0, 2 * pair], kc[0, 2 * pair + 1]], axis=1))
            node_b[2 * pair + 1] = both[:, :LANES]
            node_b[2 * pair + 2] = both[:, LANES:]

        loop(GX // 2, body, unroll=4)
        coarse_step(node_b, node_a, cc, prop, kc.at[1])

    def heat(t):
        return lambda m, row: H[m] * rows8(planes[t, row])

    sweep(bufs, cond, lhs, heat(2), ga, uc)
    coarse_known(ga, uc, cc, planes_c.at[2], lhs, kc)
    start_from_zero()
    after1, after2, is1, is0 = flags[0], flags[1], flags[2], flags[3]

    def choose2(row):
        node_a[row + 1] = after2 * node_a[row + 1] + is1 * uc0[row + 1]

    loop(GX, choose2, unroll=4)
    chain_power(node_a, node_b, cc, prop, 1)

    def keep(row):
        c_out[row] = node_a[row + 1]

    loop(GX, keep, unroll=4)
    sweep(bufs, cond, lhs, heat(1), ga, uc)
    coarse_known(ga, uc, cc, planes_c.at[1], lhs, kc)
    start_from_zero()

    def choose1(row):
        c_out[row] = c_out[row] + (after1 * node_a[row + 1] + is0 * uc0[row + 1])
        for fine in (2 * row, 2 * row + 1):
            before = buf_b[fine + 1] - twice(uc2[row + 1])
            here = init[fine + 1] - twice(uc0[row + 1])
            v_out[fine] = after1 * before + is0 * here

    loop(GX, choose1, unroll=2)
    for r in range(CXT):
        hop[r] = c_out[place[0] * CXT + r]

    def implicit_zero(row):
        im[0, row] = apply4(lhs[3], init[row + 1])

    loop(FX, implicit_zero, unroll=4)
    sweep(bufs, cond, lhs, heat(0), ga, uc, saved=(es, im, k0, planes.at[0]))
    coarse_known(ga, uc, cc, planes_c.at[0], lhs, kc_out, k0)

    def keep_plane(row):
        plane_c[row] = planes_c[0, row]

    loop(GX, keep_plane, unroll=4)


def phase_kernel(
    steps, strips_in, strips_out, place, got, c_in, cc, lhs, c_out, *rest
):
    node_a, node_b = rest[-2:]
    outs = rest[:-2]
    zero_edges(node_a)
    zero_edges(node_b)
    if strips_in:
        unpack(got, node_a)
    else:

        def load(row):
            node_a[row + 1] = got[row]

        loop(GX, load, unroll=4)
    chain_power(node_a, node_b, cc, lhs[2], steps)

    def add(row):
        c_out[row] = c_in[row] + node_a[row + 1]

    loop(GX, add, unroll=4)
    base = place[0] * CXT
    if strips_out:
        pack(c_out, base, *outs)
    else:
        for r in range(CXT):
            outs[0][r] = c_out[base + r]


def second_kernel(
    steps,
    flags,
    place,
    got,
    c_in,
    cc,
    lhs,
    k0,
    v,
    kc_in,
    cond,
    plane_c,
    c_out,
    hop,
    v_tile,
    start,
    buf_a,
    buf_b,
    dk,
    uc0,
    uc1,
    uc2,
    ga,
    kc,
    node_a,
    node_b,
    node_c,
):
    for ref in (start, buf_a, buf_b, uc0, uc1, uc2, node_a, node_b, node_c):
        zero_edges(ref)
    unpack(got, node_a)
    prop, matrix = lhs[2], lhs[3]
    chain_power(node_a, node_b, cc, prop, steps)

    def add(row):
        value = c_in[row] + node_a[row + 1]
        node_a[row + 1] = value
        wide = twice(value)
        start[2 * row + 1] = v[2 * row] + wide
        start[2 * row + 2] = v[2 * row + 1] + wide

    loop(GX, add, unroll=4)

    def spread(row, c, explicit, implicit, first):
        for m in range(4):
            total = ALPHA[m][c] * explicit + BETA[m][c] * implicit
            dk[m, row] = total if first else dk[m, row] + total

    def stage(c, src, dst):
        def body(pair):
            rows = (2 * pair, 2 * pair + 1)
            laps = [coarse_lap(src, row) for row in rows]
            ex = [cc[row] * lap for row, (_, lap) in zip(rows, laps)]
            if c == 0:
                both = apply4(matrix, jnp.concatenate([u for u, _ in laps], axis=1))
                spread(rows[0], 0, ex[0], both[:, :LANES], True)
                spread(rows[1], 0, ex[1], both[:, LANES:], True)
            else:
                spread(rows[0], c, ex[0], kc[c - 1, rows[0]], False)
                spread(rows[1], c, ex[1], kc[c - 1, rows[1]], False)
            if c < 2:
                rhs = jnp.concatenate(
                    [u + HALF * e + kc_in[c, row] for row, (u, _), e in zip(rows, laps, ex)],
                    axis=1,
                )
                node = apply4(prop, rhs)
                dst[rows[0] + 1] = node[:, :LANES]
                dst[rows[1] + 1] = node[:, LANES:]
                implicit = (node - rhs) * (1.0 / HALF)
                kc[c, rows[0]] = implicit[:, :LANES]
                kc[c, rows[1]] = implicit[:, LANES:]

        loop(GX // 2, body, unroll=2)

    stage(0, node_a, node_b)
    stage(1, node_b, node_c)
    stage(2, node_c, None)

    def known(m, row):
        return k0[m, row] + twice(dk[m, row // 2])

    uc = (uc0, uc1, uc2)
    sweep((start, buf_a, buf_b, buf_a, buf_b), cond, lhs, known, ga, uc)
    coarse_known(ga, uc, cc, plane_c, lhs, kc)
    is0 = flags[3]

    def begin(row):
        node_a[row + 1] = is0 * uc0[row + 1]

    loop(GX, begin, unroll=4)
    coarse_step(node_a, node_b, cc, prop, kc.at[0])
    coarse_step(node_b, node_a, cc, prop, kc.at[1])

    def keep(row):
        c_out[row] = node_a[row + 1]

    loop(GX, keep, unroll=4)
    base = place[0] * CXT
    for r in range(CXT):
        hop[r] = c_out[base + r]
        for q in range(2):
            fine = 2 * r + q
            v_tile[fine] = buf_b[2 * base + fine + 1] - twice(uc2[base + r + 1])


def last_kernel(steps, place, got, c_in, cc, lhs, v_tile, out, node_a, node_b):
    zero_edges(node_a)
    zero_edges(node_b)
    unpack(got, node_a)
    chain_power(node_a, node_b, cc, lhs[2], steps)
    base = place[0] * CXT
    src = lax.broadcasted_iota(jnp.int32, (2 * LANES, LANES), 0)
    dst = lane((2 * LANES, LANES))
    target = 32 + dst // 2 + jnp.where(dst % 2 == 1, LANES, 0)
    pick = jnp.where(src == target, 1.0, 0.0).astype(BF16)
    for r in range(CXT):
        wide = twice(c_in[base + r] + node_a[base + r + 1])
        for q in range(2):
            value = v_tile[2 * r + q] + wide
            out[2 * r + q] = sum(
                jnp.dot(part, pick, preferred_element_type=F32) for part in split3(value)
            )


VMEM = pl.BlockSpec(memory_space=pltpu.VMEM)
SMEM = pl.BlockSpec(memory_space=pltpu.SMEM)


def shape(*dims, dtype=F32):
    return jax.ShapeDtypeStruct(dims, dtype)


def call(kernel, name, outs, scratch, smem, *operands, limit=40, flops=10**8):
    return pl.pallas_call(
        kernel,
        name=name,
        out_shape=outs,
        in_specs=[SMEM] * smem + [VMEM] * (len(operands) - smem),
        out_specs=jax.tree.map(lambda _: VMEM, outs),
        scratch_shapes=[pltpu.VMEM(dims, F32) for dims in scratch],
        compiler_params=pltpu.CompilerParams(vmem_limit_bytes=limit * MIB),
        cost_estimate=pl.CostEstimate(flops=flops, bytes_accessed=10**6, transcendentals=0),
    )(*operands)


COARSE = (GX, DEPTH, LANES)
COARSE_PAD = (GX + 2, DEPTH, LANES)
FINE = (FX, DEPTH, 2 * LANES)
FINE_PAD = (FX + 2, DEPTH, 2 * LANES)
HOP = (CXT, DEPTH, LANES)


def shift(value, steps, sideways=0):
    slices, columns = lax.axis_size("tm"), lax.axis_size("gy")
    pairs = [
        (s * columns + g, (s + steps) * columns + g + sideways)
        for s in range(slices - steps)
        for g in range(columns)
        if 0 <= g + sideways < columns
    ]
    return lax.ppermute(value, ("tm", "gy"), pairs)


def fetch_plain(hop, steps):
    return lax.all_gather(shift(hop, steps), "gx").reshape(COARSE)


def fetch_strips(main, to_right, to_left, steps):
    parts = [shift(main, steps), shift(to_right, steps, 1), shift(to_left, steps, -1)]
    return lax.all_gather(jnp.concatenate(parts, axis=0), "gx")


def on_device(initial_temp, conductivity, vert_cond, borehole_cells, borehole_profiles, heat_table):
    slice_index = lax.axis_index("tm")
    place = lax.axis_index("gx").astype(jnp.int32).reshape(1)
    flags = jnp.stack(
        [slice_index >= 1, slice_index >= 2, slice_index == 1, slice_index == 0]
    ).astype(F32)
    profiles = heat_table.shape[0]
    tables = jnp.stack([heat_table, shift(heat_table, 1), shift(heat_table, 2)])
    tables = jnp.broadcast_to(tables, (3, profiles, LANES))
    cells = borehole_cells.reshape(-1)
    which = borehole_profiles.reshape(-1)
    at_cell = cells[:, None, None, None] == (
        jnp.arange(TX)[:, None, None] * LANES + jnp.arange(LANES)[None, None, :]
    )
    at_profile = which[:, None, None, None] == jnp.arange(profiles)[None, :, None]
    counts = jnp.sum((at_cell & at_profile).astype(F32), axis=0)

    fields = jnp.transpose(jnp.concatenate([initial_temp, conductivity], axis=0), (1, 0, 2))
    main, to_right, to_left = call(
        prep_kernel,
        "prep",
        [
            shape(TX, 2 * DEPTH + 8, LANES),
            shape(TX // 2, 2 * DEPTH + 8, LANES),
            shape(TX // 2, 2 * DEPTH + 8, LANES),
        ],
        [],
        0,
        fields,
        counts,
    )
    strip = jnp.concatenate([shift(to_right, 0, 1), shift(to_left, 0, -1)], axis=0)
    main = lax.all_gather(main, "gx")
    strip = lax.all_gather(strip, "gx")
    upper = jnp.broadcast_to(vert_cond[:, None], (DEPTH, LANES))
    lower = jnp.concatenate([vert_cond[1:], jnp.zeros((1,), F32)])
    lower = jnp.broadcast_to(lower[:, None], (DEPTH, LANES))
    lhs = call(
        props_kernel, "props", shape(4, DEPTH, 2 * LANES, dtype=BF16), [], 0, upper, lower
    )

    c, hop, k0, v, kc, cc, cond, plane_c = call(
        first_kernel,
        "first_sweeps",
        [
            shape(*COARSE),
            shape(*HOP),
            shape(4, *FINE),
            shape(*FINE),
            shape(2, *COARSE),
            shape(*COARSE),
            shape(*FINE),
            shape(GX, 8, LANES),
        ],
        [
            FINE_PAD,
            FINE_PAD,
            FINE_PAD,
            (3, FX, 8, 2 * LANES),
            (4, *FINE),
            (5, *FINE),
            COARSE_PAD,
            COARSE_PAD,
            COARSE_PAD,
            (2, *COARSE),
            (2, *COARSE),
            COARSE_PAD,
            COARSE_PAD,
            (3, GX, 8, LANES),
        ],
        2,
        flags,
        place,
        main,
        strip,
        tables,
        lhs,
        limit=60,
    )

    packed = [shape(2, DEPTH, LANES), shape(1, DEPTH, LANES), shape(1, DEPTH, LANES)]

    def phase(steps, name, got, c, strips_in, strips_out):
        outs = [shape(*COARSE)] + (packed if strips_out else [shape(*HOP)])
        kernel = functools.partial(phase_kernel, steps, strips_in, strips_out)
        c, *hops = call(
            kernel, name, outs, [COARSE_PAD, COARSE_PAD], 1, place, got, c, cc, lhs
        )
        return c, hops

    c, (hop,) = phase(2, "chain_a2", fetch_plain(hop, 2), c, False, False)
    c, hops = phase(4, "chain_a4", fetch_plain(hop, 4), c, False, True)
    got = fetch_strips(*hops, 8)
    c, hop, v_tile = call(
        functools.partial(second_kernel, 8),
        "second_sweep",
        [shape(*COARSE), shape(*HOP), shape(TX, DEPTH, 2 * LANES)],
        [
            FINE_PAD,
            FINE_PAD,
            FINE_PAD,
            (4, *COARSE),
            COARSE_PAD,
            COARSE_PAD,
            COARSE_PAD,
            (2, *COARSE),
            (2, *COARSE),
            COARSE_PAD,
            COARSE_PAD,
            COARSE_PAD,
        ],
        2,
        flags,
        place,
        got,
        c,
        cc,
        lhs,
        k0,
        v,
        kc,
        cond,
        plane_c,
        limit=60,
    )
    c, (hop,) = phase(1, "chain_b1", fetch_plain(hop, 1), c, False, False)
    c, hops = phase(2, "chain_b2", fetch_plain(hop, 2), c, False, True)
    c, hops = phase(4, "chain_b4", fetch_strips(*hops, 4), c, True, True)
    out = call(
        functools.partial(last_kernel, 8),
        "finish",
        shape(TX, DEPTH, LANES),
        [COARSE_PAD, COARSE_PAD],
        1,
        place,
        fetch_strips(*hops, 8),
        c,
        cc,
        lhs,
        v_tile,
    )
    return jnp.transpose(out, (1, 0, 2))[None]


def solution(mesh):
    placed = (
        P(None, "gx", "gy"),
        P(None, "gx", "gy"),
        P(),
        P("gx", "gy", None),
        P("gx", "gy", None),
        P(None, "tm"),
    )
    return jax.shard_map(
        on_device, mesh=mesh, in_specs=placed, out_specs=P("tm", None, "gx", "gy"), check_vma=False
    )
```

```python
import functools
import math

import jax
import jax.numpy as jnp
from jax import lax
from jax.experimental import pallas as pl
from jax.experimental.pallas import tpu as pltpu
from jax.sharding import PartitionSpec as P

F32 = jnp.float32
BF16 = jnp.bfloat16
LATERAL = 0.3
VERTICAL = 4.0
FINE_NODES = [0.0, (1.0 - math.sqrt(3.0 / 7.0)) / 2.0, 0.5, (1.0 + math.sqrt(3.0 / 7.0)) / 2.0, 1.0]
COARSE_NODES = [0.0, 0.5, 1.0]
HALF = 0.5
DEPTH = 64
TX = 8
CXT = 4
FX = 32
GX = 16
LANES = 128
MIB = 2**20


def basis_coeffs(times_list, basis_index):
    coeffs = [1.0]
    denominator = 1.0
    for other_index in range(len(times_list)):
        if other_index != basis_index:
            other_time = times_list[other_index]
            widened = [0.0] * (len(coeffs) + 1)
            for power in range(len(coeffs)):
                widened[power + 1] = widened[power + 1] + coeffs[power]
                widened[power] = widened[power] - other_time * coeffs[power]
            coeffs = widened
            denominator = denominator * (times_list[basis_index] - other_time)
    return [entry / denominator for entry in coeffs]


def poly_value(coeffs, point):
    return sum(coeffs[power] * point**power for power in range(len(coeffs)))


def poly_integral(coeffs, lower, upper):
    return sum(
        coeffs[power] * (upper ** (power + 1) - lower ** (power + 1)) / (power + 1)
        for power in range(len(coeffs))
    )


H = [FINE_NODES[m + 1] - FINE_NODES[m] for m in range(4)]
S = [
    [poly_integral(basis_coeffs(FINE_NODES, j), FINE_NODES[m], FINE_NODES[m + 1]) for j in range(5)]
    for m in range(4)
]
W = [[poly_value(basis_coeffs(COARSE_NODES, c), t) for c in range(3)] for t in FINE_NODES]
SC = [[S[2 * m][j] + S[2 * m + 1][j] for j in range(5)] for m in range(2)]
SW = [[sum(S[m][j] * W[j][c] for j in range(5)) for c in range(3)] for m in range(4)]
ALPHA = [[SW[m][c] - H[m] * W[m][c] for c in range(3)] for m in range(4)]
BETA = [[SW[m][c] - H[m] * W[m + 1][c] for c in range(3)] for m in range(4)]


def loop(count, body, unroll=1):
    def step(index, carry):
        body(index)
        return carry

    lax.fori_loop(0, count, step, 0, unroll=unroll)


def roll(value, shift):
    return pltpu.roll(value, shift % value.shape[-1], value.ndim - 1)


def lane(shape):
    return lax.broadcasted_iota(jnp.int32, shape, len(shape) - 1)


def apply4(lhs, value):
    high = value.astype(BF16)
    low = (value - high.astype(F32)).astype(BF16)
    stacked = jnp.concatenate([high, low, high, low], axis=0)
    return jnp.dot(lhs, stacked, preferred_element_type=F32)


def split3(value):
    high = value.astype(BF16)
    rest = value - high.astype(F32)
    mid = rest.astype(BF16)
    low = (rest - mid.astype(F32)).astype(BF16)
    return high, mid, low


def fine_lap(src, row):
    u = src[row + 1]
    even, odd = u[:, :LANES], u[:, LANES:]
    beside = jnp.concatenate([odd + roll(odd, 1), even + roll(even, -1)], axis=1)
    return u, (src[row] + src[row + 2]) + beside - 4.0 * u


def coarse_lap(src, row):
    u = src[row + 1]
    return u, (src[row] + src[row + 2]) + (roll(u, 1) + roll(u, -1)) - 4.0 * u


def pool(first, second):
    total = first + second
    return 0.25 * (total[:, :LANES] + total[:, LANES:])


def twice(value):
    return jnp.concatenate([value, value], axis=1)


def rows8(value):
    return jnp.concatenate([value] * (DEPTH // 8), axis=0)


def zero_edges(ref):
    edge = jnp.zeros(ref.shape[1:], F32)
    ref[0] = edge
    ref[ref.shape[0] - 1] = edge


def coarse_step(src, dst, cc, prop, known=None, count=GX, base=0):
    for pair in range(count // 2):
        parts = []
        for row in (2 * pair, 2 * pair + 1):
            u, lap = coarse_lap(src, row)
            rhs = u + cc[base + row] * lap
            parts.append(rhs if known is None else rhs + known[row])
        node = apply4(prop, jnp.concatenate(parts, axis=1))
        dst[2 * pair + 1] = node[:, :LANES]
        dst[2 * pair + 2] = node[:, LANES:]


def chain_power(first, second, cc, prop, steps, count=GX, base=0):
    each = min(steps, 4)

    def body(_):
        for _ in range(each):
            coarse_step(first, second, cc, prop, None, count, base)
            coarse_step(second, first, cc, prop, None, count, base)

    if steps == each:
        body(0)
    else:
        loop(steps // each, body)


def sweep(bufs, cond, lhs, known, pu, pe, pr=None, es=None):
    for m in range(4):
        src, dst = bufs[m], bufs[m + 1]
        prop = lhs[0] if m in (0, 3) else lhs[1]

        def body(pair, m=m, src=src, dst=dst, prop=prop):
            us, ex, rs = [], [], []
            for row in (2 * pair, 2 * pair + 1):
                u, lap = fine_lap(src, row)
                e = cond[row] * lap
                rhs = u + H[m] * e + known(m, row)
                dst[row + 1] = apply4(prop, rhs)
                if es is not None:
                    es[m, row] = e
                us.append(u)
                ex.append(e)
                rs.append(rhs)
            pu[m, pair + 1] = pool(*us)
            pe[m, pair] = pool(*ex)
            if pr is not None:
                pr[m, pair] = pool(*rs)

        loop(GX, body, unroll=8)

    def last(pair):
        us, ex = [], []
        for row in (2 * pair, 2 * pair + 1):
            u, lap = fine_lap(bufs[4], row)
            e = cond[row] * lap
            if es is not None:
                es[4, row] = e
            us.append(u)
            ex.append(e)
        pu[4, pair + 1] = pool(*us)
        pe[4, pair] = pool(*ex)

    loop(GX, last, unroll=8)


def coarse_known(pu, pe, pr, cc, plane, lhs, kc, olds=None):
    matrix = lhs[3]

    def body(pair):
        rows = (2 * pair, 2 * pair + 1)
        ic, ec = [], []
        for c in range(3):
            laps = [coarse_lap(pu.at[2 * c], row) for row in rows]
            ec.append([cc[row] * lap for row, (_, lap) in zip(rows, laps)])
            both = apply4(matrix, jnp.concatenate([u for u, _ in laps], axis=1))
            ic.append([both[:, :LANES], both[:, LANES:]])
        for place, row in enumerate(rows):
            flat = rows8(plane[row])
            u = [pu[j, row + 1] for j in range(5)]
            e = [pe[j, row] for j in range(5)]
            total = [e[0] + ic[0][place]]
            for m in range(4):
                if pr is None:
                    im = (u[m + 1] - u[m]) * (1.0 / H[m]) - (e[m] + flat)
                else:
                    im = (u[m + 1] - pr[m, row]) * (1.0 / H[m])
                total.append(e[m + 1] + im)
            for k in range(2):
                value = HALF * (flat - ic[k + 1][place]) - ec[k][place]
                for j in range(5):
                    value = value + SC[k][j] * total[j]
                kc[k, row] = value
            if olds is not None:
                for c in range(3):
                    olds[c, row] = 2.0 * ec[c][place]
                    olds[3 + c, row] = ic[c][place]

    loop(GX // 2, body, unroll=2)


def finish_known(bufs, es, olds, plane, matrix, k0):
    def body(pair):
        wide = []
        for m in range(4):
            total = ALPHA[m][0] * olds[0, pair] + BETA[m][0] * olds[3, pair]
            for c in (1, 2):
                total = total + ALPHA[m][c] * olds[c, pair] + BETA[m][c] * olds[3 + c, pair]
            wide.append(twice(total))
        for row in (2 * pair, 2 * pair + 1):
            flat = rows8(plane[row])
            u = [buf[row + 1] for buf in bufs]
            e = [es[j, row] for j in range(5)]
            total = [e[0] + apply4(matrix, u[0])]
            change = [u[m + 1] - u[m] for m in range(4)]
            for m in range(4):
                total.append(e[m + 1] + (change[m] * (1.0 / H[m]) - (e[m] + flat)))
            for m in range(4):
                value = (2.0 * H[m]) * flat - (change[m] + wide[m])
                for j in range(5):
                    value = value + S[m][j] * total[j]
                k0[m, row] = value

    loop(GX, body, unroll=4)


def pack(c_ref, base, count, main, to_right, to_left):
    at = lane((DEPTH, LANES))
    for quad in range(count // 4):
        rows = [c_ref[base + 4 * quad + r] for r in range(4)]
        for half in range(2):
            main[2 * quad + half] = jnp.where(
                at < 64, roll(rows[2 * half], -32), roll(rows[2 * half + 1], 32)
            )
        for out, start in ((to_right, 64), (to_left, 32)):
            value = roll(rows[0], -start)
            for r in range(1, 4):
                value = jnp.where(at < 32 * r, value, roll(rows[r], 32 * r - start))
            out[quad] = value


def unpack(main, left, right, count, dst, base):
    at = lane((DEPTH, LANES))
    for quad in range(count // 4):
        for r in range(4):
            centre = roll(main[2 * quad + r // 2], 32 if r % 2 == 0 else -32)
            before = roll(left[quad], -32 * r)
            after = roll(right[quad], 96 - 32 * r)
            value = jnp.where(at < 32, before, jnp.where(at < 96, centre, after))
            dst[base + 4 * quad + r + 1] = value


def put(rows, count, dst, base):
    for r in range(count):
        dst[base + r + 1] = rows[r]


def receive(kind, got, dst):
    gx = lax.axis_index("gx")
    if kind == "quads":
        for k, rows in zip((0, 1, 2, 3), got):
            put(rows, CXT, dst, CXT * lax.bitwise_xor(gx, k))
    elif kind == "quads packed":
        for k, slabs in zip((0, 1, 2, 3), got):
            base = CXT * lax.bitwise_xor(gx, k)
            unpack(slabs, slabs.at[pl.ds(2, 1)], slabs.at[pl.ds(3, 1)], CXT, dst, base)
    else:
        core = lax.bitwise_and(gx, 1)
        for k in range(2):
            unpack(*got[3 * k : 3 * k + 3], 8, dst, 8 * lax.bitwise_xor(core, k))


def window_base():
    return jnp.clip(CXT * lax.axis_index("gx") - 2, 0, 8)


def send(kind, c_ref, outs):
    gx = lax.axis_index("gx")
    if kind == "quads":
        for r in range(CXT):
            outs[0][r] = c_ref[CXT * gx + r]
    elif kind == "quads packed":
        pack(c_ref, CXT * gx, CXT, *outs)
    elif kind == "halves packed":
        pack(c_ref, 8 * lax.bitwise_and(gx, 1), 8, *outs)
    else:
        base = window_base()
        for r in range(8):
            outs[0][r] = c_ref[base + r]


def outs_of(kind):
    if kind == "quads":
        return [shape(CXT, DEPTH, LANES)]
    if kind == "window":
        return [shape(8, DEPTH, LANES)]
    count = 1 if kind == "quads packed" else 2
    return [shape(2 * count, DEPTH, LANES)] + [shape(count, DEPTH, LANES)] * 2


def takes(kind):
    return {"quads": 4, "quads packed": 4, "halves packed": 6, "window": 1}[kind]


def is_from(steps):
    return jnp.where(lax.axis_index("tm") >= steps, 1.0, 0.0).astype(F32)


def props_kernel(upper_ref, lower_ref, out_ref):
    upper, lower = upper_ref[...], lower_ref[...]
    shape = (DEPTH, LANES)
    row = lax.broadcasted_iota(jnp.int32, shape, 0)
    col = lane(shape)
    level = jnp.where(col < DEPTH, col, col - DEPTH)
    eye = jnp.where(row == level, 1.0, 0.0).astype(F32)

    def shifted(value, step):
        return pltpu.roll(value, step % DEPTH, 0)

    def inverse(length):
        a = -VERTICAL * length * jnp.where(row == 0, 0.0, upper)
        c = -VERTICAL * length * lower
        b = 1.0 + VERTICAL * length * (upper + lower)
        r = eye
        step = 1
        while step < DEPTH:
            alpha = -a / shifted(b, step)
            gamma = -c / shifted(b, -step)
            b, r, a, c = (
                b + alpha * shifted(c, step) + gamma * shifted(a, -step),
                r + alpha * shifted(r, step) + gamma * shifted(r, -step),
                alpha * shifted(a, step),
                gamma * shifted(c, -step),
            )
            step *= 2
        return r / b

    def store(index, value):
        high = value.astype(BF16)
        out_ref[index, :, :LANES] = high
        out_ref[index, :, LANES:] = (value - high.astype(F32)).astype(BF16)

    fine = inverse(jnp.where(col < DEPTH, H[0], H[1]).astype(F32))
    other = roll(fine, DEPTH)
    store(0, jnp.where(col < DEPTH, fine, other))
    store(1, jnp.where(col < DEPTH, other, fine))
    store(2, inverse(jnp.full(shape, HALF, F32)))
    matrix = jnp.where(row == level, -VERTICAL * (upper + lower), 0.0)
    matrix = matrix + jnp.where(level == row - 1, VERTICAL * upper, 0.0)
    matrix = matrix + jnp.where(level == row + 1, VERTICAL * lower, 0.0)
    store(3, matrix)


def prep_kernel(cells, profiles, temp, conduct, main, to_right, to_left, counts):
    src = lax.broadcasted_iota(jnp.int32, (LANES, LANES), 0)
    dst = lane((LANES, LANES))
    target = jnp.where(dst < 64, 2 * dst, 2 * (dst - 64) + 1)
    pick = jnp.where(src == target, 1.0, 0.0).astype(BF16)
    for row in range(TX):
        for place, ref in enumerate((temp, conduct)):
            main[row, DEPTH * place : DEPTH * (place + 1)] = sum(
                jnp.dot(part, pick, preferred_element_type=F32) for part in split3(ref[:, row, :])
            )
    counts[...] = jnp.zeros_like(counts)
    at = lane((8, LANES))
    profile = lax.broadcasted_iota(jnp.int32, (8, LANES), 0)
    for b in range(16):
        cell, which = cells[b], profiles[b]
        row, y = cell // LANES, cell % LANES
        column = y // 2 + jnp.where(y % 2 == 1, 64, 0)
        hit = (at == column) & (profile == which)
        counts[row] = counts[row] + jnp.where(hit, 1.0, 0.0)
    for row in range(TX):
        main[row, 2 * DEPTH :] = counts[row]
    at = lane((2 * DEPTH + 8, LANES))
    for slab in range(TX // 2):
        low, high = main[slab], main[slab + TX // 2]
        to_right[slab] = jnp.where(
            at < 64,
            jnp.where(at < 32, roll(low, -32), roll(low, -64)),
            jnp.where(at < 96, roll(high, 32), high),
        )
        to_left[slab] = jnp.where(
            at < 64,
            jnp.where(at < 32, low, roll(low, -32)),
            jnp.where(at < 96, roll(high, 64), roll(high, 32)),
        )


def first_kernel(
    main0,
    main1,
    main2,
    main3,
    strip0,
    strip1,
    strip2,
    strip3,
    table0,
    table1,
    table2,
    lhs,
    c_out,
    hop,
    k0_out,
    v_out,
    kc_out,
    cc,
    cond_out,
    plane_c,
    init,
    node_1,
    node_2,
    node_3,
    node_4,
    cond,
    k0,
    planes,
    planes_c,
    es,
    pu,
    pe,
    olds,
    kc,
    node_a,
    node_b,
    sems,
):
    bufs = (init, node_1, node_2, node_3, node_4)
    for ref in bufs + (node_a, node_b):
        zero_edges(ref)
    for j in range(5):
        zero_edges(pu.at[j])
    gx = lax.axis_index("gx")
    at = lane((2 * DEPTH + 8, LANES))
    rates = [jnp.broadcast_to(t[...], (8, 2 * LANES)) for t in (table0, table2, table1)]
    for k, (main, strip) in enumerate(
        ((main0, strip0), (main1, strip1), (main2, strip2), (main3, strip3))
    ):
        base = TX * lax.bitwise_xor(gx, k)

        def assemble(q, main=main, strip=strip, base=base):
            for off in (0, 64):
                row = q + off // 16
                centre = main[row]
                left, right = strip[q], strip[4 + q]
                halves = []
                for odd in range(2):
                    a = roll(left, -(off + 32 * odd))
                    b = roll(centre, 32 if odd == 0 else -32)
                    c = roll(right, 96 - off - 32 * odd)
                    halves.append(jnp.where(at < 32, a, jnp.where(at < 96, b, c)))
                window = jnp.concatenate(halves, axis=1)
                init[base + row + 1] = window[:DEPTH]
                cond[base + row] = LATERAL * window[DEPTH : 2 * DEPTH]
                counts = window[2 * DEPTH :]
                for t in range(3):
                    heat = jnp.sum(counts * rates[t], axis=0, keepdims=True)
                    planes[t, base + row] = jnp.broadcast_to(heat, (8, 2 * LANES))

        loop(TX // 2, assemble, unroll=2)
    copy_cond = pltpu.make_async_copy(cond, cond_out, sems.at[0])
    copy_cond.start()

    def coarsen(row):
        cc[row] = (0.25 * HALF) * pool(cond[2 * row], cond[2 * row + 1])
        for t in range(3):
            planes_c[t, row] = pool(planes[t, 2 * row], planes[t, 2 * row + 1])
        plane_c[row] = planes_c[0, row]

    loop(GX, coarsen, unroll=4)
    prop = lhs[2]
    copy_k0 = pltpu.make_async_copy(k0, k0_out, sems.at[1])

    def one_slice(t):
        sweep(bufs, cond, lhs, lambda m, row: rows8(H[m] * planes[t, row]), pu, pe, None, es)
        coarse_known(pu, pe, None, cc, planes_c.at[t], lhs, kc, olds)

        @pl.when(t == 0)
        def _():
            finish_known(bufs, es, olds, planes.at[0], lhs[3], k0)
            copy_k0.start()
            for k in range(2):
                for row in range(GX):
                    kc_out[k, row] = kc[k, row]

        @pl.when(t > 0)
        def _():
            for pair in range(GX // 2):
                both = apply4(
                    prop, jnp.concatenate([kc[0, 2 * pair], kc[0, 2 * pair + 1]], axis=1)
                )
                node_b[2 * pair + 1] = both[:, :LANES]
                node_b[2 * pair + 2] = both[:, LANES:]
            coarse_step(node_b, node_a, cc, prop, kc.at[1])

        @pl.when(t == 1)
        def _():
            after2 = is_from(2)
            is1 = is_from(1) - after2

            def choose(row):
                node_a[row + 1] = after2 * node_a[row + 1] + is1 * pu[0, row + 1]

            loop(GX, choose, unroll=4)
            chain_power(node_a, node_b, cc, prop, 1)

            def keep(row):
                c_out[row] = node_a[row + 1]

            loop(GX, keep, unroll=4)

    loop(3, one_slice)
    after1 = is_from(1)
    is0 = 1.0 - after1

    def choose(row):
        c_out[row] = c_out[row] + (after1 * node_a[row + 1] + is0 * pu[0, row + 1])
        for fine in (2 * row, 2 * row + 1):
            before = node_4[fine + 1] - twice(pu[4, row + 1])
            here = init[fine + 1] - twice(pu[0, row + 1])
            v_out[fine] = after1 * before + is0 * here

    loop(GX, choose, unroll=4)
    send("quads", c_out, [hop])
    copy_cond.wait()
    copy_k0.wait()


def phase_kernel(steps, kind_in, kind_out, *refs):
    count = takes(kind_in)
    got, (c_in, cc, lhs, c_out), rest = refs[:count], refs[count : count + 4], refs[count + 4 :]
    outs, (node_a, node_b) = rest[:-2], rest[-2:]
    zero_edges(node_a)
    zero_edges(node_b)
    receive(kind_in, got, node_a)
    chain_power(node_a, node_b, cc, lhs[2], steps)
    here = is_from(steps)

    def add(row):
        c_out[row] = c_in[row] + here * node_a[row + 1]

    loop(GX, add, unroll=8)
    send(kind_out, c_out, outs)


def second_kernel(
    steps,
    main_a,
    left_a,
    right_a,
    main_b,
    left_b,
    right_b,
    c_in,
    cc,
    lhs,
    k0_in,
    v_in,
    kc_in,
    cond_in,
    plane_c,
    c_out,
    hop,
    to_right,
    to_left,
    v_tile,
    k0,
    v,
    cond,
    start,
    buf_a,
    buf_b,
    dk,
    pu,
    pe,
    pr,
    kc,
    node_a,
    node_b,
    node_c,
    sems,
):
    copies = [
        pltpu.make_async_copy(src, dst, sems.at[place])
        for place, (src, dst) in enumerate(((v_in, v), (cond_in, cond), (k0_in, k0)))
    ]
    for copy in copies:
        copy.start()
    for ref in (start, buf_a, buf_b, node_a, node_b, node_c):
        zero_edges(ref)
    for j in range(5):
        zero_edges(pu.at[j])
    receive("halves packed", (main_a, left_a, right_a, main_b, left_b, right_b), node_a)
    prop, matrix = lhs[2], lhs[3]
    chain_power(node_a, node_b, cc, prop, steps)
    here = is_from(steps)
    copies[0].wait()

    def add(row):
        value = c_in[row] + here * node_a[row + 1]
        node_a[row + 1] = value
        wide = twice(value)
        start[2 * row + 1] = v[2 * row] + wide
        start[2 * row + 2] = v[2 * row + 1] + wide

    loop(GX, add, unroll=4)

    def spread(row, c, explicit, implicit):
        for m in range(4):
            total = (2.0 * ALPHA[m][c]) * explicit + BETA[m][c] * implicit
            dk[m, row] = total if c == 0 else dk[m, row] + total

    def stage(c, src, dst):
        def body(pair):
            rows = (2 * pair, 2 * pair + 1)
            laps = [coarse_lap(src, row) for row in rows]
            ex = [cc[row] * lap for row, (_, lap) in zip(rows, laps)]
            if c == 0:
                both = apply4(matrix, jnp.concatenate([u for u, _ in laps], axis=1))
                implicit = (both[:, :LANES], both[:, LANES:])
            else:
                implicit = (kc[c - 1, rows[0]], kc[c - 1, rows[1]])
            for place in range(2):
                spread(rows[place], c, ex[place], implicit[place])
            if c < 2:
                rhs = jnp.concatenate(
                    [u + e + kc_in[c, row] for row, (u, _), e in zip(rows, laps, ex)], axis=1
                )
                node = apply4(prop, rhs)
                dst[rows[0] + 1] = node[:, :LANES]
                dst[rows[1] + 1] = node[:, LANES:]
                after = (node - rhs) * (1.0 / HALF)
                kc[c, rows[0]] = after[:, :LANES]
                kc[c, rows[1]] = after[:, LANES:]

        loop(GX // 2, body, unroll=4)

    stage(0, node_a, node_b)
    stage(1, node_b, node_c)
    stage(2, node_c, None)
    copies[1].wait()
    copies[2].wait()

    def known(m, row):
        return k0[m, row] + twice(dk[m, row // 2])

    sweep((start, buf_a, buf_b, buf_a, buf_b), cond, lhs, known, pu, pe, pr)
    coarse_known(pu, pe, pr, cc, plane_c, lhs, kc)
    is0 = 1.0 - is_from(1)

    def begin(row):
        node_a[row + 1] = is0 * pu[0, row + 1]

    loop(GX, begin, unroll=4)
    coarse_step(node_a, node_b, cc, prop, kc.at[0])
    coarse_step(node_b, node_a, cc, prop, kc.at[1])

    def keep(row):
        c_out[row] = node_a[row + 1]

    loop(GX, keep, unroll=4)
    send("halves packed", c_out, (hop, to_right, to_left))
    base = CXT * lax.axis_index("gx")
    for r in range(CXT):
        for q in range(2):
            fine = 2 * r + q
            v_tile[fine] = buf_b[2 * base + fine + 1] - twice(pu[4, base + r + 1])


def last_kernel(got, c_in, cc, lhs, v_tile, out, node_a, node_b):
    zero_edges(node_a)
    zero_edges(node_b)
    put(got, 8, node_a, 0)
    base = window_base()
    coarse_step(node_a, node_b, cc, lhs[2], None, 8, base)
    coarse_step(node_b, node_a, cc, lhs[2], None, 8, base)
    here = is_from(1)
    tile = CXT * lax.axis_index("gx")
    src = lax.broadcasted_iota(jnp.int32, (2 * LANES, LANES), 0)
    dst = lane((2 * LANES, LANES))
    target = 32 + dst // 2 + jnp.where(dst % 2 == 1, LANES, 0)
    pick = jnp.where(src == target, 1.0, 0.0).astype(BF16)
    for r in range(CXT):
        wide = twice(c_in[tile + r] + here * node_a[tile - base + r + 1])
        for q in range(2):
            value = v_tile[2 * r + q] + wide
            out[0, :, 2 * r + q, :] = sum(
                jnp.dot(part, pick, preferred_element_type=F32) for part in split3(value)
            )


VMEM = pl.BlockSpec(memory_space=pltpu.VMEM)
SMEM = pl.BlockSpec(memory_space=pltpu.SMEM)
ANY = pl.BlockSpec(memory_space=pl.ANY)


def shape(*dims, dtype=F32):
    return jax.ShapeDtypeStruct(dims, dtype)


def call(kernel, name, outs, scratch, *operands, where={}, out_any=(), sems=0, limit=40):
    spaces = [where.get(index, VMEM) for index in range(len(operands))]
    single = not isinstance(outs, list)
    out_specs = [ANY if index in out_any else VMEM for index in range(1 if single else len(outs))]
    semaphores = [pltpu.SemaphoreType.DMA((sems,))] if sems else []
    return pl.pallas_call(
        kernel,
        name=name,
        out_shape=outs,
        in_specs=spaces,
        out_specs=out_specs[0] if single else out_specs,
        scratch_shapes=[pltpu.VMEM(dims, F32) for dims in scratch] + semaphores,
        compiler_params=pltpu.CompilerParams(vmem_limit_bytes=limit * MIB),
        cost_estimate=pl.CostEstimate(flops=10**8, bytes_accessed=10**6, transcendentals=0),
    )(*operands)


COARSE = (GX, DEPTH, LANES)
COARSE_PAD = (GX + 2, DEPTH, LANES)
FINE = (FX, DEPTH, 2 * LANES)
FINE_PAD = (FX + 2, DEPTH, 2 * LANES)


def shift(value, steps, sideways=0, around=False):
    slices, columns = lax.axis_size("tm"), lax.axis_size("gy")
    pairs = [
        (s * columns + g, ((s + steps) % slices) * columns + g + sideways)
        for s in range(slices if around else slices - steps)
        for g in range(columns)
        if 0 <= g + sideways < columns
    ]
    return lax.ppermute(value, ("tm", "gy"), pairs)


def swap(value, bit):
    return lax.ppermute(value, "gx", [(g, g ^ bit) for g in range(lax.axis_size("gx"))])


def quads(value):
    far = swap(value, 2)
    return [value, swap(value, 1), far, swap(far, 1)]


def halves(parts):
    return list(parts) + [swap(part, 1) for part in parts]


def fetch_strips(hops, steps):
    main, to_right, to_left = hops
    return [shift(main, steps), shift(to_right, steps, 1), shift(to_left, steps, -1)]


def on_device(initial_temp, conductivity, vert_cond, borehole_cells, borehole_profiles, heat_table):
    table1, table2 = shift(heat_table, 1, 0, True), shift(heat_table, 2, 0, True)
    main, to_right, to_left = call(
        prep_kernel,
        "prep",
        [
            shape(TX, 2 * DEPTH + 8, LANES),
            shape(TX // 2, 2 * DEPTH + 8, LANES),
            shape(TX // 2, 2 * DEPTH + 8, LANES),
        ],
        [(TX, 8, LANES)],
        borehole_cells.reshape(-1),
        borehole_profiles.reshape(-1),
        initial_temp,
        conductivity,
        where={0: SMEM, 1: SMEM},
    )
    strip = jnp.concatenate([shift(to_right, 0, 1), shift(to_left, 0, -1)], axis=0)
    upper = jnp.broadcast_to(vert_cond[:, None], (DEPTH, LANES))
    lower = jnp.concatenate([vert_cond[1:], jnp.zeros((1,), F32)])
    lower = jnp.broadcast_to(lower[:, None], (DEPTH, LANES))
    lhs = call(props_kernel, "props", shape(4, DEPTH, 2 * LANES, dtype=BF16), [], upper, lower)

    c, hop, k0, v, kc, cc, cond, plane_c = call(
        first_kernel,
        "first_sweeps",
        [
            shape(*COARSE),
            shape(CXT, DEPTH, LANES),
            shape(4, *FINE),
            shape(*FINE),
            shape(2, *COARSE),
            shape(*COARSE),
            shape(*FINE),
            shape(GX, 8, LANES),
        ],
        [FINE_PAD] * 5
        + [
            FINE,
            (4, *FINE),
            (3, FX, 8, 2 * LANES),
            (3, GX, 8, LANES),
            (5, *FINE),
            (5, *COARSE_PAD),
            (5, *COARSE),
            (6, *COARSE),
            (2, *COARSE),
            COARSE_PAD,
            COARSE_PAD,
        ],
        *quads(main),
        *quads(strip),
        heat_table,
        table1,
        table2,
        lhs,
        out_any=(2, 6),
        sems=2,
        limit=60,
    )

    def phase(steps, name, kind_in, kind_out, got, c):
        kernel = functools.partial(phase_kernel, steps, kind_in, kind_out)
        outs = [shape(*COARSE)] + outs_of(kind_out)
        c, *hops = call(kernel, name, outs, [COARSE_PAD, COARSE_PAD], *got, c, cc, lhs)
        return c, hops

    got = quads(shift(hop, 2, 0, True))
    c, hops = phase(2, "chain_a2", "quads", "quads", got, c)
    got = quads(shift(hops[0], 4))
    c, hops = phase(4, "chain_a4", "quads", "halves packed", got, c)
    got = halves(fetch_strips(hops, 8))
    c, *hops, v_tile = call(
        functools.partial(second_kernel, 8),
        "second_sweep",
        [shape(*COARSE)] + outs_of("halves packed") + [shape(TX, DEPTH, 2 * LANES)],
        [
            (4, *FINE),
            FINE,
            FINE,
            FINE_PAD,
            FINE_PAD,
            FINE_PAD,
            (4, *COARSE),
            (5, *COARSE_PAD),
            (5, *COARSE),
            (4, *COARSE),
            (2, *COARSE),
            COARSE_PAD,
            COARSE_PAD,
            COARSE_PAD,
        ],
        *got,
        c,
        cc,
        lhs,
        k0,
        v,
        kc,
        cond,
        plane_c,
        where={9: ANY, 10: ANY, 12: ANY},
        sems=3,
        limit=60,
    )
    got = halves(fetch_strips(hops, 8))
    c, hops = phase(8, "chain_b8", "halves packed", "quads packed", got, c)
    got = quads(jnp.concatenate(fetch_strips(hops, 4), axis=0))
    c, hops = phase(4, "chain_b4", "quads packed", "quads", got, c)
    got = quads(shift(hops[0], 2, 0, True))
    c, hops = phase(2, "chain_b2", "quads", "window", got, c)
    got = shift(hops[0], 1, 0, True)
    return call(
        last_kernel,
        "finish",
        shape(1, DEPTH, TX, LANES),
        [(10, DEPTH, LANES)] * 2,
        got,
        c,
        cc,
        lhs,
        v_tile,
    )


def solution(mesh):
    placed = (
        P(None, "gx", "gy"),
        P(None, "gx", "gy"),
        P(),
        P("gx", "gy", None),
        P("gx", "gy", None),
        P(None, "tm"),
    )
    return jax.shard_map(
        on_device, mesh=mesh, in_specs=placed, out_specs=P("tm", None, "gx", "gy"), check_vma=False
    )
```

```python
import functools
import math

import jax
import jax.numpy as jnp
from jax import lax
from jax.experimental import pallas as pl
from jax.experimental.pallas import tpu as pltpu
from jax.sharding import PartitionSpec as P

F32 = jnp.float32
BF16 = jnp.bfloat16
LATERAL = 0.3
VERTICAL = 4.0
FINE_NODES = [0.0, (1.0 - math.sqrt(3.0 / 7.0)) / 2.0, 0.5, (1.0 + math.sqrt(3.0 / 7.0)) / 2.0, 1.0]
COARSE_NODES = [0.0, 0.5, 1.0]
HALF = 0.5
DEPTH = 64
TX = 8
CXT = 4
FX = 32
GX = 16
LANES = 128
MIB = 2**20


def basis_coeffs(times_list, basis_index):
    coeffs = [1.0]
    denominator = 1.0
    for other_index in range(len(times_list)):
        if other_index != basis_index:
            other_time = times_list[other_index]
            widened = [0.0] * (len(coeffs) + 1)
            for power in range(len(coeffs)):
                widened[power + 1] = widened[power + 1] + coeffs[power]
                widened[power] = widened[power] - other_time * coeffs[power]
            coeffs = widened
            denominator = denominator * (times_list[basis_index] - other_time)
    return [entry / denominator for entry in coeffs]


def poly_value(coeffs, point):
    return sum(coeffs[power] * point**power for power in range(len(coeffs)))


def poly_integral(coeffs, lower, upper):
    return sum(
        coeffs[power] * (upper ** (power + 1) - lower ** (power + 1)) / (power + 1)
        for power in range(len(coeffs))
    )


H = [FINE_NODES[m + 1] - FINE_NODES[m] for m in range(4)]
S = [
    [poly_integral(basis_coeffs(FINE_NODES, j), FINE_NODES[m], FINE_NODES[m + 1]) for j in range(5)]
    for m in range(4)
]
W = [[poly_value(basis_coeffs(COARSE_NODES, c), t) for c in range(3)] for t in FINE_NODES]
SC = [[S[2 * m][j] + S[2 * m + 1][j] for j in range(5)] for m in range(2)]
SW = [[sum(S[m][j] * W[j][c] for j in range(5)) for c in range(3)] for m in range(4)]
ALPHA = [[SW[m][c] - H[m] * W[m][c] for c in range(3)] for m in range(4)]
BETA = [[SW[m][c] - H[m] * W[m + 1][c] for c in range(3)] for m in range(4)]


def loop(count, body, unroll=1):
    def step(index, carry):
        body(index)
        return carry

    lax.fori_loop(0, count, step, 0, unroll=unroll)


def roll(value, shift):
    return pltpu.roll(value, shift % value.shape[-1], value.ndim - 1)


def lane(shape):
    return lax.broadcasted_iota(jnp.int32, shape, len(shape) - 1)


def apply4(lhs, value):
    high = value.astype(BF16)
    low = (value - high.astype(F32)).astype(BF16)
    stacked = jnp.concatenate([high, low, high, low], axis=0)
    return jnp.dot(lhs, stacked, preferred_element_type=F32)


def split3(value):
    high = value.astype(BF16)
    rest = value - high.astype(F32)
    mid = rest.astype(BF16)
    low = (rest - mid.astype(F32)).astype(BF16)
    return high, mid, low


def fine_lap(src, row):
    u = src[row + 1]
    even, odd = u[:, :LANES], u[:, LANES:]
    beside = jnp.concatenate([odd + roll(odd, 1), even + roll(even, -1)], axis=1)
    return u, (src[row] + src[row + 2]) + beside - 4.0 * u


def coarse_lap(src, row):
    u = src[row + 1]
    return u, (src[row] + src[row + 2]) + (roll(u, 1) + roll(u, -1)) - 4.0 * u


def pool(first, second):
    total = first + second
    return 0.25 * (total[:, :LANES] + total[:, LANES:])


def twice(value):
    return jnp.concatenate([value, value], axis=1)


def rows8(value):
    return jnp.concatenate([value] * (DEPTH // 8), axis=0)


def zero_edges(ref):
    edge = jnp.zeros(ref.shape[1:], F32)
    ref[0] = edge
    ref[ref.shape[0] - 1] = edge


def coarse_step(src, dst, cc, prop, known=None, count=GX, base=0):
    for pair in range(count // 2):
        parts = []
        for row in (2 * pair, 2 * pair + 1):
            u, lap = coarse_lap(src, row)
            rhs = u + cc[base + row] * lap
            parts.append(rhs if known is None else rhs + known[row])
        node = apply4(prop, jnp.concatenate(parts, axis=1))
        dst[2 * pair + 1] = node[:, :LANES]
        dst[2 * pair + 2] = node[:, LANES:]


def chain_power(first, second, cc, prop, steps, count=GX, base=0):
    each = min(steps, 4)

    def body(_):
        for _ in range(each):
            coarse_step(first, second, cc, prop, None, count, base)
            coarse_step(second, first, cc, prop, None, count, base)

    if steps == each:
        body(0)
    else:
        loop(steps // each, body)


def sweep(bufs, cond, lhs, known, pu, pe, pr=None, es=None):
    for m in range(4):
        src, dst = bufs[m], bufs[m + 1]
        prop = lhs[0] if m in (0, 3) else lhs[1]

        def body(pair, m=m, src=src, dst=dst, prop=prop):
            us, ex, rs = [], [], []
            for row in (2 * pair, 2 * pair + 1):
                u, lap = fine_lap(src, row)
                e = cond[row] * lap
                rhs = u + H[m] * e + known(m, row)
                dst[row + 1] = apply4(prop, rhs)
                if es is not None:
                    es[m, row] = e
                us.append(u)
                ex.append(e)
                rs.append(rhs)
            pu[m, pair + 1] = pool(*us)
            pe[m, pair] = pool(*ex)
            if pr is not None:
                pr[m, pair] = pool(*rs)

        loop(GX, body, unroll=8)

    def last(pair):
        us, ex = [], []
        for row in (2 * pair, 2 * pair + 1):
            u, lap = fine_lap(bufs[4], row)
            e = cond[row] * lap
            if es is not None:
                es[4, row] = e
            us.append(u)
            ex.append(e)
        pu[4, pair + 1] = pool(*us)
        pe[4, pair] = pool(*ex)

    loop(GX, last, unroll=8)


def coarse_known(pu, pe, pr, cc, plane, lhs, kc, olds=None):
    matrix = lhs[3]

    def body(pair):
        rows = (2 * pair, 2 * pair + 1)
        ic, ec = [], []
        for c in range(3):
            laps = [coarse_lap(pu.at[2 * c], row) for row in rows]
            ec.append([cc[row] * lap for row, (_, lap) in zip(rows, laps)])
            both = apply4(matrix, jnp.concatenate([u for u, _ in laps], axis=1))
            ic.append([both[:, :LANES], both[:, LANES:]])
        for place, row in enumerate(rows):
            flat = rows8(plane[row])
            u = [pu[j, row + 1] for j in range(5)]
            e = [pe[j, row] for j in range(5)]
            total = [e[0] + ic[0][place]]
            for m in range(4):
                if pr is None:
                    im = (u[m + 1] - u[m]) * (1.0 / H[m]) - (e[m] + flat)
                else:
                    im = (u[m + 1] - pr[m, row]) * (1.0 / H[m])
                total.append(e[m + 1] + im)
            for k in range(2):
                value = HALF * (flat - ic[k + 1][place]) - ec[k][place]
                for j in range(5):
                    value = value + SC[k][j] * total[j]
                kc[k, row] = value
            if olds is not None:
                for c in range(3):
                    olds[c, row] = 2.0 * ec[c][place]
                    olds[3 + c, row] = ic[c][place]

    loop(GX // 2, body, unroll=4)


def finish_known(bufs, es, olds, plane, matrix, k0):
    def body(pair):
        wide = []
        for m in range(4):
            total = ALPHA[m][0] * olds[0, pair] + BETA[m][0] * olds[3, pair]
            for c in (1, 2):
                total = total + ALPHA[m][c] * olds[c, pair] + BETA[m][c] * olds[3 + c, pair]
            wide.append(twice(total))
        for row in (2 * pair, 2 * pair + 1):
            flat = rows8(plane[row])
            u = [buf[row + 1] for buf in bufs]
            e = [es[j, row] for j in range(5)]
            total = [e[0] + apply4(matrix, u[0])]
            change = [u[m + 1] - u[m] for m in range(4)]
            for m in range(4):
                total.append(e[m + 1] + (change[m] * (1.0 / H[m]) - (e[m] + flat)))
            for m in range(4):
                value = (2.0 * H[m]) * flat - (change[m] + wide[m])
                for j in range(5):
                    value = value + S[m][j] * total[j]
                k0[m, row] = value

    loop(GX, body, unroll=4)


def pack(c_ref, base, count, main, to_right, to_left):
    at = lane((DEPTH, LANES))
    for quad in range(count // 4):
        rows = [c_ref[base + 4 * quad + r] for r in range(4)]
        for half in range(2):
            main[2 * quad + half] = jnp.where(
                at < 64, roll(rows[2 * half], -32), roll(rows[2 * half + 1], 32)
            )
        for out, start in ((to_right, 64), (to_left, 32)):
            value = roll(rows[0], -start)
            for r in range(1, 4):
                value = jnp.where(at < 32 * r, value, roll(rows[r], 32 * r - start))
            out[quad] = value


def sides():
    gy = lax.axis_index("gy")
    last = lax.axis_size("gy") - 1
    return jnp.where(gy > 0, 1.0, 0.0).astype(F32), jnp.where(gy < last, 1.0, 0.0).astype(F32)


def unpack(main, left, right, count, dst, base):
    at = lane((DEPTH, LANES))
    has_left, has_right = sides()
    for quad in range(count // 4):
        for r in range(4):
            centre = roll(main[2 * quad + r // 2], 32 if r % 2 == 0 else -32)
            before = has_left * roll(left[quad], -32 * r)
            after = has_right * roll(right[quad], 96 - 32 * r)
            value = jnp.where(at < 32, before, jnp.where(at < 96, centre, after))
            dst[base + 4 * quad + r + 1] = value


def put(rows, count, dst, base):
    for r in range(count):
        dst[base + r + 1] = rows[r]


def receive(kind, got, dst):
    gx = lax.axis_index("gx")
    if kind == "quads":
        for k, rows in zip((0, 1, 2, 3), got):
            put(rows, CXT, dst, CXT * lax.bitwise_xor(gx, k))
    elif kind == "quads packed":
        for k, slabs in zip((0, 1, 2, 3), got):
            base = CXT * lax.bitwise_xor(gx, k)
            unpack(slabs, slabs.at[pl.ds(2, 1)], slabs.at[pl.ds(3, 1)], CXT, dst, base)
    else:
        core = lax.bitwise_and(gx, 1)
        for k in range(2):
            unpack(*got[3 * k : 3 * k + 3], 8, dst, 8 * lax.bitwise_xor(core, k))


def window_base():
    return jnp.clip(CXT * lax.axis_index("gx") - 2, 0, 8)


def send(kind, c_ref, outs):
    gx = lax.axis_index("gx")
    if kind == "quads":
        for r in range(CXT):
            outs[0][r] = c_ref[CXT * gx + r]
    elif kind == "quads packed":
        pack(c_ref, CXT * gx, CXT, *outs)
    elif kind == "halves packed":
        pack(c_ref, 8 * lax.bitwise_and(gx, 1), 8, *outs)
    else:
        base = window_base()
        for r in range(8):
            outs[0][r] = c_ref[base + r]


def outs_of(kind):
    if kind == "quads":
        return [shape(CXT, DEPTH, LANES)]
    if kind == "window":
        return [shape(8, DEPTH, LANES)]
    count = 1 if kind == "quads packed" else 2
    return [shape(2 * count, DEPTH, LANES)] + [shape(count, DEPTH, LANES)] * 2


def takes(kind):
    return {"quads": 4, "quads packed": 4, "halves packed": 6, "window": 1}[kind]


def is_from(steps):
    return jnp.where(lax.axis_index("tm") >= steps, 1.0, 0.0).astype(F32)


def props_kernel(faces_ref, out_ref):
    shape = (DEPTH, DEPTH)
    faces = jnp.broadcast_to(faces_ref[...], shape)
    row = lax.broadcasted_iota(jnp.int32, shape, 0)
    col = lane(shape)
    shape = (DEPTH, LANES)
    upper = jnp.sum(jnp.where(row == col, faces, 0.0), axis=1, keepdims=True)
    lower = jnp.sum(jnp.where(row + 1 == col, faces, 0.0), axis=1, keepdims=True)
    upper, lower = jnp.broadcast_to(upper, shape), jnp.broadcast_to(lower, shape)
    row = lax.broadcasted_iota(jnp.int32, shape, 0)
    col = lane(shape)
    level = jnp.where(col < DEPTH, col, col - DEPTH)
    eye = jnp.where(row == level, 1.0, 0.0).astype(F32)

    def shifted(value, step):
        return pltpu.roll(value, step % DEPTH, 0)

    def inverse(length):
        a = -VERTICAL * length * jnp.where(row == 0, 0.0, upper)
        c = -VERTICAL * length * lower
        b = 1.0 + VERTICAL * length * (upper + lower)
        r = eye
        step = 1
        while step < DEPTH:
            alpha = -a / shifted(b, step)
            gamma = -c / shifted(b, -step)
            b, r, a, c = (
                b + alpha * shifted(c, step) + gamma * shifted(a, -step),
                r + alpha * shifted(r, step) + gamma * shifted(r, -step),
                alpha * shifted(a, step),
                gamma * shifted(c, -step),
            )
            step *= 2
        return r / b

    def store(index, value):
        high = value.astype(BF16)
        out_ref[index, :, :LANES] = high
        out_ref[index, :, LANES:] = (value - high.astype(F32)).astype(BF16)

    fine = inverse(jnp.where(col < DEPTH, H[0], H[1]).astype(F32))
    other = roll(fine, DEPTH)
    store(0, jnp.where(col < DEPTH, fine, other))
    store(1, jnp.where(col < DEPTH, other, fine))
    store(2, inverse(jnp.full(shape, HALF, F32)))
    matrix = jnp.where(row == level, -VERTICAL * (upper + lower), 0.0)
    matrix = matrix + jnp.where(level == row - 1, VERTICAL * upper, 0.0)
    matrix = matrix + jnp.where(level == row + 1, VERTICAL * lower, 0.0)
    store(3, matrix)


def prep_kernel(
    cells, profiles, temp_in, conduct_in, main, to_right, to_left, counts, temp, conduct, sems
):
    copies = [
        pltpu.make_async_copy(temp_in, temp, sems.at[0]),
        pltpu.make_async_copy(conduct_in, conduct, sems.at[1]),
    ]
    for copy in copies:
        copy.start()
    src = lax.broadcasted_iota(jnp.int32, (LANES, LANES), 0)
    dst = lane((LANES, LANES))
    odd = 2 * jnp.where(dst < 32, dst + 32, dst - 96) + 1
    target = jnp.where((dst >= 32) & (dst < 96), 2 * (dst - 32), odd)
    pick = jnp.where(src == target, 1.0, 0.0).astype(BF16)
    for copy in copies:
        copy.wait()
    for row in range(TX):
        for place, ref in enumerate((temp, conduct)):
            main[row, DEPTH * place : DEPTH * (place + 1)] = sum(
                jnp.dot(part, pick, preferred_element_type=F32) for part in split3(ref[:, row, :])
            )
    counts[...] = jnp.zeros_like(counts)
    at = lane((8, LANES))
    profile = lax.broadcasted_iota(jnp.int32, (8, LANES), 0)
    for b in range(16):
        cell, which = cells[b], profiles[b]
        row, y = cell // LANES, cell % LANES
        half = y // 2
        column = jnp.where(y % 2 == 0, half + 32, jnp.where(half < 32, half + 96, half - 32))
        hit = (at == column) & (profile == which)
        counts[row] = counts[row] + jnp.where(hit, 1.0, 0.0)
    for row in range(TX):
        main[row, 2 * DEPTH :] = counts[row]
    first = lane((2 * DEPTH + 8, LANES)) % 64 < 32
    for slab in range(TX // 2):
        low, high = roll(main[slab], 64), roll(main[slab + TX // 2], 32)
        to_right[slab] = jnp.where(first, low, high)
        to_left[slab] = jnp.where(first, high, low)


def first_kernel(
    main0,
    main1,
    main2,
    main3,
    strip0,
    strip1,
    strip2,
    strip3,
    table0,
    table1,
    lhs,
    c_out,
    k0_out,
    v_out,
    kc_out,
    cc,
    cond_out,
    plane_c,
    init,
    node_1,
    node_2,
    node_3,
    node_4,
    cond,
    k0,
    planes,
    planes_c,
    es,
    pu,
    pe,
    olds,
    kc,
    node_a,
    node_b,
    sems,
):
    bufs = (init, node_1, node_2, node_3, node_4)
    for ref in bufs + (node_a, node_b):
        zero_edges(ref)
    for j in range(5):
        zero_edges(pu.at[j])
    gx = lax.axis_index("gx")
    at = lane((2 * DEPTH + 8, LANES))
    core = lax.bitwise_and(gx, 1)
    rates = [jnp.broadcast_to(t[...], (8, 2 * LANES)) for t in (table0, table1)]
    inside = (at >= 32) & (at < 96)
    first = at % 64 < 32
    has_left, has_right = sides()
    for k, (main, strip) in enumerate(
        ((main0, strip0), (main1, strip1), (main2, strip2), (main3, strip3))
    ):
        base = TX * lax.bitwise_xor(gx, k)

        def assemble(q, main=main, strip=strip, base=base):
            left, right = has_left * strip[q], has_right * strip[4 + q]
            for row, edge in (
                (q, jnp.where(first, left, right)),
                (q + 4, roll(jnp.where(first, right, left), 32)),
            ):
                centre = main[row]
                even = jnp.where(inside, centre, edge)
                odd = roll(jnp.where(inside, edge, centre), 64)
                window = jnp.concatenate([even, odd], axis=1)
                init[base + row + 1] = window[:DEPTH]
                cond[base + row] = LATERAL * window[DEPTH : 2 * DEPTH]
                counts = window[2 * DEPTH :]
                for t in range(2):
                    heat = jnp.sum(counts * rates[t], axis=0, keepdims=True)
                    planes[t, base + row] = jnp.broadcast_to(heat, (8, 2 * LANES))

        loop(TX // 2, assemble, unroll=2)
    copy_cond = pltpu.make_async_copy(cond, cond_out, sems.at[0])
    copy_cond.start()

    def coarsen(row):
        cc[row] = (0.25 * HALF) * pool(cond[2 * row], cond[2 * row + 1])
        for t in range(2):
            planes_c[t, row] = pool(planes[t, 2 * row], planes[t, 2 * row + 1])
        plane_c[row] = planes_c[0, row]

    loop(GX, coarsen, unroll=4)
    prop = lhs[2]
    copy_k0 = pltpu.make_async_copy(k0, k0_out, sems.at[1])

    def one_slice(t):
        sweep(bufs, cond, lhs, lambda m, row: rows8(H[m] * planes[t, row]), pu, pe, None, es)
        coarse_known(pu, pe, None, cc, planes_c.at[t], lhs, kc, olds)

        @pl.when(t == 0)
        def _():
            finish_known(bufs, es, olds, planes.at[0], lhs[3], k0)
            copy_k0.start()
            for k in range(2):
                for row in range(GX):
                    kc_out[k, row] = kc[k, row]

        @pl.when(t > 0)
        def _():
            for pair in range(GX // 2):
                both = apply4(
                    prop, jnp.concatenate([kc[0, 2 * pair], kc[0, 2 * pair + 1]], axis=1)
                )
                node_b[2 * pair + 1] = both[:, :LANES]
                node_b[2 * pair + 2] = both[:, LANES:]
            coarse_step(node_b, node_a, cc, prop, kc.at[1])

    loop(2, one_slice)
    after1, after2 = is_from(1), is_from(2)
    is0, is1 = 1.0 - after1, after1 - after2
    second = jnp.where(core == 1, 1.0, 0.0).astype(F32)
    swept = after1 + second * (after2 - after1)
    begun = is0 + second * (is1 - is0)

    def choose(row):
        node_a[row + 1] = swept * node_a[row + 1] + begun * pu[0, row + 1]
        for fine in (2 * row, 2 * row + 1):
            before = node_4[fine + 1] - twice(pu[4, row + 1])
            here = init[fine + 1] - twice(pu[0, row + 1])
            v_out[fine] = after1 * before + is0 * here

    loop(GX, choose, unroll=4)

    @pl.when(core == 1)
    def _():
        chain_power(node_a, node_b, cc, prop, 1)

    def keep(row):
        c_out[row] = node_a[row + 1]

    loop(GX, keep, unroll=8)
    copy_cond.wait()
    copy_k0.wait()


def phase_kernel(steps, parts, kind_in, kind_out, *refs):
    count = takes(kind_in)
    got, refs = refs[:count], refs[count:]
    c_in, (cc_in, lhs, c_out), refs = refs[:parts], refs[parts : parts + 3], refs[parts + 3 :]
    outs, (node_a, node_b, cc, c_old, sems) = refs[:-5], refs[-5:]
    copy_cc = pltpu.make_async_copy(cc_in, cc, sems.at[0])
    copy_cc.start()
    copies = [
        pltpu.make_async_copy(c_in[k], c_old.at[k], sems.at[1 + k]) for k in range(parts)
    ]
    for copy in copies:
        copy.start()
    zero_edges(node_a)
    zero_edges(node_b)
    receive(kind_in, got, node_a)
    copy_cc.wait()
    chain_power(node_a, node_b, cc, lhs[2], steps)
    here = is_from(steps)
    for copy in copies:
        copy.wait()

    def add(row):
        value = c_old[0, row] + here * node_a[row + 1]
        for k in range(1, parts):
            value = value + c_old[k, row]
        c_out[row] = value

    loop(GX, add, unroll=8)
    send(kind_out, c_out, outs)


def second_kernel(
    steps,
    main_a,
    left_a,
    right_a,
    main_b,
    left_b,
    right_b,
    c_in,
    cc,
    lhs,
    k0_in,
    v_first,
    v_second,
    kc_in,
    cond_in,
    plane_c,
    c_out,
    hop,
    to_right,
    to_left,
    v_tile,
    k0,
    v,
    cond,
    start,
    buf_a,
    buf_b,
    dk,
    pu,
    pe,
    pr,
    kc,
    node_a,
    node_b,
    node_c,
    sems,
):
    copies = [
        pltpu.make_async_copy(src, dst, sems.at[place])
        for place, (src, dst) in enumerate(((v_first, v), (cond_in, cond), (k0_in, k0)))
    ]
    core = lax.bitwise_and(lax.axis_index("gx"), 1)

    @pl.when(core == 0)
    def _():
        copies[0].start()

    @pl.when(core == 1)
    def _():
        pltpu.make_async_copy(v_second, v, sems.at[0]).start()

    for copy in copies[1:]:
        copy.start()
    for ref in (start, buf_a, buf_b, node_a, node_b, node_c):
        zero_edges(ref)
    for j in range(5):
        zero_edges(pu.at[j])
    receive("halves packed", (main_a, left_a, right_a, main_b, left_b, right_b), node_a)
    prop, matrix = lhs[2], lhs[3]
    chain_power(node_a, node_b, cc, prop, steps)
    here = is_from(steps)
    copies[0].wait()

    def add(row):
        value = c_in[row] + here * node_a[row + 1]
        node_a[row + 1] = value
        wide = twice(value)
        start[2 * row + 1] = v[2 * row] + wide
        start[2 * row + 2] = v[2 * row + 1] + wide

    loop(GX, add, unroll=4)

    def spread(row, c, explicit, implicit):
        for m in range(4):
            total = (2.0 * ALPHA[m][c]) * explicit + BETA[m][c] * implicit
            dk[m, row] = total if c == 0 else dk[m, row] + total

    def stage(c, src, dst):
        def body(pair):
            rows = (2 * pair, 2 * pair + 1)
            laps = [coarse_lap(src, row) for row in rows]
            ex = [cc[row] * lap for row, (_, lap) in zip(rows, laps)]
            if c == 0:
                both = apply4(matrix, jnp.concatenate([u for u, _ in laps], axis=1))
                implicit = (both[:, :LANES], both[:, LANES:])
            else:
                implicit = (kc[c - 1, rows[0]], kc[c - 1, rows[1]])
            for place in range(2):
                spread(rows[place], c, ex[place], implicit[place])
            if c < 2:
                rhs = jnp.concatenate(
                    [u + e + kc_in[c, row] for row, (u, _), e in zip(rows, laps, ex)], axis=1
                )
                node = apply4(prop, rhs)
                dst[rows[0] + 1] = node[:, :LANES]
                dst[rows[1] + 1] = node[:, LANES:]
                after = (node - rhs) * (1.0 / HALF)
                kc[c, rows[0]] = after[:, :LANES]
                kc[c, rows[1]] = after[:, LANES:]

        loop(GX // 2, body, unroll=4)

    stage(0, node_a, node_b)
    stage(1, node_b, node_c)
    stage(2, node_c, None)
    copies[1].wait()
    copies[2].wait()

    def known(m, row):
        return k0[m, row] + twice(dk[m, row // 2])

    sweep((start, buf_a, buf_b, buf_a, buf_b), cond, lhs, known, pu, pe, pr)
    coarse_known(pu, pe, pr, cc, plane_c, lhs, kc)
    is0 = 1.0 - is_from(1)

    def begin(row):
        node_a[row + 1] = is0 * pu[0, row + 1]

    loop(GX, begin, unroll=4)
    coarse_step(node_a, node_b, cc, prop, kc.at[0])
    coarse_step(node_b, node_a, cc, prop, kc.at[1])

    def keep(row):
        c_out[row] = node_a[row + 1]

    loop(GX, keep, unroll=4)
    send("halves packed", c_out, (hop, to_right, to_left))
    base = CXT * lax.axis_index("gx")
    for r in range(CXT):
        for q in range(2):
            fine = 2 * r + q
            v_tile[fine] = buf_b[2 * base + fine + 1] - twice(pu[4, base + r + 1])


def last_kernel(got, c_in, cc, lhs, v_tile, out, node_a, node_b):
    zero_edges(node_a)
    zero_edges(node_b)
    put(got, 8, node_a, 0)
    base = window_base()
    coarse_step(node_a, node_b, cc, lhs[2], None, 8, base)
    coarse_step(node_b, node_a, cc, lhs[2], None, 8, base)
    here = is_from(1)
    tile = CXT * lax.axis_index("gx")
    src = lax.broadcasted_iota(jnp.int32, (2 * LANES, LANES), 0)
    dst = lane((2 * LANES, LANES))
    target = 32 + dst // 2 + jnp.where(dst % 2 == 1, LANES, 0)
    pick = jnp.where(src == target, 1.0, 0.0).astype(BF16)
    for r in range(CXT):
        wide = twice(c_in[tile + r] + here * node_a[tile - base + r + 1])
        for q in range(2):
            value = v_tile[2 * r + q] + wide
            out[0, :, 2 * r + q, :] = sum(
                jnp.dot(part, pick, preferred_element_type=F32) for part in split3(value)
            )


VMEM = pl.BlockSpec(memory_space=pltpu.VMEM)
SMEM = pl.BlockSpec(memory_space=pltpu.SMEM)
ANY = pl.BlockSpec(memory_space=pl.ANY)
HBM = pl.BlockSpec(memory_space=pltpu.HBM)


def shape(*dims, dtype=F32):
    return jax.ShapeDtypeStruct(dims, dtype)


def call(kernel, name, outs, scratch, *operands, where={}, out_any=(), sems=0, limit=16):
    spaces = [where.get(index, VMEM) for index in range(len(operands))]
    single = not isinstance(outs, list)
    out_specs = [ANY if index in out_any else VMEM for index in range(1 if single else len(outs))]
    semaphores = [pltpu.SemaphoreType.DMA((sems,))] if sems else []
    return pl.pallas_call(
        kernel,
        name=name,
        out_shape=outs,
        in_specs=spaces,
        out_specs=out_specs[0] if single else out_specs,
        scratch_shapes=[pltpu.VMEM(dims, F32) for dims in scratch] + semaphores,
        compiler_params=pltpu.CompilerParams(vmem_limit_bytes=limit * MIB),
        cost_estimate=pl.CostEstimate(flops=10**8, bytes_accessed=10**6, transcendentals=0),
    )(*operands)


COARSE = (GX, DEPTH, LANES)
COARSE_PAD = (GX + 2, DEPTH, LANES)
FINE = (FX, DEPTH, 2 * LANES)
FINE_PAD = (FX + 2, DEPTH, 2 * LANES)


def shift(value, steps, sideways=0):
    slices, columns = lax.axis_size("tm"), lax.axis_size("gy")
    pairs = [
        (s * columns + g, (s + steps) % slices * columns + (g + sideways) % columns)
        for s in range(slices)
        for g in range(columns)
    ]
    return lax.ppermute(value, ("tm", "gy"), pairs)


def swap(value, bit):
    return lax.ppermute(value, "gx", [(g, g ^ bit) for g in range(lax.axis_size("gx"))])


def quads(value):
    far = swap(value, 2)
    return [value, swap(value, 1), far, swap(far, 1)]


def halves(parts):
    return list(parts) + [swap(part, 1) for part in parts]


def fetch_strips(hops, steps):
    main, to_right, to_left = hops
    return [shift(main, steps), shift(to_right, steps, 1), shift(to_left, steps, -1)]


def on_device(initial_temp, conductivity, vert_cond, borehole_cells, borehole_profiles, heat_table):
    slices, rows = lax.axis_size("tm"), lax.axis_size("gx")
    pairs = [
        (t * rows + g, (t + 1 + g % 2) % slices * rows + g)
        for t in range(slices)
        for g in range(rows)
    ]
    table1 = lax.ppermute(heat_table, ("tm", "gx"), pairs)
    main, to_right, to_left = call(
        prep_kernel,
        "prep",
        [
            shape(TX, 2 * DEPTH + 8, LANES),
            shape(TX // 2, 2 * DEPTH + 8, LANES),
            shape(TX // 2, 2 * DEPTH + 8, LANES),
        ],
        [(TX, 8, LANES), (DEPTH, TX, LANES), (DEPTH, TX, LANES)],
        borehole_cells.reshape(-1),
        borehole_profiles.reshape(-1),
        initial_temp,
        conductivity,
        where={0: SMEM, 1: SMEM, 2: HBM, 3: HBM},
        sems=2,
    )
    mains = quads(main)
    lhs = call(
        props_kernel,
        "props",
        shape(4, DEPTH, 2 * LANES, dtype=BF16),
        [],
        vert_cond.reshape(1, DEPTH),
    )
    near = (shift(to_right, 0, 1), shift(to_left, 0, -1), table1, lhs)
    from_left, from_right, table1, lhs = lax.optimization_barrier(near)
    strip = jnp.concatenate([from_left, from_right], axis=0)

    c, k0, v, kc, cc, cond, plane_c = call(
        first_kernel,
        "first_sweeps",
        [
            shape(*COARSE),
            shape(4, *FINE),
            shape(*FINE),
            shape(2, *COARSE),
            shape(*COARSE),
            shape(*FINE),
            shape(GX, 8, LANES),
        ],
        [FINE_PAD] * 5
        + [
            FINE,
            (4, *FINE),
            (2, FX, 8, 2 * LANES),
            (2, GX, 8, LANES),
            (5, *FINE),
            (5, *COARSE_PAD),
            (5, *COARSE),
            (6, *COARSE),
            (2, *COARSE),
            COARSE_PAD,
            COARSE_PAD,
        ],
        *mains,
        *quads(strip),
        heat_table,
        table1,
        lhs,
        out_any=(1, 5),
        sems=2,
        limit=60,
    )

    def phase(steps, name, kind_in, kind_out, got, c):
        kernel = functools.partial(phase_kernel, steps, len(c), kind_in, kind_out)
        outs = [shape(*COARSE)] + outs_of(kind_out)
        scratch = [COARSE_PAD, COARSE_PAD, COARSE, (len(c), *COARSE)]
        where = {len(got) + k: HBM for k in range(len(c))}
        where[len(got) + len(c)] = ANY
        c, *hops = call(
            kernel, name, outs, scratch, *got, *c, cc, lhs, where=where, sems=1 + len(c)
        )
        return [c], hops

    c = [c, swap(c, 1)]
    base = CXT * lax.axis_index("gx")
    hop = sum(lax.dynamic_slice_in_dim(part, base, CXT, axis=0) for part in c)
    v, hop = lax.optimization_barrier((v, hop))
    v_other = swap(v, 1)
    got = quads(shift(hop, 2))
    c, hops = phase(2, "chain_a2", "quads", "quads", got, c)
    got = quads(shift(hops[0], 4))
    c, hops = phase(4, "chain_a4", "quads", "halves packed", got, c)
    got = halves(fetch_strips(hops, 8))
    c, *hops, v_tile = call(
        functools.partial(second_kernel, 8),
        "second_sweep",
        [shape(*COARSE)] + outs_of("halves packed") + [shape(TX, DEPTH, 2 * LANES)],
        [
            (4, *FINE),
            FINE,
            FINE,
            FINE_PAD,
            FINE_PAD,
            FINE_PAD,
            (4, *COARSE),
            (5, *COARSE_PAD),
            (5, *COARSE),
            (4, *COARSE),
            (2, *COARSE),
            COARSE_PAD,
            COARSE_PAD,
            COARSE_PAD,
        ],
        *got,
        c[0],
        cc,
        lhs,
        k0,
        v,
        v_other,
        kc,
        cond,
        plane_c,
        where={9: ANY, 10: ANY, 11: ANY, 13: ANY},
        sems=3,
        limit=60,
    )
    got = halves(fetch_strips(hops, 8))
    c, hops = phase(8, "chain_b8", "halves packed", "quads packed", got, [c])
    got = quads(jnp.concatenate(fetch_strips(hops, 4), axis=0))
    c, hops = phase(4, "chain_b4", "quads packed", "quads", got, c)
    got = quads(shift(hops[0], 2))
    c, hops = phase(2, "chain_b2", "quads", "window", got, c)
    got = shift(hops[0], 1)
    return call(
        last_kernel,
        "finish",
        shape(1, DEPTH, TX, LANES),
        [(10, DEPTH, LANES)] * 2,
        got,
        c[0],
        cc,
        lhs,
        v_tile,
    )


def solution(mesh):
    placed = (
        P(None, "gx", "gy"),
        P(None, "gx", "gy"),
        P(),
        P("gx", "gy", None),
        P("gx", "gy", None),
        P(None, "tm"),
    )
    return jax.shard_map(
        on_device, mesh=mesh, in_specs=placed, out_specs=P("tm", None, "gx", "gy"), check_vma=False
    )
```

```python
import functools
import math

import jax
import jax.numpy as jnp
from jax import lax
from jax.experimental import pallas as pl
from jax.experimental.pallas import tpu as pltpu
from jax.sharding import PartitionSpec as P

F32 = jnp.float32
BF16 = jnp.bfloat16
LATERAL = 0.3
VERTICAL = 4.0
FINE_NODES = [0.0, (1.0 - math.sqrt(3.0 / 7.0)) / 2.0, 0.5, (1.0 + math.sqrt(3.0 / 7.0)) / 2.0, 1.0]
COARSE_NODES = [0.0, 0.5, 1.0]
HALF = 0.5
DEPTH = 64
TX = 8
CXT = 4
FX = 32
GX = 16
LANES = 128
MIB = 2**20


def basis_coeffs(times_list, basis_index):
    coeffs = [1.0]
    denominator = 1.0
    for other_index in range(len(times_list)):
        if other_index != basis_index:
            other_time = times_list[other_index]
            widened = [0.0] * (len(coeffs) + 1)
            for power in range(len(coeffs)):
                widened[power + 1] = widened[power + 1] + coeffs[power]
                widened[power] = widened[power] - other_time * coeffs[power]
            coeffs = widened
            denominator = denominator * (times_list[basis_index] - other_time)
    return [entry / denominator for entry in coeffs]


def poly_value(coeffs, point):
    return sum(coeffs[power] * point**power for power in range(len(coeffs)))


def poly_integral(coeffs, lower, upper):
    return sum(
        coeffs[power] * (upper ** (power + 1) - lower ** (power + 1)) / (power + 1)
        for power in range(len(coeffs))
    )


H = [FINE_NODES[m + 1] - FINE_NODES[m] for m in range(4)]
S = [
    [poly_integral(basis_coeffs(FINE_NODES, j), FINE_NODES[m], FINE_NODES[m + 1]) for j in range(5)]
    for m in range(4)
]
W = [[poly_value(basis_coeffs(COARSE_NODES, c), t) for c in range(3)] for t in FINE_NODES]
SC = [[S[2 * m][j] + S[2 * m + 1][j] for j in range(5)] for m in range(2)]
SW = [[sum(S[m][j] * W[j][c] for j in range(5)) for c in range(3)] for m in range(4)]
ALPHA = [[SW[m][c] - H[m] * W[m][c] for c in range(3)] for m in range(4)]
BETA = [[SW[m][c] - H[m] * W[m + 1][c] for c in range(3)] for m in range(4)]


def loop(count, body, unroll=1):
    def step(index, carry):
        body(index)
        return carry

    lax.fori_loop(0, count, step, 0, unroll=unroll)


def roll(value, shift):
    return pltpu.roll(value, shift % value.shape[-1], value.ndim - 1)


def lane(shape):
    return lax.broadcasted_iota(jnp.int32, shape, len(shape) - 1)


def apply4(lhs, value):
    high = value.astype(BF16)
    low = (value - high.astype(F32)).astype(BF16)
    stacked = jnp.concatenate([high, low, high, low], axis=0)
    return jnp.dot(lhs, stacked, preferred_element_type=F32)


def split3(value):
    high = value.astype(BF16)
    rest = value - high.astype(F32)
    mid = rest.astype(BF16)
    low = (rest - mid.astype(F32)).astype(BF16)
    return high, mid, low


def fine_lap(src, row):
    u = src[row + 1]
    even, odd = u[:, :LANES], u[:, LANES:]
    beside = jnp.concatenate([odd + roll(odd, 1), even + roll(even, -1)], axis=1)
    return u, (src[row] + src[row + 2]) + beside - 4.0 * u


def coarse_lap(src, row):
    u = src[row + 1]
    return u, (src[row] + src[row + 2]) + (roll(u, 1) + roll(u, -1)) - 4.0 * u


def pool(first, second):
    total = first + second
    return 0.25 * (total[:, :LANES] + total[:, LANES:])


def twice(value):
    return jnp.concatenate([value, value], axis=1)


def rows8(value):
    return jnp.concatenate([value] * (DEPTH // 8), axis=0)


def zero_edges(ref):
    edge = jnp.zeros(ref.shape[1:], F32)
    ref[0] = edge
    ref[ref.shape[0] - 1] = edge


def coarse_step(src, dst, cc, prop, known=None, count=GX, base=0):
    for pair in range(count // 2):
        parts = []
        for row in (2 * pair, 2 * pair + 1):
            u, lap = coarse_lap(src, row)
            rhs = u + cc[base + row] * lap
            parts.append(rhs if known is None else rhs + known[row])
        node = apply4(prop, jnp.concatenate(parts, axis=1))
        dst[2 * pair + 1] = node[:, :LANES]
        dst[2 * pair + 2] = node[:, LANES:]


def chain_power(first, second, cc, prop, steps, count=GX, base=0):
    each = min(steps, 4)

    def body(_):
        for _ in range(each):
            coarse_step(first, second, cc, prop, None, count, base)
            coarse_step(second, first, cc, prop, None, count, base)

    if steps == each:
        body(0)
    else:
        loop(steps // each, body)


def sweep(bufs, cond, lhs, known, pu, pe, pr=None, es=None):
    for m in range(4):
        src, dst = bufs[m], bufs[m + 1]
        prop = lhs[0] if m in (0, 3) else lhs[1]

        def body(pair, m=m, src=src, dst=dst, prop=prop):
            us, ex, rs = [], [], []
            for row in (2 * pair, 2 * pair + 1):
                u, lap = fine_lap(src, row)
                e = cond[row] * lap
                rhs = u + H[m] * e + known(m, row)
                dst[row + 1] = apply4(prop, rhs)
                if es is not None:
                    es[m, row] = e
                us.append(u)
                ex.append(e)
                rs.append(rhs)
            pu[m, pair + 1] = pool(*us)
            pe[m, pair] = pool(*ex)
            if pr is not None:
                pr[m, pair] = pool(*rs)

        loop(GX, body, unroll=8)

    def last(pair):
        us, ex = [], []
        for row in (2 * pair, 2 * pair + 1):
            u, lap = fine_lap(bufs[4], row)
            e = cond[row] * lap
            if es is not None:
                es[4, row] = e
            us.append(u)
            ex.append(e)
        pu[4, pair + 1] = pool(*us)
        pe[4, pair] = pool(*ex)

    loop(GX, last, unroll=8)


def coarse_known(pu, pe, pr, cc, plane, lhs, kc, olds=None):
    matrix = lhs[3]

    def body(pair):
        rows = (2 * pair, 2 * pair + 1)
        ic, ec = [], []
        for c in range(3):
            laps = [coarse_lap(pu.at[2 * c], row) for row in rows]
            ec.append([cc[row] * lap for row, (_, lap) in zip(rows, laps)])
            both = apply4(matrix, jnp.concatenate([u for u, _ in laps], axis=1))
            ic.append([both[:, :LANES], both[:, LANES:]])
        for place, row in enumerate(rows):
            flat = rows8(plane[row])
            u = [pu[j, row + 1] for j in range(5)]
            e = [pe[j, row] for j in range(5)]
            total = [e[0] + ic[0][place]]
            for m in range(4):
                if pr is None:
                    im = (u[m + 1] - u[m]) * (1.0 / H[m]) - (e[m] + flat)
                else:
                    im = (u[m + 1] - pr[m, row]) * (1.0 / H[m])
                total.append(e[m + 1] + im)
            for k in range(2):
                value = HALF * (flat - ic[k + 1][place]) - ec[k][place]
                for j in range(5):
                    value = value + SC[k][j] * total[j]
                kc[k, row] = value
            if olds is not None:
                for c in range(3):
                    olds[c, row] = 2.0 * ec[c][place]
                    olds[3 + c, row] = ic[c][place]

    loop(GX // 2, body, unroll=4)


def finish_known(bufs, es, olds, plane, matrix, k0, part, parts):
    count = GX // parts

    def body(index):
        pair = part * count + index
        wide = []
        for m in range(4):
            total = ALPHA[m][0] * olds[0, pair] + BETA[m][0] * olds[3, pair]
            for c in (1, 2):
                total = total + ALPHA[m][c] * olds[c, pair] + BETA[m][c] * olds[3 + c, pair]
            wide.append(twice(total))
        for row in (2 * pair, 2 * pair + 1):
            flat = rows8(plane[row])
            u = [buf[row + 1] for buf in bufs]
            e = [es[j, row] for j in range(5)]
            total = [e[0] + apply4(matrix, u[0])]
            change = [u[m + 1] - u[m] for m in range(4)]
            for m in range(4):
                total.append(e[m + 1] + (change[m] * (1.0 / H[m]) - (e[m] + flat)))
            for m in range(4):
                value = (2.0 * H[m]) * flat - (change[m] + wide[m])
                for j in range(5):
                    value = value + S[m][j] * total[j]
                k0[m, row] = value

    loop(count, body, unroll=4)


def pack(c_ref, base, count, main, to_right, to_left):
    at = lane((DEPTH, LANES))
    for quad in range(count // 4):
        rows = [c_ref[base + 4 * quad + r] for r in range(4)]
        for half in range(2 if main is not None else 0):
            main[2 * quad + half] = jnp.where(
                at < 64, roll(rows[2 * half], -32), roll(rows[2 * half + 1], 32)
            )
        for out, start in ((to_right, 64), (to_left, 32)):
            value = roll(rows[0], -start)
            for r in range(1, 4):
                value = jnp.where(at < 32 * r, value, roll(rows[r], 32 * r - start))
            out[quad] = value


def sides():
    gy = lax.axis_index("gy")
    last = lax.axis_size("gy") - 1
    return jnp.where(gy > 0, 1.0, 0.0).astype(F32), jnp.where(gy < last, 1.0, 0.0).astype(F32)


def unpack(main, left, right, count, dst, base):
    at = lane((DEPTH, LANES))
    has_left, has_right = sides()
    for quad in range(count // 4):
        for r in range(4):
            centre = roll(main[2 * quad + r // 2], 32 if r % 2 == 0 else -32)
            before = has_left * roll(left[quad], -32 * r)
            after = has_right * roll(right[quad], 96 - 32 * r)
            value = jnp.where(at < 32, before, jnp.where(at < 96, centre, after))
            dst[base + 4 * quad + r + 1] = value


def put(rows, count, dst, base):
    for r in range(count):
        dst[base + r + 1] = rows[r]


def receive(kind, got, dst):
    gx = lax.axis_index("gx")
    if kind == "quads":
        for k, rows in zip((0, 1, 2, 3), got):
            put(rows, CXT, dst, CXT * lax.bitwise_xor(gx, k))
    elif kind == "quads packed":
        for k, slabs in zip((0, 1, 2, 3), got):
            base = CXT * lax.bitwise_xor(gx, k)
            unpack(slabs, slabs.at[pl.ds(2, 1)], slabs.at[pl.ds(3, 1)], CXT, dst, base)
    else:
        core = lax.bitwise_and(gx, 1)
        for k in range(2):
            unpack(*got[3 * k : 3 * k + 3], 8, dst, 8 * lax.bitwise_xor(core, k))


def window_base():
    return jnp.clip(CXT * lax.axis_index("gx") - 2, 0, 8)


def send(kind, c_ref, outs):
    gx = lax.axis_index("gx")
    if kind == "quads":
        for r in range(CXT):
            outs[0][r] = c_ref[CXT * gx + r]
    elif kind == "quads packed":
        pack(c_ref, CXT * gx, CXT, *outs)
    elif kind == "halves packed":
        pack(c_ref, 8 * lax.bitwise_and(gx, 1), 8, *outs)
    else:
        base = window_base()
        for r in range(8):
            outs[0][r] = c_ref[base + r]


def outs_of(kind):
    if kind == "quads":
        return [shape(CXT, DEPTH, LANES)]
    if kind == "window":
        return [shape(8, DEPTH, LANES)]
    count = 1 if kind == "quads packed" else 2
    return [shape(2 * count, DEPTH, LANES)] + [shape(count, DEPTH, LANES)] * 2


def takes(kind):
    return {"quads": 4, "quads packed": 4, "halves packed": 6, "window": 1}[kind]


def is_from(steps):
    return jnp.where(lax.axis_index("tm") >= steps, 1.0, 0.0).astype(F32)


def props_kernel(faces_ref, out_ref):
    shape = (DEPTH, DEPTH)
    faces = jnp.broadcast_to(faces_ref[...], shape)
    row = lax.broadcasted_iota(jnp.int32, shape, 0)
    col = lane(shape)
    shape = (DEPTH, LANES)
    upper = jnp.sum(jnp.where(row == col, faces, 0.0), axis=1, keepdims=True)
    lower = jnp.sum(jnp.where(row + 1 == col, faces, 0.0), axis=1, keepdims=True)
    upper, lower = jnp.broadcast_to(upper, shape), jnp.broadcast_to(lower, shape)
    row = lax.broadcasted_iota(jnp.int32, shape, 0)
    col = lane(shape)
    level = jnp.where(col < DEPTH, col, col - DEPTH)
    eye = jnp.where(row == level, 1.0, 0.0).astype(F32)

    def shifted(value, step):
        return pltpu.roll(value, step % DEPTH, 0)

    def inverse(length):
        a = -VERTICAL * length * jnp.where(row == 0, 0.0, upper)
        c = -VERTICAL * length * lower
        b = 1.0 + VERTICAL * length * (upper + lower)
        r = eye
        step = 1
        while step < DEPTH:
            alpha = -a / shifted(b, step)
            gamma = -c / shifted(b, -step)
            b, r, a, c = (
                b + alpha * shifted(c, step) + gamma * shifted(a, -step),
                r + alpha * shifted(r, step) + gamma * shifted(r, -step),
                alpha * shifted(a, step),
                gamma * shifted(c, -step),
            )
            step *= 2
        return r / b

    def store(index, value):
        high = value.astype(BF16)
        out_ref[index, :, :LANES] = high
        out_ref[index, :, LANES:] = (value - high.astype(F32)).astype(BF16)

    fine = inverse(jnp.where(col < DEPTH, H[0], H[1]).astype(F32))
    other = roll(fine, DEPTH)
    store(0, jnp.where(col < DEPTH, fine, other))
    store(1, jnp.where(col < DEPTH, other, fine))
    store(2, inverse(jnp.full(shape, HALF, F32)))
    matrix = jnp.where(row == level, -VERTICAL * (upper + lower), 0.0)
    matrix = matrix + jnp.where(level == row - 1, VERTICAL * upper, 0.0)
    matrix = matrix + jnp.where(level == row + 1, VERTICAL * lower, 0.0)
    store(3, matrix)


def prep_kernel(
    cells, profiles, temp_in, conduct_in, main, to_right, to_left, counts, temp, conduct, sems
):
    copies = [
        pltpu.make_async_copy(temp_in, temp, sems.at[0]),
        pltpu.make_async_copy(conduct_in, conduct, sems.at[1]),
    ]
    for copy in copies:
        copy.start()
    src = lax.broadcasted_iota(jnp.int32, (LANES, LANES), 0)
    dst = lane((LANES, LANES))
    odd = 2 * jnp.where(dst < 32, dst + 32, dst - 96) + 1
    target = jnp.where((dst >= 32) & (dst < 96), 2 * (dst - 32), odd)
    pick = jnp.where(src == target, 1.0, 0.0).astype(BF16)
    for copy in copies:
        copy.wait()
    for row in range(TX):
        for place, ref in enumerate((temp, conduct)):
            main[row, DEPTH * place : DEPTH * (place + 1)] = sum(
                jnp.dot(part, pick, preferred_element_type=F32) for part in split3(ref[:, row, :])
            )
    counts[...] = jnp.zeros_like(counts)
    at = lane((8, LANES))
    profile = lax.broadcasted_iota(jnp.int32, (8, LANES), 0)
    for b in range(16):
        cell, which = cells[b], profiles[b]
        row, y = cell // LANES, cell % LANES
        half = y // 2
        column = jnp.where(y % 2 == 0, half + 32, jnp.where(half < 32, half + 96, half - 32))
        hit = (at == column) & (profile == which)
        counts[row] = counts[row] + jnp.where(hit, 1.0, 0.0)
    for row in range(TX):
        main[row, 2 * DEPTH :] = counts[row]
    first = lane((2 * DEPTH + 8, LANES)) % 64 < 32
    for slab in range(TX // 2):
        low, high = roll(main[slab], 64), roll(main[slab + TX // 2], 32)
        to_right[slab] = jnp.where(first, low, high)
        to_left[slab] = jnp.where(first, high, low)


def first_kernel(
    main0,
    main1,
    main2,
    main3,
    strip0,
    strip1,
    strip2,
    strip3,
    table0,
    table1,
    table2,
    lhs,
    c_out,
    v_out,
    cc,
    cond_out,
    init_out,
    plane,
    plane_c,
    init,
    buf_a,
    buf_b,
    cond,
    early,
    early_c,
    pu,
    pe,
    kc,
    node_a,
    node_b,
    sems,
):
    bufs = (init, buf_a, buf_b, buf_a, buf_b)
    planes = (plane, early.at[0], early.at[1])
    planes_c = (plane_c, early_c.at[0], early_c.at[1])
    for ref in (init, buf_a, buf_b, node_a, node_b):
        zero_edges(ref)
    for j in range(5):
        zero_edges(pu.at[j])
    gx = lax.axis_index("gx")
    at = lane((2 * DEPTH + 8, LANES))
    core = lax.bitwise_and(gx, 1)
    rates = [jnp.broadcast_to(t[...], (8, 2 * LANES)) for t in (table0, table2, table1)]
    inside = (at >= 32) & (at < 96)
    first = at % 64 < 32
    has_left, has_right = sides()
    for k, (main, strip) in enumerate(
        ((main0, strip0), (main1, strip1), (main2, strip2), (main3, strip3))
    ):
        base = TX * lax.bitwise_xor(gx, k)

        def assemble(q, main=main, strip=strip, base=base):
            left, right = has_left * strip[q], has_right * strip[4 + q]
            for row, edge in (
                (q, jnp.where(first, left, right)),
                (q + 4, roll(jnp.where(first, right, left), 32)),
            ):
                centre = main[row]
                even = jnp.where(inside, centre, edge)
                odd = roll(jnp.where(inside, edge, centre), 64)
                window = jnp.concatenate([even, odd], axis=1)
                init[base + row + 1] = window[:DEPTH]
                cond[base + row] = LATERAL * window[DEPTH : 2 * DEPTH]
                counts = window[2 * DEPTH :]
                for t in range(3):
                    heat = jnp.sum(counts * rates[t], axis=0, keepdims=True)
                    planes[t][base + row] = jnp.broadcast_to(heat, (8, 2 * LANES))

        loop(TX // 2, assemble, unroll=2)
    copies = [
        pltpu.make_async_copy(cond, cond_out, sems.at[0]),
        pltpu.make_async_copy(init, init_out, sems.at[1]),
    ]
    for copy in copies:
        copy.start()

    def coarsen(row):
        cc[row] = (0.25 * HALF) * pool(cond[2 * row], cond[2 * row + 1])
        for t in range(3):
            planes_c[t][row] = pool(planes[t][2 * row], planes[t][2 * row + 1])

    loop(GX, coarsen, unroll=4)
    prop = lhs[2]
    index = lax.axis_index("tm")

    def one_slice(t):
        sweep(bufs, cond, lhs, lambda m, row: rows8(H[m] * early[t, row]), pu, pe)
        coarse_known(pu, pe, None, cc, early_c.at[t], lhs, kc)
        for pair in range(GX // 2):
            both = apply4(prop, jnp.concatenate([kc[0, 2 * pair], kc[0, 2 * pair + 1]], axis=1))
            node_b[2 * pair + 1] = both[:, :LANES]
            node_b[2 * pair + 2] = both[:, LANES:]
        coarse_step(node_b, node_a, cc, prop, kc.at[1])
        back = 3 + core - 2 * t
        swept = jnp.where(index >= back, 1.0, 0.0).astype(F32)
        begun = jnp.where(index == back - 1, 1.0, 0.0).astype(F32)

        def choose(row):
            node_a[row + 1] = swept * node_a[row + 1] + begun * pu[0, row + 1]

        loop(GX, choose, unroll=8)

        @pl.when(t == 0)
        def _():
            chain_power(node_a, node_b, cc, prop, 2)
            for row in range(GX):
                c_out[row] = node_a[row + 1]

    loop(2, one_slice)
    after1 = is_from(1)
    is0 = 1.0 - after1

    def choose(row):
        node_a[row + 1] = c_out[row] + node_a[row + 1]
        for fine in (2 * row, 2 * row + 1):
            before = buf_b[fine + 1] - twice(pu[4, row + 1])
            here = init[fine + 1] - twice(pu[0, row + 1])
            v_out[fine] = after1 * before + is0 * here

    loop(GX, choose, unroll=4)

    @pl.when(core == 1)
    def _():
        chain_power(node_a, node_b, cc, prop, 1)

    for row in range(GX):
        c_out[row] = node_a[row + 1]
    for copy in copies:
        copy.wait()


def known_kernel(
    init,
    cond,
    plane,
    plane_c,
    cc,
    lhs,
    k0_out,
    kc,
    k0,
    node_1,
    node_2,
    node_3,
    node_4,
    es,
    pu,
    pe,
    olds,
    sems,
):
    bufs = (init, node_1, node_2, node_3, node_4)
    for ref in bufs[1:]:
        zero_edges(ref)
    for j in range(5):
        zero_edges(pu.at[j])
    sweep(bufs, cond, lhs, lambda m, row: rows8(H[m] * plane[row]), pu, pe, None, es)
    coarse_known(pu, pe, None, cc, plane_c, lhs, kc, olds)
    copies = []
    for part in range(4):
        finish_known(bufs, es, olds, plane, lhs[3], k0, part, 4)
        rows = pl.ds(part * (FX // 4), FX // 4)
        copies.append(
            pltpu.make_async_copy(k0.at[:, rows], k0_out.at[:, rows], sems.at[part])
        )
        copies[-1].start()
    for copy in copies:
        copy.wait()


def phase_kernel(steps, parts, kind_in, kind_out, beside, *refs):
    count = takes(kind_in)
    got, refs = refs[:count], refs[count:]
    own, refs = refs[: 2 * beside], refs[2 * beside :]
    c_in, (cc_in, lhs, c_out), refs = refs[:parts], refs[parts : parts + 3], refs[parts + 3 :]
    outs, (node_a, node_b, cc, c_old, sems) = refs[:-5], refs[-5:]
    copy_cc = pltpu.make_async_copy(cc_in, cc, sems.at[0])
    copy_cc.start()
    copies = [
        pltpu.make_async_copy(c_in[k], c_old.at[k], sems.at[1 + k]) for k in range(parts)
    ]
    for copy in copies:
        copy.start()
    zero_edges(node_a)
    zero_edges(node_b)
    receive(kind_in, got, node_a)
    copy_cc.wait()
    chain_power(node_a, node_b, cc, lhs[2], steps)
    here = is_from(steps)
    for copy in copies:
        copy.wait()

    if beside:
        at = lane((DEPTH, LANES))
        has_left, has_right = sides()
        for row in range(GX):
            before = has_left * roll(own[0][row // 4], -32 * (row % 4))
            after = has_right * roll(own[1][row // 4], 96 - 32 * (row % 4))
            c_old[0, row] = jnp.where(at < 32, before, jnp.where(at < 96, c_old[0, row], after))

    def add(row):
        value = c_old[0, row] + here * node_a[row + 1]
        for k in range(1, parts):
            value = value + c_old[k, row]
        c_out[row] = value

    loop(GX, add, unroll=8)
    send(kind_out, c_out, outs)


def second_kernel(
    steps,
    main_a,
    left_a,
    right_a,
    main_b,
    left_b,
    right_b,
    c_in,
    cc,
    lhs,
    k0_in,
    v_first,
    v_second,
    kc_in,
    cond_in,
    plane_c,
    c_out,
    hop,
    to_right,
    to_left,
    own_right,
    own_left,
    v_tile,
    k0,
    v,
    cond,
    start,
    buf_a,
    buf_b,
    dk,
    pu,
    pe,
    pr,
    kc,
    node_a,
    node_b,
    node_c,
    sems,
):
    copies = [
        pltpu.make_async_copy(src, dst, sems.at[place])
        for place, (src, dst) in enumerate(((v_first, v), (cond_in, cond), (k0_in, k0)))
    ]
    core = lax.bitwise_and(lax.axis_index("gx"), 1)

    @pl.when(core == 0)
    def _():
        copies[0].start()

    @pl.when(core == 1)
    def _():
        pltpu.make_async_copy(v_second, v, sems.at[0]).start()

    for copy in copies[1:]:
        copy.start()
    for ref in (start, buf_a, buf_b, node_a, node_b, node_c):
        zero_edges(ref)
    for j in range(5):
        zero_edges(pu.at[j])
    receive("halves packed", (main_a, left_a, right_a, main_b, left_b, right_b), node_a)
    prop, matrix = lhs[2], lhs[3]
    chain_power(node_a, node_b, cc, prop, steps)
    here = is_from(steps)
    copies[0].wait()

    def add(row):
        value = c_in[row] + here * node_a[row + 1]
        node_a[row + 1] = value
        wide = twice(value)
        start[2 * row + 1] = v[2 * row] + wide
        start[2 * row + 2] = v[2 * row + 1] + wide

    loop(GX, add, unroll=4)

    def spread(row, c, explicit, implicit):
        for m in range(4):
            total = (2.0 * ALPHA[m][c]) * explicit + BETA[m][c] * implicit
            dk[m, row] = total if c == 0 else dk[m, row] + total

    def stage(c, src, dst):
        def body(pair):
            rows = (2 * pair, 2 * pair + 1)
            laps = [coarse_lap(src, row) for row in rows]
            ex = [cc[row] * lap for row, (_, lap) in zip(rows, laps)]
            if c == 0:
                both = apply4(matrix, jnp.concatenate([u for u, _ in laps], axis=1))
                implicit = (both[:, :LANES], both[:, LANES:])
            else:
                implicit = (kc[c - 1, rows[0]], kc[c - 1, rows[1]])
            for place in range(2):
                spread(rows[place], c, ex[place], implicit[place])
            if c < 2:
                rhs = jnp.concatenate(
                    [u + e + kc_in[c, row] for row, (u, _), e in zip(rows, laps, ex)], axis=1
                )
                node = apply4(prop, rhs)
                dst[rows[0] + 1] = node[:, :LANES]
                dst[rows[1] + 1] = node[:, LANES:]
                after = (node - rhs) * (1.0 / HALF)
                kc[c, rows[0]] = after[:, :LANES]
                kc[c, rows[1]] = after[:, LANES:]

        loop(GX // 2, body, unroll=4)

    stage(0, node_a, node_b)
    stage(1, node_b, node_c)
    stage(2, node_c, None)
    copies[1].wait()
    copies[2].wait()

    def known(m, row):
        return k0[m, row] + twice(dk[m, row // 2])

    sweep((start, buf_a, buf_b, buf_a, buf_b), cond, lhs, known, pu, pe, pr)
    coarse_known(pu, pe, pr, cc, plane_c, lhs, kc)
    is0 = 1.0 - is_from(1)

    def begin(row):
        node_a[row + 1] = is0 * pu[0, row + 1]

    loop(GX, begin, unroll=4)
    coarse_step(node_a, node_b, cc, prop, kc.at[0])
    coarse_step(node_b, node_a, cc, prop, kc.at[1])

    def keep(row):
        c_out[row] = node_a[row + 1]

    loop(GX, keep, unroll=4)
    send("halves packed", c_out, (hop, to_right, to_left))
    pack(c_out, 0, GX, None, own_right, own_left)
    base = CXT * lax.axis_index("gx")
    for r in range(CXT):
        for q in range(2):
            fine = 2 * r + q
            v_tile[fine] = buf_b[2 * base + fine + 1] - twice(pu[4, base + r + 1])


def last_kernel(got, c_in, cc, lhs, v_tile, out, node_a, node_b):
    zero_edges(node_a)
    zero_edges(node_b)
    put(got, 8, node_a, 0)
    base = window_base()
    coarse_step(node_a, node_b, cc, lhs[2], None, 8, base)
    coarse_step(node_b, node_a, cc, lhs[2], None, 8, base)
    here = is_from(1)
    tile = CXT * lax.axis_index("gx")
    src = lax.broadcasted_iota(jnp.int32, (2 * LANES, LANES), 0)
    dst = lane((2 * LANES, LANES))
    target = 32 + dst // 2 + jnp.where(dst % 2 == 1, LANES, 0)
    pick = jnp.where(src == target, 1.0, 0.0).astype(BF16)
    for r in range(CXT):
        wide = twice(c_in[tile + r] + here * node_a[tile - base + r + 1])
        for q in range(2):
            value = v_tile[2 * r + q] + wide
            out[0, :, 2 * r + q, :] = sum(
                jnp.dot(part, pick, preferred_element_type=F32) for part in split3(value)
            )


VMEM = pl.BlockSpec(memory_space=pltpu.VMEM)
SMEM = pl.BlockSpec(memory_space=pltpu.SMEM)
ANY = pl.BlockSpec(memory_space=pl.ANY)
HBM = pl.BlockSpec(memory_space=pltpu.HBM)


def shape(*dims, dtype=F32):
    return jax.ShapeDtypeStruct(dims, dtype)


def call(kernel, name, outs, scratch, *operands, where={}, out_any=(), sems=0, limit=16, flops=10**8):
    spaces = [where.get(index, VMEM) for index in range(len(operands))]
    single = not isinstance(outs, list)
    out_specs = [ANY if index in out_any else VMEM for index in range(1 if single else len(outs))]
    semaphores = [pltpu.SemaphoreType.DMA((sems,))] if sems else []
    return pl.pallas_call(
        kernel,
        name=name,
        out_shape=outs,
        in_specs=spaces,
        out_specs=out_specs[0] if single else out_specs,
        scratch_shapes=[pltpu.VMEM(dims, F32) for dims in scratch] + semaphores,
        compiler_params=pltpu.CompilerParams(vmem_limit_bytes=limit * MIB),
        cost_estimate=pl.CostEstimate(flops=flops, bytes_accessed=10**6, transcendentals=0),
    )(*operands)


COARSE = (GX, DEPTH, LANES)
COARSE_PAD = (GX + 2, DEPTH, LANES)
FINE = (FX, DEPTH, 2 * LANES)
FINE_PAD = (FX + 2, DEPTH, 2 * LANES)


def shift(value, steps, sideways=0):
    slices, columns = lax.axis_size("tm"), lax.axis_size("gy")
    pairs = [
        (s * columns + g, (s + steps) % slices * columns + (g + sideways) % columns)
        for s in range(slices)
        for g in range(columns)
    ]
    return lax.ppermute(value, ("tm", "gy"), pairs)


def swap(value, bit):
    return lax.ppermute(value, "gx", [(g, g ^ bit) for g in range(lax.axis_size("gx"))])


def quads(value):
    far = swap(value, 2)
    return [value, swap(value, 1), far, swap(far, 1)]


def halves(parts):
    return list(parts) + [swap(part, 1) for part in parts]


def fetch_strips(hops, steps):
    main, to_right, to_left = hops
    return [shift(main, steps), shift(to_right, steps, 1), shift(to_left, steps, -1)]


def on_device(initial_temp, conductivity, vert_cond, borehole_cells, borehole_profiles, heat_table):
    slices, rows = lax.axis_size("tm"), lax.axis_size("gx")

    def earlier(back):
        pairs = [
            (t * rows + g, (t + back + g % 2) % slices * rows + g)
            for t in range(slices)
            for g in range(rows)
        ]
        return lax.ppermute(heat_table, ("tm", "gx"), pairs)

    main, to_right, to_left = call(
        prep_kernel,
        "prep",
        [
            shape(TX, 2 * DEPTH + 8, LANES),
            shape(TX // 2, 2 * DEPTH + 8, LANES),
            shape(TX // 2, 2 * DEPTH + 8, LANES),
        ],
        [(TX, 8, LANES), (DEPTH, TX, LANES), (DEPTH, TX, LANES)],
        borehole_cells.reshape(-1),
        borehole_profiles.reshape(-1),
        initial_temp,
        conductivity,
        where={0: SMEM, 1: SMEM, 2: HBM, 3: HBM},
        sems=2,
    )
    beside = swap(main, 1)
    to_right, to_left, beside = lax.optimization_barrier((to_right, to_left, beside))
    far, table1, table2 = lax.optimization_barrier((swap(main, 2), earlier(1), earlier(3)))
    mains = [main, beside, far, swap(far, 1)]
    lhs = call(
        props_kernel,
        "props",
        shape(4, DEPTH, 2 * LANES, dtype=BF16),
        [],
        vert_cond.reshape(1, DEPTH),
    )
    near = (shift(to_right, 0, 1), shift(to_left, 0, -1), lhs)
    from_left, from_right, lhs = lax.optimization_barrier(near)
    strip = jnp.concatenate([from_left, from_right], axis=0)

    c, v, cc, cond, init, plane, plane_c = call(
        first_kernel,
        "early_sweep",
        [
            shape(*COARSE),
            shape(*FINE),
            shape(*COARSE),
            shape(*FINE),
            shape(*FINE_PAD),
            shape(FX, 8, 2 * LANES),
            shape(GX, 8, LANES),
        ],
        [FINE_PAD] * 3
        + [
            FINE,
            (2, FX, 8, 2 * LANES),
            (2, GX, 8, LANES),
            (5, *COARSE_PAD),
            (5, *COARSE),
            (2, *COARSE),
            COARSE_PAD,
            COARSE_PAD,
        ],
        *mains,
        *quads(strip),
        heat_table,
        table1,
        table2,
        lhs,
        out_any=(3, 4),
        sems=2,
        limit=60,
    )
    k0, kc = call(
        known_kernel,
        "own_sweep",
        [shape(4, *FINE), shape(2, *COARSE)],
        [(4, *FINE)] + [FINE_PAD] * 4 + [(5, *FINE), (5, *COARSE_PAD), (5, *COARSE), (6, *COARSE)],
        init,
        cond,
        plane,
        plane_c,
        cc,
        lhs,
        out_any=(0,),
        sems=4,
        limit=60,
        flops=10**10,
    )

    def phase(steps, name, kind_in, kind_out, got, c, own=()):
        kernel = functools.partial(
            phase_kernel, steps, len(c), kind_in, kind_out, len(own) // 2
        )
        outs = [shape(*COARSE)] + outs_of(kind_out)
        scratch = [COARSE_PAD, COARSE_PAD, COARSE, (len(c), *COARSE)]
        got = [*got, *own]
        where = {len(got) + k: HBM for k in range(len(c))}
        where[len(got) + len(c)] = ANY
        c, *hops = call(
            kernel, name, outs, scratch, *got, *c, cc, lhs, where=where, sems=1 + len(c)
        )
        return [c], hops

    c = [c, swap(c, 1)]
    base = CXT * lax.axis_index("gx")
    hop = sum(lax.dynamic_slice_in_dim(part, base, CXT, axis=0) for part in c)
    v, hop = lax.optimization_barrier((v, hop))
    v_other = swap(v, 1)
    got, k0, kc = lax.optimization_barrier((shift(hop, 4), k0, kc))
    got = quads(got)
    c, hops = phase(4, "chain_a4", "quads", "halves packed", got, c)
    got = halves(fetch_strips(hops, 8))
    c, *hops, own_right, own_left, v_tile = call(
        functools.partial(second_kernel, 8),
        "second_sweep",
        [shape(*COARSE)]
        + outs_of("halves packed")
        + [shape(4, DEPTH, LANES)] * 2
        + [shape(TX, DEPTH, 2 * LANES)],
        [
            (4, *FINE),
            FINE,
            FINE,
            FINE_PAD,
            FINE_PAD,
            FINE_PAD,
            (4, *COARSE),
            (5, *COARSE_PAD),
            (5, *COARSE),
            (4, *COARSE),
            (2, *COARSE),
            COARSE_PAD,
            COARSE_PAD,
            COARSE_PAD,
        ],
        *got,
        c[0],
        cc,
        lhs,
        k0,
        v,
        v_other,
        kc,
        cond,
        plane_c,
        where={9: ANY, 10: ANY, 11: ANY, 13: ANY},
        sems=3,
        limit=60,
    )
    got = halves(fetch_strips(hops, 8))
    own = (shift(own_right, 0, 1), shift(own_left, 0, -1))
    c, hops = phase(8, "chain_b8", "halves packed", "quads", got, [c], own)
    got = quads(shift(hops[0], 4))
    c, hops = phase(4, "chain_b4", "quads", "quads", got, c)
    got = quads(shift(hops[0], 2))
    c, hops = phase(2, "chain_b2", "quads", "window", got, c)
    got = shift(hops[0], 1)
    return call(
        last_kernel,
        "finish",
        shape(1, DEPTH, TX, LANES),
        [(10, DEPTH, LANES)] * 2,
        got,
        c[0],
        cc,
        lhs,
        v_tile,
    )


def solution(mesh):
    placed = (
        P(None, "gx", "gy"),
        P(None, "gx", "gy"),
        P(),
        P("gx", "gy", None),
        P("gx", "gy", None),
        P(None, "tm"),
    )
    return jax.shard_map(
        on_device, mesh=mesh, in_specs=placed, out_specs=P("tm", None, "gx", "gy"), check_vma=False
    )
```

```python
import functools
import math

import jax
import jax.numpy as jnp
from jax import lax
from jax.experimental import pallas as pl
from jax.experimental.pallas import tpu as pltpu
from jax.sharding import PartitionSpec as P

F32 = jnp.float32
BF16 = jnp.bfloat16
LATERAL = 0.3
VERTICAL = 4.0
FINE_NODES = [0.0, (1.0 - math.sqrt(3.0 / 7.0)) / 2.0, 0.5, (1.0 + math.sqrt(3.0 / 7.0)) / 2.0, 1.0]
COARSE_NODES = [0.0, 0.5, 1.0]
HALF = 0.5
DEPTH = 64
TX = 8
CXT = 4
FX = 32
GX = 16
LANES = 128
MIB = 2**20


def basis_coeffs(times_list, basis_index):
    coeffs = [1.0]
    denominator = 1.0
    for other_index in range(len(times_list)):
        if other_index != basis_index:
            other_time = times_list[other_index]
            widened = [0.0] * (len(coeffs) + 1)
            for power in range(len(coeffs)):
                widened[power + 1] = widened[power + 1] + coeffs[power]
                widened[power] = widened[power] - other_time * coeffs[power]
            coeffs = widened
            denominator = denominator * (times_list[basis_index] - other_time)
    return [entry / denominator for entry in coeffs]


def poly_value(coeffs, point):
    return sum(coeffs[power] * point**power for power in range(len(coeffs)))


def poly_integral(coeffs, lower, upper):
    return sum(
        coeffs[power] * (upper ** (power + 1) - lower ** (power + 1)) / (power + 1)
        for power in range(len(coeffs))
    )


H = [FINE_NODES[m + 1] - FINE_NODES[m] for m in range(4)]
S = [
    [poly_integral(basis_coeffs(FINE_NODES, j), FINE_NODES[m], FINE_NODES[m + 1]) for j in range(5)]
    for m in range(4)
]
W = [[poly_value(basis_coeffs(COARSE_NODES, c), t) for c in range(3)] for t in FINE_NODES]
SC = [[S[2 * m][j] + S[2 * m + 1][j] for j in range(5)] for m in range(2)]
SW = [[sum(S[m][j] * W[j][c] for j in range(5)) for c in range(3)] for m in range(4)]
ALPHA = [[SW[m][c] - H[m] * W[m][c] for c in range(3)] for m in range(4)]
BETA = [[SW[m][c] - H[m] * W[m + 1][c] for c in range(3)] for m in range(4)]


def loop(count, body, unroll=1):
    def step(index, carry):
        body(index)
        return carry

    lax.fori_loop(0, count, step, 0, unroll=unroll)


def roll(value, shift):
    return pltpu.roll(value, shift % value.shape[-1], value.ndim - 1)


def lane(shape):
    return lax.broadcasted_iota(jnp.int32, shape, len(shape) - 1)


def apply4(lhs, value):
    high = value.astype(BF16)
    low = (value - high.astype(F32)).astype(BF16)
    stacked = jnp.concatenate([high, low, high, low], axis=0)
    return jnp.dot(lhs, stacked, preferred_element_type=F32)


def split3(value):
    high = value.astype(BF16)
    rest = value - high.astype(F32)
    mid = rest.astype(BF16)
    low = (rest - mid.astype(F32)).astype(BF16)
    return high, mid, low


def fine_lap(src, row):
    u = src[row + 1]
    even, odd = u[:, :LANES], u[:, LANES:]
    beside = jnp.concatenate([odd + roll(odd, 1), even + roll(even, -1)], axis=1)
    return u, (src[row] + src[row + 2]) + beside - 4.0 * u


def coarse_lap(src, row):
    u = src[row + 1]
    return u, (src[row] + src[row + 2]) + (roll(u, 1) + roll(u, -1)) - 4.0 * u


def pool(first, second):
    total = first + second
    return 0.25 * (total[:, :LANES] + total[:, LANES:])


def twice(value):
    return jnp.concatenate([value, value], axis=1)


def rows8(value):
    return jnp.concatenate([value] * (DEPTH // 8), axis=0)


def zero_edges(ref):
    edge = jnp.zeros(ref.shape[1:], F32)
    ref[0] = edge
    ref[ref.shape[0] - 1] = edge


def coarse_step(src, dst, cc, prop, known=None, count=GX, base=0):
    for pair in range(count // 2):
        parts = []
        for row in (2 * pair, 2 * pair + 1):
            u, lap = coarse_lap(src, row)
            rhs = u + cc[base + row] * lap
            parts.append(rhs if known is None else rhs + known[row])
        node = apply4(prop, jnp.concatenate(parts, axis=1))
        dst[2 * pair + 1] = node[:, :LANES]
        dst[2 * pair + 2] = node[:, LANES:]


def chain_power(first, second, cc, prop, steps, count=GX, base=0):
    each = min(steps, 4)

    def body(_):
        for _ in range(each):
            coarse_step(first, second, cc, prop, None, count, base)
            coarse_step(second, first, cc, prop, None, count, base)

    if steps == each:
        body(0)
    else:
        loop(steps // each, body)


def sweep(bufs, cond, lhs, known, pu, pe, pr=None, es=None):
    for m in range(4):
        src, dst = bufs[m], bufs[m + 1]
        prop = lhs[0] if m in (0, 3) else lhs[1]

        def body(pair, m=m, src=src, dst=dst, prop=prop):
            us, ex, rs = [], [], []
            for row in (2 * pair, 2 * pair + 1):
                u, lap = fine_lap(src, row)
                e = cond[row] * lap
                rhs = u + H[m] * e + known(m, row)
                dst[row + 1] = apply4(prop, rhs)
                if es is not None:
                    es[m, row] = e
                us.append(u)
                ex.append(e)
                rs.append(rhs)
            pu[m, pair + 1] = pool(*us)
            pe[m, pair] = pool(*ex)
            if pr is not None:
                pr[m, pair] = pool(*rs)

        loop(GX, body, unroll=8)

    def last(pair):
        us, ex = [], []
        for row in (2 * pair, 2 * pair + 1):
            u, lap = fine_lap(bufs[4], row)
            e = cond[row] * lap
            if es is not None:
                es[4, row] = e
            us.append(u)
            ex.append(e)
        pu[4, pair + 1] = pool(*us)
        pe[4, pair] = pool(*ex)

    loop(GX, last, unroll=8)


def coarse_known(pu, pe, pr, cc, plane, lhs, kc, olds=None):
    matrix = lhs[3]

    def body(pair):
        rows = (2 * pair, 2 * pair + 1)
        ic, ec = [], []
        for c in range(3):
            laps = [coarse_lap(pu.at[2 * c], row) for row in rows]
            ec.append([cc[row] * lap for row, (_, lap) in zip(rows, laps)])
            both = apply4(matrix, jnp.concatenate([u for u, _ in laps], axis=1))
            ic.append([both[:, :LANES], both[:, LANES:]])
        for place, row in enumerate(rows):
            flat = rows8(plane[row])
            u = [pu[j, row + 1] for j in range(5)]
            e = [pe[j, row] for j in range(5)]
            total = [e[0] + ic[0][place]]
            for m in range(4):
                if pr is None:
                    im = (u[m + 1] - u[m]) * (1.0 / H[m]) - (e[m] + flat)
                else:
                    im = (u[m + 1] - pr[m, row]) * (1.0 / H[m])
                total.append(e[m + 1] + im)
            for k in range(2):
                value = HALF * (flat - ic[k + 1][place]) - ec[k][place]
                for j in range(5):
                    value = value + SC[k][j] * total[j]
                kc[k, row] = value
            if olds is not None:
                for c in range(3):
                    olds[c, row] = 2.0 * ec[c][place]
                    olds[3 + c, row] = ic[c][place]

    loop(GX // 2, body, unroll=4)


def finish_known(bufs, es, olds, plane, matrix, k0, part, parts):
    count = GX // parts

    def body(index):
        pair = part * count + index
        wide = []
        for m in range(4):
            total = ALPHA[m][0] * olds[0, pair] + BETA[m][0] * olds[3, pair]
            for c in (1, 2):
                total = total + ALPHA[m][c] * olds[c, pair] + BETA[m][c] * olds[3 + c, pair]
            wide.append(twice(total))
        for row in (2 * pair, 2 * pair + 1):
            flat = rows8(plane[row])
            u = [buf[row + 1] for buf in bufs]
            e = [es[j, row] for j in range(5)]
            total = [e[0] + apply4(matrix, u[0])]
            change = [u[m + 1] - u[m] for m in range(4)]
            for m in range(4):
                total.append(e[m + 1] + (change[m] * (1.0 / H[m]) - (e[m] + flat)))
            sums = [total[0] + total[4], total[1] + total[3], total[2]]
            gaps = [total[0] - total[4], total[1] - total[3]]
            for m in range(2):
                even = sum(0.5 * (S[m][j] + S[m][4 - j]) * sums[j] for j in range(2))
                even = even + S[m][2] * sums[2] + (2.0 * H[m]) * flat
                odd = sum(0.5 * (S[m][j] - S[m][4 - j]) * gaps[j] for j in range(2))
                k0[m, row] = (even + odd) - (change[m] + wide[m])
                k0[3 - m, row] = (even - odd) - (change[3 - m] + wide[3 - m])

    loop(count, body, unroll=4)


def pack(c_ref, base, count, main, to_right, to_left):
    at = lane((DEPTH, LANES))
    for quad in range(count // 4):
        rows = [c_ref[base + 4 * quad + r] for r in range(4)]
        for half in range(2 if main is not None else 0):
            main[2 * quad + half] = jnp.where(
                at < 64, roll(rows[2 * half], -32), roll(rows[2 * half + 1], 32)
            )
        for out, start in ((to_right, 64), (to_left, 32)):
            value = roll(rows[0], -start)
            for r in range(1, 4):
                value = jnp.where(at < 32 * r, value, roll(rows[r], 32 * r - start))
            out[quad] = value


def sides():
    gy = lax.axis_index("gy")
    last = lax.axis_size("gy") - 1
    return jnp.where(gy > 0, 1.0, 0.0).astype(F32), jnp.where(gy < last, 1.0, 0.0).astype(F32)


def unpack(main, left, right, count, dst, base):
    at = lane((DEPTH, LANES))
    has_left, has_right = sides()
    for quad in range(count // 4):
        for r in range(4):
            centre = roll(main[2 * quad + r // 2], 32 if r % 2 == 0 else -32)
            before = has_left * roll(left[quad], -32 * r)
            after = has_right * roll(right[quad], 96 - 32 * r)
            value = jnp.where(at < 32, before, jnp.where(at < 96, centre, after))
            dst[base + 4 * quad + r + 1] = value


def pack_near(rows, out):
    at = lane((DEPTH, LANES))
    count = len(rows)
    width = 64 // count
    for half in range(count // 2):
        out[half] = jnp.where(at < 64, roll(rows[2 * half], -32), roll(rows[2 * half + 1], 32))
    edges = None
    for r in range(count):
        begin = 2 * width * r
        before = roll(rows[r], begin - (32 - width))
        after = roll(rows[r], begin + width - 96)
        both = jnp.where(at < begin + width, before, after)
        edges = both if edges is None else jnp.where(at < begin, edges, both)
    out[count // 2] = edges


def unpack_near(slabs, count, dst, base):
    at = lane((DEPTH, LANES))
    width = 64 // count
    filled = (at >= 32 - width) & (at < 96 + width)
    edges = slabs[count // 2]
    for r in range(count):
        begin = 2 * width * r
        centre = roll(slabs[r // 2], 32 if r % 2 == 0 else -32)
        before = roll(edges, 32 - width - begin)
        after = roll(edges, 96 - width - begin)
        value = jnp.where(at < 32, before, jnp.where(at < 96, centre, after))
        dst[base + r + 1] = jnp.where(filled, value, 0.0)


def receive(kind, got, dst):
    gx = lax.axis_index("gx")
    if kind == "quads":
        for k, rows in zip((0, 1, 2, 3), got):
            unpack_near(rows, CXT, dst, CXT * lax.bitwise_xor(gx, k))
    else:
        core = lax.bitwise_and(gx, 1)
        for k in range(2):
            unpack(*got[3 * k : 3 * k + 3], 8, dst, 8 * lax.bitwise_xor(core, k))


def window_base():
    return jnp.clip(CXT * lax.axis_index("gx") - 2, 0, 8)


def send(kind, c_ref, outs):
    gx = lax.axis_index("gx")
    if kind == "quads":
        pack_near([c_ref[CXT * gx + r] for r in range(CXT)], outs[0])
    elif kind == "halves packed":
        pack(c_ref, 8 * lax.bitwise_and(gx, 1), 8, *outs)
    else:
        base = window_base()
        pack_near([c_ref[base + r] for r in range(8)], outs[0])


def outs_of(kind):
    if kind == "quads":
        return [shape(3, DEPTH, LANES)]
    if kind == "window":
        return [shape(5, DEPTH, LANES)]
    return [shape(4, DEPTH, LANES)] + [shape(2, DEPTH, LANES)] * 2


def takes(kind):
    return {"quads": 4, "halves packed": 6, "window": 1}[kind]


def is_from(steps):
    return jnp.where(lax.axis_index("tm") >= steps, 1.0, 0.0).astype(F32)


def props_kernel(faces_ref, out_ref):
    shape = (DEPTH, DEPTH)
    faces = jnp.broadcast_to(faces_ref[...], shape)
    row = lax.broadcasted_iota(jnp.int32, shape, 0)
    col = lane(shape)
    shape = (DEPTH, LANES)
    upper = jnp.sum(jnp.where(row == col, faces, 0.0), axis=1, keepdims=True)
    lower = jnp.sum(jnp.where(row + 1 == col, faces, 0.0), axis=1, keepdims=True)
    upper, lower = jnp.broadcast_to(upper, shape), jnp.broadcast_to(lower, shape)
    row = lax.broadcasted_iota(jnp.int32, shape, 0)
    col = lane(shape)
    level = jnp.where(col < DEPTH, col, col - DEPTH)
    eye = jnp.where(row == level, 1.0, 0.0).astype(F32)

    def shifted(value, step):
        return pltpu.roll(value, step % DEPTH, 0)

    def inverse(length):
        a = -VERTICAL * length * jnp.where(row == 0, 0.0, upper)
        c = -VERTICAL * length * lower
        b = 1.0 + VERTICAL * length * (upper + lower)
        r = eye
        step = 1
        while step < DEPTH:
            alpha = -a / shifted(b, step)
            gamma = -c / shifted(b, -step)
            b, r, a, c = (
                b + alpha * shifted(c, step) + gamma * shifted(a, -step),
                r + alpha * shifted(r, step) + gamma * shifted(r, -step),
                alpha * shifted(a, step),
                gamma * shifted(c, -step),
            )
            step *= 2
        return r / b

    def store(index, value):
        high = value.astype(BF16)
        out_ref[index, :, :LANES] = high
        out_ref[index, :, LANES:] = (value - high.astype(F32)).astype(BF16)

    fine = inverse(jnp.where(col < DEPTH, H[0], H[1]).astype(F32))
    other = roll(fine, DEPTH)
    store(0, jnp.where(col < DEPTH, fine, other))
    store(1, jnp.where(col < DEPTH, other, fine))
    store(2, inverse(jnp.full(shape, HALF, F32)))
    matrix = jnp.where(row == level, -VERTICAL * (upper + lower), 0.0)
    matrix = matrix + jnp.where(level == row - 1, VERTICAL * upper, 0.0)
    matrix = matrix + jnp.where(level == row + 1, VERTICAL * lower, 0.0)
    store(3, matrix)


def prep_kernel(
    cells, profiles, temp_in, conduct_in, main, to_right, to_left, counts, temp, conduct, sems
):
    copies = [
        pltpu.make_async_copy(temp_in, temp, sems.at[0]),
        pltpu.make_async_copy(conduct_in, conduct, sems.at[1]),
    ]
    for copy in copies:
        copy.start()
    src = lax.broadcasted_iota(jnp.int32, (LANES, LANES), 0)
    dst = lane((LANES, LANES))
    odd = 2 * jnp.where(dst < 32, dst + 32, dst - 96) + 1
    target = jnp.where((dst >= 32) & (dst < 96), 2 * (dst - 32), odd)
    pick = jnp.where(src == target, 1.0, 0.0).astype(BF16)
    for copy in copies:
        copy.wait()
    for row in range(TX):
        for place, ref in enumerate((temp, conduct)):
            main[row, DEPTH * place : DEPTH * (place + 1)] = sum(
                jnp.dot(part, pick, preferred_element_type=F32) for part in split3(ref[:, row, :])
            )
    counts[...] = jnp.zeros_like(counts)
    at = lane((8, LANES))
    profile = lax.broadcasted_iota(jnp.int32, (8, LANES), 0)
    for b in range(16):
        cell, which = cells[b], profiles[b]
        row, y = cell // LANES, cell % LANES
        half = y // 2
        column = jnp.where(y % 2 == 0, half + 32, jnp.where(half < 32, half + 96, half - 32))
        hit = (at == column) & (profile == which)
        counts[row] = counts[row] + jnp.where(hit, 1.0, 0.0)
    for row in range(TX):
        main[row, 2 * DEPTH :] = counts[row]
    first = lane((2 * DEPTH + 8, LANES)) % 64 < 32
    for slab in range(TX // 2):
        low, high = roll(main[slab], 64), roll(main[slab + TX // 2], 32)
        to_right[slab] = jnp.where(first, low, high)
        to_left[slab] = jnp.where(first, high, low)


def first_kernel(
    main0,
    main1,
    main2,
    main3,
    strip0,
    strip1,
    strip2,
    strip3,
    table0,
    table1,
    table2,
    lhs,
    c_out,
    v_out,
    cc,
    cond_out,
    init_out,
    plane,
    plane_c,
    init,
    buf_a,
    buf_b,
    cond,
    early,
    early_c,
    pu,
    pe,
    kc,
    node_a,
    node_b,
    sems,
):
    bufs = (init, buf_a, buf_b, buf_a, buf_b)
    planes = (plane, early.at[0], early.at[1])
    planes_c = (plane_c, early_c.at[0], early_c.at[1])
    for ref in (init, buf_a, buf_b, node_a, node_b):
        zero_edges(ref)
    for j in range(5):
        zero_edges(pu.at[j])
    gx = lax.axis_index("gx")
    at = lane((2 * DEPTH + 8, LANES))
    core = lax.bitwise_and(gx, 1)
    rates = [jnp.broadcast_to(t[...], (8, 2 * LANES)) for t in (table0, table2, table1)]
    inside = (at >= 32) & (at < 96)
    first = at % 64 < 32
    has_left, has_right = sides()
    for k, (main, strip) in enumerate(
        ((main0, strip0), (main1, strip1), (main2, strip2), (main3, strip3))
    ):
        base = TX * lax.bitwise_xor(gx, k)

        def assemble(q, main=main, strip=strip, base=base):
            left, right = has_left * strip[q], has_right * strip[4 + q]
            for row, edge in (
                (q, jnp.where(first, left, right)),
                (q + 4, roll(jnp.where(first, right, left), 32)),
            ):
                centre = main[row]
                even = jnp.where(inside, centre, edge)
                odd = roll(jnp.where(inside, edge, centre), 64)
                window = jnp.concatenate([even, odd], axis=1)
                init[base + row + 1] = window[:DEPTH]
                cond[base + row] = LATERAL * window[DEPTH : 2 * DEPTH]
                counts = window[2 * DEPTH :]
                for t in range(3):
                    heat = jnp.sum(counts * rates[t], axis=0, keepdims=True)
                    planes[t][base + row] = jnp.broadcast_to(heat, (8, 2 * LANES))

        loop(TX // 2, assemble, unroll=2)
    copies = [
        pltpu.make_async_copy(cond, cond_out, sems.at[0]),
        pltpu.make_async_copy(init, init_out, sems.at[1]),
    ]
    for copy in copies:
        copy.start()

    def coarsen(row):
        cc[row] = (0.25 * HALF) * pool(cond[2 * row], cond[2 * row + 1])
        for t in range(3):
            planes_c[t][row] = pool(planes[t][2 * row], planes[t][2 * row + 1])

    loop(GX, coarsen, unroll=4)
    prop = lhs[2]
    index = lax.axis_index("tm")

    def one_slice(t):
        sweep(bufs, cond, lhs, lambda m, row: rows8(H[m] * early[t, row]), pu, pe)
        coarse_known(pu, pe, None, cc, early_c.at[t], lhs, kc)
        for pair in range(GX // 2):
            both = apply4(prop, jnp.concatenate([kc[0, 2 * pair], kc[0, 2 * pair + 1]], axis=1))
            node_b[2 * pair + 1] = both[:, :LANES]
            node_b[2 * pair + 2] = both[:, LANES:]
        coarse_step(node_b, node_a, cc, prop, kc.at[1])
        back = 3 + core - 2 * t
        swept = jnp.where(index >= back, 1.0, 0.0).astype(F32)
        begun = jnp.where(index == back - 1, 1.0, 0.0).astype(F32)

        def choose(row):
            node_a[row + 1] = swept * node_a[row + 1] + begun * pu[0, row + 1]

        loop(GX, choose, unroll=8)

        @pl.when(t == 0)
        def _():
            chain_power(node_a, node_b, cc, prop, 2)
            for row in range(GX):
                c_out[row] = node_a[row + 1]

    loop(2, one_slice)
    after1 = is_from(1)
    is0 = 1.0 - after1

    def choose(row):
        node_a[row + 1] = c_out[row] + node_a[row + 1]
        for fine in (2 * row, 2 * row + 1):
            before = buf_b[fine + 1] - twice(pu[4, row + 1])
            here = init[fine + 1] - twice(pu[0, row + 1])
            v_out[fine] = after1 * before + is0 * here

    loop(GX, choose, unroll=4)

    @pl.when(core == 1)
    def _():
        chain_power(node_a, node_b, cc, prop, 1)

    for row in range(GX):
        c_out[row] = node_a[row + 1]
    for copy in copies:
        copy.wait()


def known_kernel(
    init,
    cond,
    plane,
    plane_c,
    cc,
    lhs,
    k0_out,
    kc,
    k0,
    node_1,
    node_2,
    node_3,
    node_4,
    es,
    pu,
    pe,
    olds,
    sems,
):
    bufs = (init, node_1, node_2, node_3, node_4)
    for ref in bufs[1:]:
        zero_edges(ref)
    for j in range(5):
        zero_edges(pu.at[j])
    sweep(bufs, cond, lhs, lambda m, row: rows8(H[m] * plane[row]), pu, pe, None, es)
    coarse_known(pu, pe, None, cc, plane_c, lhs, kc, olds)
    copies = []
    for part in range(4):
        finish_known(bufs, es, olds, plane, lhs[3], k0, part, 4)
        rows = pl.ds(part * (FX // 4), FX // 4)
        copies.append(
            pltpu.make_async_copy(k0.at[:, rows], k0_out.at[:, rows], sems.at[part])
        )
        copies[-1].start()
    for copy in copies:
        copy.wait()


def phase_kernel(steps, parts, kind_in, kind_out, beside, *refs):
    count = takes(kind_in)
    got, refs = refs[:count], refs[count:]
    own, refs = refs[: 2 * beside], refs[2 * beside :]
    c_in, (cc_in, lhs, c_out), refs = refs[:parts], refs[parts : parts + 3], refs[parts + 3 :]
    outs, (node_a, node_b, cc, c_old, sems) = refs[:-5], refs[-5:]
    copy_cc = pltpu.make_async_copy(cc_in, cc, sems.at[0])
    copy_cc.start()
    copies = [
        pltpu.make_async_copy(c_in[k], c_old.at[k], sems.at[1 + k]) for k in range(parts)
    ]
    for copy in copies:
        copy.start()
    zero_edges(node_a)
    zero_edges(node_b)
    receive(kind_in, got, node_a)
    copy_cc.wait()
    chain_power(node_a, node_b, cc, lhs[2], steps)
    here = is_from(steps)
    for copy in copies:
        copy.wait()

    if beside:
        at = lane((DEPTH, LANES))
        has_left, has_right = sides()
        for row in range(GX):
            before = has_left * roll(own[0][row // 4], -32 * (row % 4))
            after = has_right * roll(own[1][row // 4], 96 - 32 * (row % 4))
            c_old[0, row] = jnp.where(at < 32, before, jnp.where(at < 96, c_old[0, row], after))

    def add(row):
        value = c_old[0, row] + here * node_a[row + 1]
        for k in range(1, parts):
            value = value + c_old[k, row]
        c_out[row] = value

    loop(GX, add, unroll=8)
    send(kind_out, c_out, outs)


def join_kernel(first, second, hop):
    base = CXT * lax.axis_index("gx")
    pack_near([first[base + r] + second[base + r] for r in range(CXT)], hop)


def second_kernel(
    steps,
    main_a,
    left_a,
    right_a,
    main_b,
    left_b,
    right_b,
    c_in,
    cc,
    lhs,
    k0_in,
    v_first,
    v_second,
    kc_in,
    cond_in,
    plane_c,
    c_out,
    hop,
    to_right,
    to_left,
    own_right,
    own_left,
    v_tile,
    k0,
    v,
    cond,
    start,
    buf_a,
    buf_b,
    dk,
    pu,
    pe,
    pr,
    kc,
    node_a,
    node_b,
    node_c,
    sems,
):
    copies = [
        pltpu.make_async_copy(src, dst, sems.at[place])
        for place, (src, dst) in enumerate(((v_first, v), (cond_in, cond), (k0_in, k0)))
    ]
    core = lax.bitwise_and(lax.axis_index("gx"), 1)

    @pl.when(core == 0)
    def _():
        copies[0].start()

    @pl.when(core == 1)
    def _():
        pltpu.make_async_copy(v_second, v, sems.at[0]).start()

    for copy in copies[1:]:
        copy.start()
    for ref in (start, buf_a, buf_b, node_a, node_b, node_c):
        zero_edges(ref)
    for j in range(5):
        zero_edges(pu.at[j])
    receive("halves packed", (main_a, left_a, right_a, main_b, left_b, right_b), node_a)
    prop, matrix = lhs[2], lhs[3]
    chain_power(node_a, node_b, cc, prop, steps)
    here = is_from(steps)
    copies[0].wait()

    def add(row):
        value = c_in[row] + here * node_a[row + 1]
        node_a[row + 1] = value
        wide = twice(value)
        start[2 * row + 1] = v[2 * row] + wide
        start[2 * row + 2] = v[2 * row + 1] + wide

    loop(GX, add, unroll=4)

    def spread(row, c, explicit, implicit):
        for m in range(4):
            total = (2.0 * ALPHA[m][c]) * explicit + BETA[m][c] * implicit
            dk[m, row] = total if c == 0 else dk[m, row] + total

    def stage(c, src, dst):
        def body(pair):
            rows = (2 * pair, 2 * pair + 1)
            laps = [coarse_lap(src, row) for row in rows]
            ex = [cc[row] * lap for row, (_, lap) in zip(rows, laps)]
            if c == 0:
                both = apply4(matrix, jnp.concatenate([u for u, _ in laps], axis=1))
                implicit = (both[:, :LANES], both[:, LANES:])
            else:
                implicit = (kc[c - 1, rows[0]], kc[c - 1, rows[1]])
            for place in range(2):
                spread(rows[place], c, ex[place], implicit[place])
            if c < 2:
                rhs = jnp.concatenate(
                    [u + e + kc_in[c, row] for row, (u, _), e in zip(rows, laps, ex)], axis=1
                )
                node = apply4(prop, rhs)
                dst[rows[0] + 1] = node[:, :LANES]
                dst[rows[1] + 1] = node[:, LANES:]
                after = (node - rhs) * (1.0 / HALF)
                kc[c, rows[0]] = after[:, :LANES]
                kc[c, rows[1]] = after[:, LANES:]

        loop(GX // 2, body, unroll=4)

    stage(0, node_a, node_b)
    stage(1, node_b, node_c)
    stage(2, node_c, None)
    copies[1].wait()
    copies[2].wait()

    def known(m, row):
        return k0[m, row] + twice(dk[m, row // 2])

    sweep((start, buf_a, buf_b, buf_a, buf_b), cond, lhs, known, pu, pe, pr)
    coarse_known(pu, pe, pr, cc, plane_c, lhs, kc)
    is0 = 1.0 - is_from(1)

    def begin(row):
        node_a[row + 1] = is0 * pu[0, row + 1]

    loop(GX, begin, unroll=4)
    coarse_step(node_a, node_b, cc, prop, kc.at[0])
    coarse_step(node_b, node_a, cc, prop, kc.at[1])

    def keep(row):
        c_out[row] = node_a[row + 1]

    loop(GX, keep, unroll=4)
    send("halves packed", c_out, (hop, to_right, to_left))
    pack(c_out, 0, GX, None, own_right, own_left)
    base = CXT * lax.axis_index("gx")
    for r in range(CXT):
        for q in range(2):
            fine = 2 * r + q
            v_tile[fine] = buf_b[2 * base + fine + 1] - twice(pu[4, base + r + 1])


def last_kernel(got, c_in, cc, lhs, v_tile, out, node_a, node_b):
    zero_edges(node_a)
    zero_edges(node_b)
    unpack_near(got, 8, node_a, 0)
    base = window_base()
    coarse_step(node_a, node_b, cc, lhs[2], None, 8, base)
    coarse_step(node_b, node_a, cc, lhs[2], None, 8, base)
    here = is_from(1)
    tile = CXT * lax.axis_index("gx")
    src = lax.broadcasted_iota(jnp.int32, (2 * LANES, LANES), 0)
    dst = lane((2 * LANES, LANES))
    target = 32 + dst // 2 + jnp.where(dst % 2 == 1, LANES, 0)
    pick = jnp.where(src == target, 1.0, 0.0).astype(BF16)
    for r in range(CXT):
        wide = twice(c_in[tile + r] + here * node_a[tile - base + r + 1])
        for q in range(2):
            value = v_tile[2 * r + q] + wide
            out[0, :, 2 * r + q, :] = sum(
                jnp.dot(part, pick, preferred_element_type=F32) for part in split3(value)
            )


VMEM = pl.BlockSpec(memory_space=pltpu.VMEM)
SMEM = pl.BlockSpec(memory_space=pltpu.SMEM)
ANY = pl.BlockSpec(memory_space=pl.ANY)
HBM = pl.BlockSpec(memory_space=pltpu.HBM)


def shape(*dims, dtype=F32):
    return jax.ShapeDtypeStruct(dims, dtype)


def call(kernel, name, outs, scratch, *operands, where={}, out_any=(), sems=0, limit=16, flops=10**8):
    spaces = [where.get(index, VMEM) for index in range(len(operands))]
    single = not isinstance(outs, list)
    out_specs = [ANY if index in out_any else VMEM for index in range(1 if single else len(outs))]
    semaphores = [pltpu.SemaphoreType.DMA((sems,))] if sems else []
    return pl.pallas_call(
        kernel,
        name=name,
        out_shape=outs,
        in_specs=spaces,
        out_specs=out_specs[0] if single else out_specs,
        scratch_shapes=[pltpu.VMEM(dims, F32) for dims in scratch] + semaphores,
        compiler_params=pltpu.CompilerParams(vmem_limit_bytes=limit * MIB),
        cost_estimate=pl.CostEstimate(flops=flops, bytes_accessed=10**6, transcendentals=0),
    )(*operands)


COARSE = (GX, DEPTH, LANES)
COARSE_PAD = (GX + 2, DEPTH, LANES)
FINE = (FX, DEPTH, 2 * LANES)
FINE_PAD = (FX + 2, DEPTH, 2 * LANES)


def shift(value, steps, sideways=0):
    slices, columns = lax.axis_size("tm"), lax.axis_size("gy")
    pairs = [
        (s * columns + g, (s + steps) % slices * columns + (g + sideways) % columns)
        for s in range(slices)
        for g in range(columns)
    ]
    return lax.ppermute(value, ("tm", "gy"), pairs)


def swap(value, bit):
    return lax.ppermute(value, "gx", [(g, g ^ bit) for g in range(lax.axis_size("gx"))])


def quads(value):
    far = swap(value, 2)
    return [value, swap(value, 1), far, swap(far, 1)]


def halves(parts):
    return list(parts) + [swap(part, 1) for part in parts]


def fetch_strips(hops, steps):
    main, to_right, to_left = hops
    return [shift(main, steps), shift(to_right, steps, 1), shift(to_left, steps, -1)]


def on_device(initial_temp, conductivity, vert_cond, borehole_cells, borehole_profiles, heat_table):
    slices, rows = lax.axis_size("tm"), lax.axis_size("gx")

    def earlier(back):
        pairs = [
            (t * rows + g, (t + back + g % 2) % slices * rows + g)
            for t in range(slices)
            for g in range(rows)
        ]
        return lax.ppermute(heat_table, ("tm", "gx"), pairs)

    main, to_right, to_left = call(
        prep_kernel,
        "prep",
        [
            shape(TX, 2 * DEPTH + 8, LANES),
            shape(TX // 2, 2 * DEPTH + 8, LANES),
            shape(TX // 2, 2 * DEPTH + 8, LANES),
        ],
        [(TX, 8, LANES), (DEPTH, TX, LANES), (DEPTH, TX, LANES)],
        borehole_cells.reshape(-1),
        borehole_profiles.reshape(-1),
        initial_temp,
        conductivity,
        where={0: SMEM, 1: SMEM, 2: HBM, 3: HBM},
        sems=2,
    )
    beside = swap(main, 1)
    to_right, to_left, beside = lax.optimization_barrier((to_right, to_left, beside))
    far, table1, table2 = lax.optimization_barrier((swap(main, 2), earlier(1), earlier(3)))
    mains = [main, beside, far, swap(far, 1)]
    lhs = call(
        props_kernel,
        "props",
        shape(4, DEPTH, 2 * LANES, dtype=BF16),
        [],
        vert_cond.reshape(1, DEPTH),
    )
    near = (shift(to_right, 0, 1), shift(to_left, 0, -1), lhs)
    from_left, from_right, lhs = lax.optimization_barrier(near)
    strip = jnp.concatenate([from_left, from_right], axis=0)

    c, v, cc, cond, init, plane, plane_c = call(
        first_kernel,
        "early_sweep",
        [
            shape(*COARSE),
            shape(*FINE),
            shape(*COARSE),
            shape(*FINE),
            shape(*FINE_PAD),
            shape(FX, 8, 2 * LANES),
            shape(GX, 8, LANES),
        ],
        [FINE_PAD] * 3
        + [
            FINE,
            (2, FX, 8, 2 * LANES),
            (2, GX, 8, LANES),
            (5, *COARSE_PAD),
            (5, *COARSE),
            (2, *COARSE),
            COARSE_PAD,
            COARSE_PAD,
        ],
        *mains,
        *quads(strip),
        heat_table,
        table1,
        table2,
        lhs,
        out_any=(3, 4),
        sems=2,
        limit=60,
    )
    k0, kc = call(
        known_kernel,
        "own_sweep",
        [shape(4, *FINE), shape(2, *COARSE)],
        [(4, *FINE)] + [FINE_PAD] * 4 + [(5, *FINE), (5, *COARSE_PAD), (5, *COARSE), (6, *COARSE)],
        init,
        cond,
        plane,
        plane_c,
        cc,
        lhs,
        out_any=(0,),
        sems=4,
        limit=60,
        flops=10**10,
    )

    def phase(steps, name, kind_in, kind_out, got, c, own=()):
        kernel = functools.partial(
            phase_kernel, steps, len(c), kind_in, kind_out, len(own) // 2
        )
        outs = [shape(*COARSE)] + outs_of(kind_out)
        scratch = [COARSE_PAD, COARSE_PAD, COARSE, (len(c), *COARSE)]
        got = [*got, *own]
        where = {len(got) + k: HBM for k in range(len(c))}
        where[len(got) + len(c)] = ANY
        c, *hops = call(
            kernel, name, outs, scratch, *got, *c, cc, lhs, where=where, sems=1 + len(c)
        )
        return [c], hops

    c = [c, swap(c, 1)]
    hop = call(join_kernel, "join", shape(3, DEPTH, LANES), [], *c)
    v, hop = lax.optimization_barrier((v, hop))
    v_other = swap(v, 1)
    got, k0, kc = lax.optimization_barrier((shift(hop, 4), k0, kc))
    got = quads(got)
    c, hops = phase(4, "chain_a4", "quads", "halves packed", got, c)
    got = halves(fetch_strips(hops, 8))
    c, *hops, own_right, own_left, v_tile = call(
        functools.partial(second_kernel, 8),
        "second_sweep",
        [shape(*COARSE)]
        + outs_of("halves packed")
        + [shape(4, DEPTH, LANES)] * 2
        + [shape(TX, DEPTH, 2 * LANES)],
        [
            (4, *FINE),
            FINE,
            FINE,
            FINE_PAD,
            FINE_PAD,
            FINE_PAD,
            (4, *COARSE),
            (5, *COARSE_PAD),
            (5, *COARSE),
            (4, *COARSE),
            (2, *COARSE),
            COARSE_PAD,
            COARSE_PAD,
            COARSE_PAD,
        ],
        *got,
        c[0],
        cc,
        lhs,
        k0,
        v,
        v_other,
        kc,
        cond,
        plane_c,
        where={9: ANY, 10: ANY, 11: ANY, 13: ANY},
        sems=3,
        limit=42,
    )
    got = halves(fetch_strips(hops, 8))
    own = (shift(own_right, 0, 1), shift(own_left, 0, -1))
    c, hops = phase(8, "chain_b8", "halves packed", "quads", got, [c], own)
    got = quads(shift(hops[0], 4))
    c, hops = phase(4, "chain_b4", "quads", "quads", got, c)
    got = quads(shift(hops[0], 2))
    c, hops = phase(2, "chain_b2", "quads", "window", got, c)
    got = shift(hops[0], 1)
    return call(
        last_kernel,
        "finish",
        shape(1, DEPTH, TX, LANES),
        [(10, DEPTH, LANES)] * 2,
        got,
        c[0],
        cc,
        lhs,
        v_tile,
    )


def solution(mesh):
    placed = (
        P(None, "gx", "gy"),
        P(None, "gx", "gy"),
        P(),
        P("gx", "gy", None),
        P("gx", "gy", None),
        P(None, "tm"),
    )
    return jax.shard_map(
        on_device, mesh=mesh, in_specs=placed, out_specs=P("tm", None, "gx", "gy"), check_vma=False
    )
```

```python
import functools
import math

import jax
import jax.numpy as jnp
from jax import lax
from jax.experimental import pallas as pl
from jax.experimental.pallas import tpu as pltpu
from jax.sharding import PartitionSpec as P

F32 = jnp.float32
BF16 = jnp.bfloat16
LATERAL = 0.3
VERTICAL = 4.0
FINE_NODES = [0.0, (1.0 - math.sqrt(3.0 / 7.0)) / 2.0, 0.5, (1.0 + math.sqrt(3.0 / 7.0)) / 2.0, 1.0]
COARSE_NODES = [0.0, 0.5, 1.0]
HALF = 0.5
DEPTH = 64
TX = 8
CXT = 4
FX = 32
GX = 16
LANES = 128
MIB = 2**20


def basis_coeffs(times_list, basis_index):
    coeffs = [1.0]
    denominator = 1.0
    for other_index in range(len(times_list)):
        if other_index != basis_index:
            other_time = times_list[other_index]
            widened = [0.0] * (len(coeffs) + 1)
            for power in range(len(coeffs)):
                widened[power + 1] = widened[power + 1] + coeffs[power]
                widened[power] = widened[power] - other_time * coeffs[power]
            coeffs = widened
            denominator = denominator * (times_list[basis_index] - other_time)
    return [entry / denominator for entry in coeffs]


def poly_value(coeffs, point):
    return sum(coeffs[power] * point**power for power in range(len(coeffs)))


def poly_integral(coeffs, lower, upper):
    return sum(
        coeffs[power] * (upper ** (power + 1) - lower ** (power + 1)) / (power + 1)
        for power in range(len(coeffs))
    )


H = [FINE_NODES[m + 1] - FINE_NODES[m] for m in range(4)]
S = [
    [poly_integral(basis_coeffs(FINE_NODES, j), FINE_NODES[m], FINE_NODES[m + 1]) for j in range(5)]
    for m in range(4)
]
W = [[poly_value(basis_coeffs(COARSE_NODES, c), t) for c in range(3)] for t in FINE_NODES]
SC = [[S[2 * m][j] + S[2 * m + 1][j] for j in range(5)] for m in range(2)]
SW = [[sum(S[m][j] * W[j][c] for j in range(5)) for c in range(3)] for m in range(4)]
ALPHA = [[SW[m][c] - H[m] * W[m][c] for c in range(3)] for m in range(4)]
BETA = [[SW[m][c] - H[m] * W[m + 1][c] for c in range(3)] for m in range(4)]


def loop(count, body, unroll=1):
    def step(index, carry):
        body(index)
        return carry

    lax.fori_loop(0, count, step, 0, unroll=unroll)


def roll(value, shift):
    return pltpu.roll(value, shift % value.shape[-1], value.ndim - 1)


def lane(shape):
    return lax.broadcasted_iota(jnp.int32, shape, len(shape) - 1)


def apply4(lhs, value):
    high = value.astype(BF16)
    low = (value - high.astype(F32)).astype(BF16)
    stacked = jnp.concatenate([high, low, high, low], axis=0)
    return jnp.dot(lhs, stacked, preferred_element_type=F32)


def split3(value):
    high = value.astype(BF16)
    rest = value - high.astype(F32)
    mid = rest.astype(BF16)
    low = (rest - mid.astype(F32)).astype(BF16)
    return high, mid, low


def fine_lap(src, row):
    u = src[row + 1]
    even, odd = u[:, :LANES], u[:, LANES:]
    beside = jnp.concatenate([odd + roll(odd, 1), even + roll(even, -1)], axis=1)
    return u, (src[row] + src[row + 2]) + beside - 4.0 * u


def coarse_lap(src, row):
    u = src[row + 1]
    return u, (src[row] + src[row + 2]) + (roll(u, 1) + roll(u, -1)) - 4.0 * u


def pool(first, second):
    total = first + second
    return 0.25 * (total[:, :LANES] + total[:, LANES:])


def twice(value):
    return jnp.concatenate([value, value], axis=1)


def rows8(value):
    return jnp.concatenate([value] * (DEPTH // 8), axis=0)


def zero_edges(ref):
    edge = jnp.zeros(ref.shape[1:], F32)
    ref[0] = edge
    ref[ref.shape[0] - 1] = edge


def coarse_step(src, dst, cc, prop, known=None, count=GX, base=0):
    for pair in range(count // 2):
        parts = []
        for row in (2 * pair, 2 * pair + 1):
            u, lap = coarse_lap(src, row)
            rhs = u + cc[base + row] * lap
            parts.append(rhs if known is None else rhs + known[row])
        node = apply4(prop, jnp.concatenate(parts, axis=1))
        dst[2 * pair + 1] = node[:, :LANES]
        dst[2 * pair + 2] = node[:, LANES:]


def chain_power(first, second, cc, prop, steps, count=GX, base=0):
    each = min(steps, 4)

    def body(_):
        for _ in range(each):
            coarse_step(first, second, cc, prop, None, count, base)
            coarse_step(second, first, cc, prop, None, count, base)

    if steps == each:
        body(0)
    else:
        loop(steps // each, body)


def sweep(bufs, cond, lhs, known, pu, pe, pr=None, es=None):
    for m in range(4):
        src, dst = bufs[m], bufs[m + 1]
        prop = lhs[0] if m in (0, 3) else lhs[1]

        def body(pair, m=m, src=src, dst=dst, prop=prop):
            us, ex, rs = [], [], []
            for row in (2 * pair, 2 * pair + 1):
                u, lap = fine_lap(src, row)
                e = cond[row] * lap
                rhs = u + H[m] * e + known(m, row)
                dst[row + 1] = apply4(prop, rhs)
                if es is not None:
                    es[m, row] = e
                us.append(u)
                ex.append(e)
                rs.append(rhs)
            pu[m, pair + 1] = pool(*us)
            pe[m, pair] = pool(*ex)
            if pr is not None:
                pr[m, pair] = pool(*rs)

        loop(GX, body, unroll=8)

    def last(pair):
        us, ex = [], []
        for row in (2 * pair, 2 * pair + 1):
            u, lap = fine_lap(bufs[4], row)
            e = cond[row] * lap
            if es is not None:
                es[4, row] = e
            us.append(u)
            ex.append(e)
        pu[4, pair + 1] = pool(*us)
        pe[4, pair] = pool(*ex)

    loop(GX, last, unroll=8)


def coarse_known(pu, pe, pr, cc, plane, lhs, kc, olds=None):
    matrix = lhs[3]

    def body(pair):
        rows = (2 * pair, 2 * pair + 1)
        ic, ec = [], []
        for c in range(3):
            laps = [coarse_lap(pu.at[2 * c], row) for row in rows]
            ec.append([cc[row] * lap for row, (_, lap) in zip(rows, laps)])
            both = apply4(matrix, jnp.concatenate([u for u, _ in laps], axis=1))
            ic.append([both[:, :LANES], both[:, LANES:]])
        for place, row in enumerate(rows):
            flat = rows8(plane[row])
            u = [pu[j, row + 1] for j in range(5)]
            e = [pe[j, row] for j in range(5)]
            total = [e[0] + ic[0][place]]
            for m in range(4):
                if pr is None:
                    im = (u[m + 1] - u[m]) * (1.0 / H[m]) - (e[m] + flat)
                else:
                    im = (u[m + 1] - pr[m, row]) * (1.0 / H[m])
                total.append(e[m + 1] + im)
            for k in range(2):
                value = HALF * (flat - ic[k + 1][place]) - ec[k][place]
                for j in range(5):
                    value = value + SC[k][j] * total[j]
                kc[k, row] = value
            if olds is not None:
                for c in range(3):
                    olds[c, row] = 2.0 * ec[c][place]
                    olds[3 + c, row] = ic[c][place]

    loop(GX // 2, body, unroll=4)


def finish_known(bufs, es, olds, plane, matrix, k0, part, parts):
    count = GX // parts

    def body(index):
        pair = part * count + index
        wide = []
        for m in range(4):
            total = ALPHA[m][0] * olds[0, pair] + BETA[m][0] * olds[3, pair]
            for c in (1, 2):
                total = total + ALPHA[m][c] * olds[c, pair] + BETA[m][c] * olds[3 + c, pair]
            wide.append(twice(total))
        for row in (2 * pair, 2 * pair + 1):
            flat = rows8(plane[row])
            u = [buf[row + 1] for buf in bufs]
            e = [es[j, row] for j in range(5)]
            total = [e[0] + apply4(matrix, u[0])]
            change = [u[m + 1] - u[m] for m in range(4)]
            for m in range(4):
                total.append(e[m + 1] + (change[m] * (1.0 / H[m]) - (e[m] + flat)))
            sums = [total[0] + total[4], total[1] + total[3], total[2]]
            gaps = [total[0] - total[4], total[1] - total[3]]
            for m in range(2):
                even = sum(0.5 * (S[m][j] + S[m][4 - j]) * sums[j] for j in range(2))
                even = even + S[m][2] * sums[2] + (2.0 * H[m]) * flat
                odd = sum(0.5 * (S[m][j] - S[m][4 - j]) * gaps[j] for j in range(2))
                k0[m, row] = (even + odd) - (change[m] + wide[m])
                k0[3 - m, row] = (even - odd) - (change[3 - m] + wide[3 - m])

    loop(count, body, unroll=4)


def pack(c_ref, base, count, main, to_right, to_left):
    at = lane((DEPTH, LANES))
    for quad in range(count // 4):
        rows = [c_ref[base + 4 * quad + r] for r in range(4)]
        for half in range(2 if main is not None else 0):
            main[2 * quad + half] = jnp.where(
                at < 64, roll(rows[2 * half], -32), roll(rows[2 * half + 1], 32)
            )
        for out, start in ((to_right, 64), (to_left, 32)):
            value = roll(rows[0], -start)
            for r in range(1, 4):
                value = jnp.where(at < 32 * r, value, roll(rows[r], 32 * r - start))
            out[quad] = value


def sides():
    gy = lax.axis_index("gy")
    last = lax.axis_size("gy") - 1
    return jnp.where(gy > 0, 1.0, 0.0).astype(F32), jnp.where(gy < last, 1.0, 0.0).astype(F32)


def unpack(main, left, right, count, dst, base):
    at = lane((DEPTH, LANES))
    has_left, has_right = sides()
    for quad in range(count // 4):
        for r in range(4):
            centre = roll(main[2 * quad + r // 2], 32 if r % 2 == 0 else -32)
            before = has_left * roll(left[quad], -32 * r)
            after = has_right * roll(right[quad], 96 - 32 * r)
            value = jnp.where(at < 32, before, jnp.where(at < 96, centre, after))
            dst[base + 4 * quad + r + 1] = value


def pack_near(rows, out, width):
    at = lane((DEPTH, LANES))
    count, per = len(rows), 64 // width
    for half in range(count // 2):
        out[half] = jnp.where(at < 64, roll(rows[2 * half], -32), roll(rows[2 * half + 1], 32))
    for slab in range(count // per):
        edges = None
        for r in range(per):
            begin, row = 2 * width * r, rows[per * slab + r]
            before = roll(row, begin - (32 - width))
            after = roll(row, begin + width - 96)
            both = jnp.where(at < begin + width, before, after)
            edges = both if edges is None else jnp.where(at < begin, edges, both)
        out[count // 2 + slab] = edges


def unpack_near(slabs, count, width, dst, base):
    at = lane((DEPTH, LANES))
    per = 64 // width
    filled = (at >= 32 - width) & (at < 96 + width)
    for r in range(count):
        edges = slabs[count // 2 + r // per]
        begin = 2 * width * (r % per)
        centre = roll(slabs[r // 2], 32 if r % 2 == 0 else -32)
        before = roll(edges, 32 - width - begin)
        after = roll(edges, 96 - width - begin)
        value = jnp.where(at < 32, before, jnp.where(at < 96, centre, after))
        dst[base + r + 1] = jnp.where(filled, value, 0.0)


NEAR = {"halves 8": 8, "halves 16": 16}


def receive(kind, got, dst):
    gx = lax.axis_index("gx")
    if kind == "quads":
        for k, rows in zip((0, 1, 2, 3), got):
            unpack_near(rows, CXT, 16, dst, CXT * lax.bitwise_xor(gx, k))
    elif kind in NEAR:
        core = lax.bitwise_and(gx, 1)
        for k in range(2):
            unpack_near(got[k], 8, NEAR[kind], dst, 8 * lax.bitwise_xor(core, k))
    else:
        core = lax.bitwise_and(gx, 1)
        for k in range(2):
            unpack(*got[3 * k : 3 * k + 3], 8, dst, 8 * lax.bitwise_xor(core, k))


def window_base():
    return jnp.clip(CXT * lax.axis_index("gx") - 2, 0, 8)


def send(kind, c_ref, outs):
    gx = lax.axis_index("gx")
    if kind == "quads":
        pack_near([c_ref[CXT * gx + r] for r in range(CXT)], outs[0], 16)
    elif kind in NEAR:
        base = 8 * lax.bitwise_and(gx, 1)
        pack_near([c_ref[base + r] for r in range(8)], outs[0], NEAR[kind])
    elif kind == "halves packed":
        pack(c_ref, 8 * lax.bitwise_and(gx, 1), 8, *outs)
    else:
        base = window_base()
        pack_near([c_ref[base + r] for r in range(8)], outs[0], 8)


def outs_of(kind):
    if kind == "quads":
        return [shape(3, DEPTH, LANES)]
    if kind in NEAR:
        return [shape(4 + NEAR[kind] // 8, DEPTH, LANES)]
    if kind == "window":
        return [shape(5, DEPTH, LANES)]
    return [shape(4, DEPTH, LANES)] + [shape(2, DEPTH, LANES)] * 2


def takes(kind):
    return {"quads": 4, "halves packed": 6, "halves 8": 2, "halves 16": 2}[kind]


def is_from(steps):
    return jnp.where(lax.axis_index("tm") >= steps, 1.0, 0.0).astype(F32)


def props_kernel(faces_ref, out_ref):
    shape = (DEPTH, DEPTH)
    faces = jnp.broadcast_to(faces_ref[...], shape)
    row = lax.broadcasted_iota(jnp.int32, shape, 0)
    col = lane(shape)
    shape = (DEPTH, LANES)
    upper = jnp.sum(jnp.where(row == col, faces, 0.0), axis=1, keepdims=True)
    lower = jnp.sum(jnp.where(row + 1 == col, faces, 0.0), axis=1, keepdims=True)
    upper, lower = jnp.broadcast_to(upper, shape), jnp.broadcast_to(lower, shape)
    row = lax.broadcasted_iota(jnp.int32, shape, 0)
    col = lane(shape)
    level = jnp.where(col < DEPTH, col, col - DEPTH)
    eye = jnp.where(row == level, 1.0, 0.0).astype(F32)

    def shifted(value, step):
        return pltpu.roll(value, step % DEPTH, 0)

    def inverse(length):
        a = -VERTICAL * length * jnp.where(row == 0, 0.0, upper)
        c = -VERTICAL * length * lower
        b = 1.0 + VERTICAL * length * (upper + lower)
        r = eye
        step = 1
        while step < DEPTH:
            alpha = -a / shifted(b, step)
            gamma = -c / shifted(b, -step)
            b, r, a, c = (
                b + alpha * shifted(c, step) + gamma * shifted(a, -step),
                r + alpha * shifted(r, step) + gamma * shifted(r, -step),
                alpha * shifted(a, step),
                gamma * shifted(c, -step),
            )
            step *= 2
        return r / b

    def store(index, value):
        high = value.astype(BF16)
        out_ref[index, :, :LANES] = high
        out_ref[index, :, LANES:] = (value - high.astype(F32)).astype(BF16)

    fine = inverse(jnp.where(col < DEPTH, H[0], H[1]).astype(F32))
    other = roll(fine, DEPTH)
    store(0, jnp.where(col < DEPTH, fine, other))
    store(1, jnp.where(col < DEPTH, other, fine))
    store(2, inverse(jnp.full(shape, HALF, F32)))
    matrix = jnp.where(row == level, -VERTICAL * (upper + lower), 0.0)
    matrix = matrix + jnp.where(level == row - 1, VERTICAL * upper, 0.0)
    matrix = matrix + jnp.where(level == row + 1, VERTICAL * lower, 0.0)
    store(3, matrix)


def prep_kernel(
    cells, profiles, temp_in, conduct_in, main, to_right, to_left, counts, temp, conduct, sems
):
    copies = [
        pltpu.make_async_copy(temp_in, temp, sems.at[0]),
        pltpu.make_async_copy(conduct_in, conduct, sems.at[1]),
    ]
    for copy in copies:
        copy.start()
    src = lax.broadcasted_iota(jnp.int32, (LANES, LANES), 0)
    dst = lane((LANES, LANES))
    odd = 2 * jnp.where(dst < 32, dst + 32, dst - 96) + 1
    target = jnp.where((dst >= 32) & (dst < 96), 2 * (dst - 32), odd)
    pick = jnp.where(src == target, 1.0, 0.0).astype(BF16)
    for copy in copies:
        copy.wait()
    for row in range(TX):
        for place, ref in enumerate((temp, conduct)):
            main[row, DEPTH * place : DEPTH * (place + 1)] = sum(
                jnp.dot(part, pick, preferred_element_type=F32) for part in split3(ref[:, row, :])
            )
    counts[...] = jnp.zeros_like(counts)
    at = lane((8, LANES))
    profile = lax.broadcasted_iota(jnp.int32, (8, LANES), 0)
    for b in range(16):
        cell, which = cells[b], profiles[b]
        row, y = cell // LANES, cell % LANES
        half = y // 2
        column = jnp.where(y % 2 == 0, half + 32, jnp.where(half < 32, half + 96, half - 32))
        hit = (at == column) & (profile == which)
        counts[row] = counts[row] + jnp.where(hit, 1.0, 0.0)
    for row in range(TX):
        main[row, 2 * DEPTH :] = counts[row]
    first = lane((2 * DEPTH + 8, LANES)) % 64 < 32
    for slab in range(TX // 2):
        low, high = roll(main[slab], 64), roll(main[slab + TX // 2], 32)
        to_right[slab] = jnp.where(first, low, high)
        to_left[slab] = jnp.where(first, high, low)


def first_kernel(
    main0,
    main1,
    main2,
    main3,
    strip0,
    strip1,
    strip2,
    strip3,
    table0,
    table1,
    table2,
    lhs,
    c_out,
    v_out,
    cc,
    cond_out,
    init_out,
    plane,
    plane_c,
    init,
    buf_a,
    buf_b,
    cond,
    early,
    early_c,
    pu,
    pe,
    kc,
    node_a,
    node_b,
    sems,
):
    bufs = (init, buf_a, buf_b, buf_a, buf_b)
    planes = (plane, early.at[0], early.at[1])
    planes_c = (plane_c, early_c.at[0], early_c.at[1])
    for ref in (init, buf_a, buf_b, node_a, node_b):
        zero_edges(ref)
    for j in range(5):
        zero_edges(pu.at[j])
    gx = lax.axis_index("gx")
    at = lane((2 * DEPTH + 8, LANES))
    core = lax.bitwise_and(gx, 1)
    rates = [jnp.broadcast_to(t[...], (8, 2 * LANES)) for t in (table0, table2, table1)]
    inside = (at >= 32) & (at < 96)
    first = at % 64 < 32
    has_left, has_right = sides()
    for k, (main, strip) in enumerate(
        ((main0, strip0), (main1, strip1), (main2, strip2), (main3, strip3))
    ):
        base = TX * lax.bitwise_xor(gx, k)

        def assemble(q, main=main, strip=strip, base=base):
            left, right = has_left * strip[q], has_right * strip[4 + q]
            for row, edge in (
                (q, jnp.where(first, left, right)),
                (q + 4, roll(jnp.where(first, right, left), 32)),
            ):
                centre = main[row]
                even = jnp.where(inside, centre, edge)
                odd = roll(jnp.where(inside, edge, centre), 64)
                window = jnp.concatenate([even, odd], axis=1)
                init[base + row + 1] = window[:DEPTH]
                cond[base + row] = LATERAL * window[DEPTH : 2 * DEPTH]
                counts = window[2 * DEPTH :]
                for t in range(3):
                    heat = jnp.sum(counts * rates[t], axis=0, keepdims=True)
                    planes[t][base + row] = jnp.broadcast_to(heat, (8, 2 * LANES))

        loop(TX // 2, assemble, unroll=2)
    copies = [
        pltpu.make_async_copy(cond, cond_out, sems.at[0]),
        pltpu.make_async_copy(init, init_out, sems.at[1]),
    ]
    for copy in copies:
        copy.start()

    def coarsen(row):
        cc[row] = (0.25 * HALF) * pool(cond[2 * row], cond[2 * row + 1])
        for t in range(3):
            planes_c[t][row] = pool(planes[t][2 * row], planes[t][2 * row + 1])

    loop(GX, coarsen, unroll=4)
    prop = lhs[2]
    index = lax.axis_index("tm")

    def one_slice(t):
        sweep(bufs, cond, lhs, lambda m, row: rows8(H[m] * early[t, row]), pu, pe)
        coarse_known(pu, pe, None, cc, early_c.at[t], lhs, kc)
        for pair in range(GX // 2):
            both = apply4(prop, jnp.concatenate([kc[0, 2 * pair], kc[0, 2 * pair + 1]], axis=1))
            node_b[2 * pair + 1] = both[:, :LANES]
            node_b[2 * pair + 2] = both[:, LANES:]
        coarse_step(node_b, node_a, cc, prop, kc.at[1])
        back = 3 + core - 2 * t
        swept = jnp.where(index >= back, 1.0, 0.0).astype(F32)
        begun = jnp.where(index == back - 1, 1.0, 0.0).astype(F32)

        def choose(row):
            node_a[row + 1] = swept * node_a[row + 1] + begun * pu[0, row + 1]

        loop(GX, choose, unroll=8)

        @pl.when(t == 0)
        def _():
            chain_power(node_a, node_b, cc, prop, 2)
            for row in range(GX):
                c_out[row] = node_a[row + 1]

    loop(2, one_slice)
    after1 = is_from(1)
    is0 = 1.0 - after1

    def choose(row):
        node_a[row + 1] = c_out[row] + node_a[row + 1]
        for fine in (2 * row, 2 * row + 1):
            before = buf_b[fine + 1] - twice(pu[4, row + 1])
            here = init[fine + 1] - twice(pu[0, row + 1])
            v_out[fine] = after1 * before + is0 * here

    loop(GX, choose, unroll=4)

    @pl.when(core == 1)
    def _():
        chain_power(node_a, node_b, cc, prop, 1)

    for row in range(GX):
        c_out[row] = node_a[row + 1]
    for copy in copies:
        copy.wait()


def known_kernel(
    init,
    cond,
    plane,
    plane_c,
    cc,
    lhs,
    k0_out,
    kc,
    k0,
    node_1,
    node_2,
    node_3,
    node_4,
    es,
    pu,
    pe,
    olds,
    sems,
):
    bufs = (init, node_1, node_2, node_3, node_4)
    for ref in bufs[1:]:
        zero_edges(ref)
    for j in range(5):
        zero_edges(pu.at[j])
    sweep(bufs, cond, lhs, lambda m, row: rows8(H[m] * plane[row]), pu, pe, None, es)
    coarse_known(pu, pe, None, cc, plane_c, lhs, kc, olds)
    copies = []
    for part in range(4):
        finish_known(bufs, es, olds, plane, lhs[3], k0, part, 4)
        rows = pl.ds(part * (FX // 4), FX // 4)
        copies.append(
            pltpu.make_async_copy(k0.at[:, rows], k0_out.at[:, rows], sems.at[part])
        )
        copies[-1].start()
    for copy in copies:
        copy.wait()


def phase_kernel(steps, parts, kind_in, kind_out, beside, *refs):
    count = takes(kind_in)
    got, refs = refs[:count], refs[count:]
    own, refs = refs[: 2 * beside], refs[2 * beside :]
    c_in, (cc_in, lhs, c_out), refs = refs[:parts], refs[parts : parts + 3], refs[parts + 3 :]
    outs, (node_a, node_b, cc, c_old, sems) = refs[:-5], refs[-5:]
    copy_cc = pltpu.make_async_copy(cc_in, cc, sems.at[0])
    copy_cc.start()
    copies = [
        pltpu.make_async_copy(c_in[k], c_old.at[k], sems.at[1 + k]) for k in range(parts)
    ]
    for copy in copies:
        copy.start()
    zero_edges(node_a)
    zero_edges(node_b)
    receive(kind_in, got, node_a)
    copy_cc.wait()
    chain_power(node_a, node_b, cc, lhs[2], steps)
    here = is_from(steps)
    for copy in copies:
        copy.wait()

    if beside:
        at = lane((DEPTH, LANES))
        has_left, has_right = sides()
        for row in range(GX):
            before = has_left * roll(own[0][row // 4], -32 * (row % 4))
            after = has_right * roll(own[1][row // 4], 96 - 32 * (row % 4))
            c_old[0, row] = jnp.where(at < 32, before, jnp.where(at < 96, c_old[0, row], after))

    def add(row):
        value = c_old[0, row] + here * node_a[row + 1]
        for k in range(1, parts):
            value = value + c_old[k, row]
        c_out[row] = value

    loop(GX, add, unroll=8)
    send(kind_out, c_out, outs)


def join_kernel(first, second, hop):
    base = 8 * lax.bitwise_and(lax.axis_index("gx"), 1)
    pack_near([first[base + r] + second[base + r] for r in range(8)], hop, 16)


def second_kernel(
    steps,
    main_a,
    left_a,
    right_a,
    main_b,
    left_b,
    right_b,
    c_in,
    cc,
    lhs,
    k0_in,
    v_first,
    v_second,
    kc_in,
    cond_in,
    plane_c,
    c_out,
    hop,
    to_right,
    to_left,
    own_right,
    own_left,
    v_tile,
    k0,
    v,
    cond,
    start,
    buf_a,
    buf_b,
    dk,
    pu,
    pe,
    pr,
    kc,
    node_a,
    node_b,
    node_c,
    sems,
):
    copies = [
        pltpu.make_async_copy(src, dst, sems.at[place])
        for place, (src, dst) in enumerate(((v_first, v), (cond_in, cond), (k0_in, k0)))
    ]
    core = lax.bitwise_and(lax.axis_index("gx"), 1)

    @pl.when(core == 0)
    def _():
        copies[0].start()

    @pl.when(core == 1)
    def _():
        pltpu.make_async_copy(v_second, v, sems.at[0]).start()

    for copy in copies[1:]:
        copy.start()
    for ref in (start, buf_a, buf_b, node_a, node_b, node_c):
        zero_edges(ref)
    for j in range(5):
        zero_edges(pu.at[j])
    receive("halves packed", (main_a, left_a, right_a, main_b, left_b, right_b), node_a)
    prop, matrix = lhs[2], lhs[3]
    chain_power(node_a, node_b, cc, prop, steps)
    here = is_from(steps)
    copies[0].wait()

    def add(row):
        value = c_in[row] + here * node_a[row + 1]
        node_a[row + 1] = value
        wide = twice(value)
        start[2 * row + 1] = v[2 * row] + wide
        start[2 * row + 2] = v[2 * row + 1] + wide

    loop(GX, add, unroll=4)

    def spread(row, c, explicit, implicit):
        for m in range(4):
            total = (2.0 * ALPHA[m][c]) * explicit + BETA[m][c] * implicit
            dk[m, row] = total if c == 0 else dk[m, row] + total

    def stage(c, src, dst):
        def body(pair):
            rows = (2 * pair, 2 * pair + 1)
            laps = [coarse_lap(src, row) for row in rows]
            ex = [cc[row] * lap for row, (_, lap) in zip(rows, laps)]
            if c == 0:
                both = apply4(matrix, jnp.concatenate([u for u, _ in laps], axis=1))
                implicit = (both[:, :LANES], both[:, LANES:])
            else:
                implicit = (kc[c - 1, rows[0]], kc[c - 1, rows[1]])
            for place in range(2):
                spread(rows[place], c, ex[place], implicit[place])
            if c < 2:
                rhs = jnp.concatenate(
                    [u + e + kc_in[c, row] for row, (u, _), e in zip(rows, laps, ex)], axis=1
                )
                node = apply4(prop, rhs)
                dst[rows[0] + 1] = node[:, :LANES]
                dst[rows[1] + 1] = node[:, LANES:]
                after = (node - rhs) * (1.0 / HALF)
                kc[c, rows[0]] = after[:, :LANES]
                kc[c, rows[1]] = after[:, LANES:]

        loop(GX // 2, body, unroll=4)

    stage(0, node_a, node_b)
    stage(1, node_b, node_c)
    stage(2, node_c, None)
    copies[1].wait()
    copies[2].wait()

    def known(m, row):
        return k0[m, row] + twice(dk[m, row // 2])

    sweep((start, buf_a, buf_b, buf_a, buf_b), cond, lhs, known, pu, pe, pr)
    coarse_known(pu, pe, pr, cc, plane_c, lhs, kc)
    is0 = 1.0 - is_from(1)

    def begin(row):
        node_a[row + 1] = is0 * pu[0, row + 1]

    loop(GX, begin, unroll=4)
    coarse_step(node_a, node_b, cc, prop, kc.at[0])
    coarse_step(node_b, node_a, cc, prop, kc.at[1])

    def keep(row):
        c_out[row] = node_a[row + 1]

    loop(GX, keep, unroll=4)
    send("halves packed", c_out, (hop, to_right, to_left))
    pack(c_out, 0, GX, None, own_right, own_left)
    base = CXT * lax.axis_index("gx")
    for r in range(CXT):
        for q in range(2):
            fine = 2 * r + q
            v_tile[fine] = buf_b[2 * base + fine + 1] - twice(pu[4, base + r + 1])


def last_kernel(got, c_in, cc, lhs, v_tile, out, node_a, node_b):
    zero_edges(node_a)
    zero_edges(node_b)
    unpack_near(got, 8, 8, node_a, 0)
    base = window_base()
    coarse_step(node_a, node_b, cc, lhs[2], None, 8, base)
    coarse_step(node_b, node_a, cc, lhs[2], None, 8, base)
    here = is_from(1)
    tile = CXT * lax.axis_index("gx")
    src = lax.broadcasted_iota(jnp.int32, (2 * LANES, LANES), 0)
    dst = lane((2 * LANES, LANES))
    target = 32 + dst // 2 + jnp.where(dst % 2 == 1, LANES, 0)
    pick = jnp.where(src == target, 1.0, 0.0).astype(BF16)
    for r in range(CXT):
        wide = twice(c_in[tile + r] + here * node_a[tile - base + r + 1])
        for q in range(2):
            value = v_tile[2 * r + q] + wide
            out[0, :, 2 * r + q, :] = sum(
                jnp.dot(part, pick, preferred_element_type=F32) for part in split3(value)
            )


VMEM = pl.BlockSpec(memory_space=pltpu.VMEM)
SMEM = pl.BlockSpec(memory_space=pltpu.SMEM)
ANY = pl.BlockSpec(memory_space=pl.ANY)
HBM = pl.BlockSpec(memory_space=pltpu.HBM)


def shape(*dims, dtype=F32):
    return jax.ShapeDtypeStruct(dims, dtype)


def call(kernel, name, outs, scratch, *operands, where={}, out_any=(), sems=0, limit=16, flops=10**8):
    spaces = [where.get(index, VMEM) for index in range(len(operands))]
    single = not isinstance(outs, list)
    out_specs = [ANY if index in out_any else VMEM for index in range(1 if single else len(outs))]
    semaphores = [pltpu.SemaphoreType.DMA((sems,))] if sems else []
    return pl.pallas_call(
        kernel,
        name=name,
        out_shape=outs,
        in_specs=spaces,
        out_specs=out_specs[0] if single else out_specs,
        scratch_shapes=[pltpu.VMEM(dims, F32) for dims in scratch] + semaphores,
        compiler_params=pltpu.CompilerParams(vmem_limit_bytes=limit * MIB),
        cost_estimate=pl.CostEstimate(flops=flops, bytes_accessed=10**6, transcendentals=0),
    )(*operands)


COARSE = (GX, DEPTH, LANES)
COARSE_PAD = (GX + 2, DEPTH, LANES)
FINE = (FX, DEPTH, 2 * LANES)
FINE_PAD = (FX + 2, DEPTH, 2 * LANES)


def shift(value, steps, sideways=0):
    slices, columns = lax.axis_size("tm"), lax.axis_size("gy")
    pairs = [
        (s * columns + g, (s + steps) % slices * columns + (g + sideways) % columns)
        for s in range(slices)
        for g in range(columns)
    ]
    return lax.ppermute(value, ("tm", "gy"), pairs)


def swap(value, bit):
    return lax.ppermute(value, "gx", [(g, g ^ bit) for g in range(lax.axis_size("gx"))])


def quads(value):
    far = swap(value, 2)
    return [value, swap(value, 1), far, swap(far, 1)]


def halves(parts):
    return list(parts) + [swap(part, 1) for part in parts]


def fetch_strips(hops, steps):
    main, to_right, to_left = hops
    return [shift(main, steps), shift(to_right, steps, 1), shift(to_left, steps, -1)]


def on_device(initial_temp, conductivity, vert_cond, borehole_cells, borehole_profiles, heat_table):
    slices, rows = lax.axis_size("tm"), lax.axis_size("gx")

    def earlier(back):
        pairs = [
            (t * rows + g, (t + back + g % 2) % slices * rows + g)
            for t in range(slices)
            for g in range(rows)
        ]
        return lax.ppermute(heat_table, ("tm", "gx"), pairs)

    main, to_right, to_left = call(
        prep_kernel,
        "prep",
        [
            shape(TX, 2 * DEPTH + 8, LANES),
            shape(TX // 2, 2 * DEPTH + 8, LANES),
            shape(TX // 2, 2 * DEPTH + 8, LANES),
        ],
        [(TX, 8, LANES), (DEPTH, TX, LANES), (DEPTH, TX, LANES)],
        borehole_cells.reshape(-1),
        borehole_profiles.reshape(-1),
        initial_temp,
        conductivity,
        where={0: SMEM, 1: SMEM, 2: HBM, 3: HBM},
        sems=2,
        limit=60,
    )
    beside = swap(main, 1)
    to_right, to_left, beside = lax.optimization_barrier((to_right, to_left, beside))
    far, table1, table2 = lax.optimization_barrier((swap(main, 2), earlier(1), earlier(3)))
    mains = [main, beside, far, swap(far, 1)]
    lhs = call(
        props_kernel,
        "props",
        shape(4, DEPTH, 2 * LANES, dtype=BF16),
        [],
        vert_cond.reshape(1, DEPTH),
    )
    near = (shift(to_right, 0, 1), shift(to_left, 0, -1), lhs)
    from_left, from_right, lhs = lax.optimization_barrier(near)
    strip = jnp.concatenate([from_left, from_right], axis=0)

    c, v, cc, cond, init, plane, plane_c = call(
        first_kernel,
        "early_sweep",
        [
            shape(*COARSE),
            shape(*FINE),
            shape(*COARSE),
            shape(*FINE),
            shape(*FINE_PAD),
            shape(FX, 8, 2 * LANES),
            shape(GX, 8, LANES),
        ],
        [FINE_PAD] * 3
        + [
            FINE,
            (2, FX, 8, 2 * LANES),
            (2, GX, 8, LANES),
            (5, *COARSE_PAD),
            (5, *COARSE),
            (2, *COARSE),
            COARSE_PAD,
            COARSE_PAD,
        ],
        *mains,
        *quads(strip),
        heat_table,
        table1,
        table2,
        lhs,
        out_any=(3, 4),
        sems=2,
        limit=60,
    )
    k0, kc = call(
        known_kernel,
        "own_sweep",
        [shape(4, *FINE), shape(2, *COARSE)],
        [(4, *FINE)] + [FINE_PAD] * 4 + [(5, *FINE), (5, *COARSE_PAD), (5, *COARSE), (6, *COARSE)],
        init,
        cond,
        plane,
        plane_c,
        cc,
        lhs,
        out_any=(0,),
        sems=4,
        limit=60,
        flops=10**10,
    )

    def phase(steps, name, kind_in, kind_out, got, c, own=()):
        kernel = functools.partial(
            phase_kernel, steps, len(c), kind_in, kind_out, len(own) // 2
        )
        outs = [shape(*COARSE)] + outs_of(kind_out)
        scratch = [COARSE_PAD, COARSE_PAD, COARSE, (len(c), *COARSE)]
        got = [*got, *own]
        where = {len(got) + k: HBM for k in range(len(c))}
        where[len(got) + len(c)] = ANY
        c, *hops = call(
            kernel, name, outs, scratch, *got, *c, cc, lhs, where=where, sems=1 + len(c)
        )
        return [c], hops

    c = [c, swap(c, 1)]
    hop = call(join_kernel, "join", shape(6, DEPTH, LANES), [], *c)
    v, hop = lax.optimization_barrier((v, hop))
    v_other = swap(v, 1)
    got, k0, kc = lax.optimization_barrier((shift(hop, 4), k0, kc))
    c, hops = phase(4, "chain_a4", "halves 16", "halves packed", halves([got]), c)
    got = halves(fetch_strips(hops, 8))
    c, *hops, own_right, own_left, v_tile = call(
        functools.partial(second_kernel, 8),
        "second_sweep",
        [shape(*COARSE)]
        + outs_of("halves packed")
        + [shape(4, DEPTH, LANES)] * 2
        + [shape(TX, DEPTH, 2 * LANES)],
        [
            (4, *FINE),
            FINE,
            FINE,
            FINE_PAD,
            FINE_PAD,
            FINE_PAD,
            (4, *COARSE),
            (5, *COARSE_PAD),
            (5, *COARSE),
            (4, *COARSE),
            (2, *COARSE),
            COARSE_PAD,
            COARSE_PAD,
            COARSE_PAD,
        ],
        *got,
        c[0],
        cc,
        lhs,
        k0,
        v,
        v_other,
        kc,
        cond,
        plane_c,
        where={9: ANY, 10: ANY, 11: ANY, 13: ANY},
        sems=3,
        limit=42,
    )
    got = halves(fetch_strips(hops, 8))
    own = (shift(own_right, 0, 1), shift(own_left, 0, -1))
    c, hops = phase(8, "chain_b8", "halves packed", "quads", got, [c], own)
    got = quads(shift(hops[0], 4))
    c, hops = phase(4, "chain_b4", "quads", "halves 8", got, c)
    got = halves([shift(hops[0], 2)])
    c, hops = phase(2, "chain_b2", "halves 8", "window", got, c)
    got = shift(hops[0], 1)
    return call(
        last_kernel,
        "finish",
        shape(1, DEPTH, TX, LANES),
        [(10, DEPTH, LANES)] * 2,
        got,
        c[0],
        cc,
        lhs,
        v_tile,
    )


def solution(mesh):
    placed = (
        P(None, "gx", "gy"),
        P(None, "gx", "gy"),
        P(),
        P("gx", "gy", None),
        P("gx", "gy", None),
        P(None, "tm"),
    )
    return jax.shard_map(
        on_device, mesh=mesh, in_specs=placed, out_specs=P("tm", None, "gx", "gy"), check_vma=False
    )
```
